128 devices in a mesh: meta: 8 (over x, z_hi), node: 16 (over y, z_lo, core).
Axes of the slice: x: 4, y: 4, z: 4 (z_hi: 2, z_lo: 2; z = z_hi * 2 + z_lo), core: 2. Of those that a mesh axis runs over, the one named last changes fastest.
Arguments:
- aggregates: bfloat16 [16, 32768, 768], P('meta', 'node'), may hold values from -6 to 6
- batch_ids: int32 [24576], P('node'), may hold values from 0 to 2047
- labels: int32 [24576], P('node'), may hold values from 0 to 152
- w_proj: bfloat16 [16, 768, 512], P('meta'), may hold values from -0.21875 to 0.21875
- w_qk: bfloat16 [512, 128], replicated, may hold values from -0.25 to 0.25
- w_value: bfloat16 [512, 512], replicated, may hold values from -0.25 to 0.25
- w_class: bfloat16 [153, 8192], replicated, may hold values from -0.1875 to 0.1875
Outputs:
- grad_proj: float32 [16, 768, 512], P('meta')
- grad_qk: float32 [512, 128], replicated
- grad_value: float32 [512, 512], replicated
- grad_class: float32 [153, 8192], P(None, 'meta')
- loss: float32 [], replicated
The draws below stay inside these ranges and needn't reach their ends.
All inputs are finite; a program needn't handle non-finite values.
Results may differ from the reference program's by a relative error of at most 0.024.
Values may be sent and summed in bfloat16 or wider, within the bound.
A program may use at most 128 MiB of HBM per device.

```python
import jax
import jax.numpy as jnp
from jax import lax

METAPATHS = 16
FEAT = 768
PROJ = 512
QK = 64
CLASSES = 153
R_DEV = 2048
B_DEV = 1536
NODES = 32768
BATCH = 24576
N_NODE = 16


def with_ends(array, rng, least, largest):
    shape = array.shape
    index_at = [jax.random.randint(jax.random.fold_in(rng, axis), (), 0, shape[axis]) for axis in range(len(shape))]
    array = array.at[tuple(index_at)].set(least)
    longest = shape.index(max(shape))
    index_at[longest] = (index_at[longest] + 1) % shape[longest]
    return array.at[tuple(index_at)].set(largest)


def steps_of(own_key, extent, shards, smallest, high):
    def one(position, shards_of):
        draws = jax.random.uniform(jax.random.fold_in(jax.random.fold_in(own_key, 6), position), (shards_of,), jnp.float32, smallest / len(shards), high / len(shards))
        return jnp.repeat(jnp.exp(draws), extent[position] // shards_of).reshape((-1,) + (1,) * (len(extent) - position - 1))

    loudness = one(*shards[0])
    for cut in shards[1:]:
        loudness = loudness * one(*cut)
    return loudness


def centred(own_key, dims, scale, limit, cuts=(), held_as=jnp.bfloat16):
    result = scale * jax.random.normal(own_key, dims, jnp.float32)
    if cuts:
        result = result * steps_of(own_key, dims, cuts, -0.22, 0.18)
    return jnp.clip(result, -limit, limit).astype(held_as)


def setup_inputs(seed: int = 0) -> dict:
    arg_keys = jax.random.split(jax.random.key(seed), 8)
    return {
        "aggregates": centred(arg_keys[0], (METAPATHS, NODES, FEAT), 1.0, 6.0, ((0, 8), (1, 16))),
        "batch_ids": with_ends(jax.random.randint(arg_keys[1], (BATCH,), 0, R_DEV), jax.random.fold_in(arg_keys[1], 1), 0, R_DEV - 1).astype(jnp.int32),
        "labels": with_ends(jax.random.randint(arg_keys[2], (BATCH,), 0, CLASSES), jax.random.fold_in(arg_keys[2], 1), 0, CLASSES - 1).astype(jnp.int32),
        "w_proj": centred(arg_keys[3], (METAPATHS, FEAT, PROJ), FEAT ** -0.5, 0.21875, ((0, 8),)),
        "w_qk": centred(arg_keys[4], (PROJ, 2 * QK), PROJ ** -0.5, 0.25),
        "w_value": centred(arg_keys[5], (PROJ, PROJ), PROJ ** -0.5, 0.25),
        "w_class": centred(arg_keys[6], (CLASSES, METAPATHS * PROJ), (3.0 / (METAPATHS * PROJ) ** 0.5), 0.1875),
    }


def product(pattern, first_op, second_op):
    return jnp.einsum(pattern, first_op.astype(jnp.float32), second_op.astype(jnp.float32))


def head_step(hidden, targets, w_qk, w_value, w_class, grad_seed):
    meta_count, node_count, proj_width = hidden.shape
    key_width = w_qk.shape[1] // 2
    key_scale = key_width ** -0.5
    query_keys = product('mnp,pc->mnc', hidden, w_qk).astype(jnp.bfloat16)
    queries = query_keys[..., :key_width]
    key_rows = query_keys[..., key_width:]
    values = product('mnp,pe->mne', hidden, w_value).astype(jnp.bfloat16)
    scores = product('inc,jnc->nij', queries, key_rows) * key_scale
    weights = jnp.exp(scores)
    attention = weights / jnp.sum(weights, axis=2, keepdims=True)
    attn_bf = attention.astype(jnp.bfloat16)
    joined_rows = (product('nij,jne->ine', attn_bf, values) + hidden.astype(jnp.float32)).astype(jnp.bfloat16)
    class_count = w_class.shape[0]
    class_w = w_class.reshape(class_count, meta_count, proj_width)
    logits = product('mnp,cmp->nc', joined_rows, class_w)
    exp_logits = jnp.exp(logits)
    row_total = jnp.sum(exp_logits, axis=1, keepdims=True)
    onehot = (targets[:, None] == jnp.arange(class_count, dtype=jnp.int32)[None, :]).astype(jnp.float32)
    loss_sum = jnp.sum(jnp.log(row_total[:, 0]) - jnp.sum(onehot * logits, axis=1))
    dlogits = (grad_seed * (exp_logits / row_total - onehot)).astype(jnp.bfloat16)
    grad_class = product('nc,mnp->cmp', dlogits, joined_rows).reshape(class_count, meta_count * proj_width)
    d_joined = product('nc,cmp->mnp', dlogits, class_w).astype(jnp.bfloat16)
    d_values = product('nij,ine->jne', attn_bf, d_joined).astype(jnp.bfloat16)
    d_attention = product('ine,jne->nij', d_joined, values)
    d_scores = (attention * (d_attention - jnp.sum(attention * d_attention, axis=2, keepdims=True)) * key_scale).astype(jnp.bfloat16)
    d_queries = product('nij,jnc->inc', d_scores, key_rows)
    d_keys = product('nij,inc->jnc', d_scores, queries)
    d_query_keys = jnp.concatenate([d_queries, d_keys], axis=2).astype(jnp.bfloat16)
    grad_qk = product('mnp,mnc->pc', hidden, d_query_keys)
    grad_value = product('mnp,mne->pe', hidden, d_values)
    back_rows = (d_joined.astype(jnp.float32) + product('mnc,pc->mnp', d_query_keys, w_qk)
                 + product('mne,pe->mnp', d_values, w_value)).astype(jnp.bfloat16)
    return loss_sum, grad_qk, grad_value, grad_class, back_rows


def reference(aggregates, batch_ids, labels, w_proj, w_qk, w_value, w_class):
    grad_seed = 1.0 / (BATCH ** 0.5)
    owner_ids = batch_ids.reshape(N_NODE, B_DEV)
    owner_labels = labels.reshape(N_NODE, B_DEV)
    owner_index = jnp.arange(N_NODE, dtype=jnp.int32)

    def block(totals, pieces):
        block_ids, block_labels, owner = pieces
        row_ids = (block_ids + owner * R_DEV).astype(jnp.int32)
        gathered = jnp.take(aggregates, row_ids, axis=1)
        hidden = product('pbf,pfd->pbd', gathered, w_proj).astype(jnp.bfloat16)
        loss_sum, grad_qk, grad_value, grad_class, back_rows = head_step(hidden, block_labels, w_qk, w_value, w_class, grad_seed)
        grad_proj = product('pbf,pbd->pfd', gathered, back_rows)
        terms = (grad_proj, grad_qk, grad_value, grad_class, loss_sum)
        return tuple(t + s for t, s in zip(totals, terms)), None

    start = (jnp.zeros((METAPATHS, FEAT, PROJ), jnp.float32), jnp.zeros((PROJ, 2 * QK), jnp.float32),
             jnp.zeros((PROJ, PROJ), jnp.float32), jnp.zeros((CLASSES, METAPATHS * PROJ), jnp.float32),
             jnp.zeros((), jnp.float32))
    totals, _ = lax.scan(block, start, (owner_ids, owner_labels, owner_index))
    grad_proj, grad_qk, grad_value, grad_class, loss_sum = totals
    return grad_proj, grad_qk, grad_value, grad_class, loss_sum / BATCH
```

```python
import functools

import jax
import jax.numpy as jnp
from jax import lax
from jax.experimental import pallas as pl
from jax.experimental.pallas import tpu as pltpu
from jax.sharding import PartitionSpec as P

MESH = pl.DeviceIdType.MESH
F32 = jnp.float32
BF16 = jnp.bfloat16
GROUPS = 8
CHIPS = 8
PAPERS = 192
BLOCK = 16
CLASS_PAD = 160


def dot(a, b):
    return jnp.dot(a, b, preferred_element_type=F32)


def dot_nt(a, b):
    return lax.dot_general(a, b, (((1,), (1,)), ((), ())), preferred_element_type=F32)


def dot_tn(a, b):
    return lax.dot_general(a, b, (((0,), (0,)), ((), ())), preferred_element_type=F32)


def remote(src, dst, send_sem, recv_sem, where):
    return pltpu.make_async_remote_copy(
        src_ref=src, dst_ref=dst, send_sem=send_sem, recv_sem=recv_sem, device_id=where, device_id_type=MESH
    )


def front_kernel(ids_ref, agg_ref, w_ref, gathered_ref, hidden_ref, outbox, send_sem, recv_sem, own_sem):
    me = lax.axis_index("meta")
    barrier = pltpu.get_barrier_semaphore()
    for j in range(1, GROUPS):
        pl.semaphore_signal(barrier, inc=1, device_id={"meta": lax.rem(me + j, GROUPS)}, device_id_type=MESH)
    pl.semaphore_wait(barrier, GROUPS - 1)

    rows = agg_ref.shape[1]

    def work(peer):
        at = pl.ds(pl.multiple_of(peer * PAPERS, PAPERS), PAPERS)
        picks = ids_ref[at, :] == lax.broadcasted_iota(jnp.int32, (PAPERS, rows), 1)
        picks = picks.astype(F32).astype(BF16)
        for m in range(2):
            got = dot(picks, agg_ref[m]).astype(BF16)
            gathered_ref[m, at, :] = got
            outbox[peer, m] = dot(got, w_ref[m]).astype(BF16)

    def copy_to(peer):
        return remote(
            outbox.at[peer], hidden_ref.at[pl.ds(2 * me, 2)], send_sem.at[peer], recv_sem.at[me], {"meta": peer}
        )

    def step(j, carry):
        peer = lax.rem(me + j, GROUPS)
        work(peer)
        copy_to(peer).start()
        return carry

    lax.fori_loop(1, GROUPS, step, 0)
    work(me)
    own = pltpu.make_async_copy(outbox.at[me], hidden_ref.at[pl.ds(2 * me, 2)], own_sem)
    own.start()
    for j in range(1, GROUPS):
        peer = lax.rem(me + j, GROUPS)
        remote(
            outbox.at[peer], hidden_ref.at[pl.ds(2 * peer, 2)], send_sem.at[peer], recv_sem.at[peer], {"meta": peer}
        ).wait()
    own.wait()


def front(ids, aggregates, w_proj):
    count, rows, feat = aggregates.shape
    width = w_proj.shape[2]
    batch = ids.shape[0]
    vmem = pl.BlockSpec(memory_space=pltpu.VMEM)
    return pl.pallas_call(
        front_kernel,
        out_shape=(
            jax.ShapeDtypeStruct((count, batch, feat), BF16),
            jax.ShapeDtypeStruct((GROUPS * count, PAPERS, width), BF16),
        ),
        in_specs=[vmem] * 3,
        out_specs=(vmem, pl.BlockSpec(memory_space=pl.ANY)),
        scratch_shapes=[
            pltpu.VMEM((GROUPS, count, PAPERS, width), BF16),
            pltpu.SemaphoreType.DMA((GROUPS,)),
            pltpu.SemaphoreType.DMA((GROUPS,)),
            pltpu.SemaphoreType.DMA,
        ],
        compiler_params=pltpu.CompilerParams(
            collective_id=0, has_side_effects=True, vmem_limit_bytes=56 * 1024 * 1024
        ),
    )(ids, aggregates, w_proj)


def back_kernel(
    seed, class_count,
    hidden, w_class, w_all, labels, gathered,
    proj_out, qk_out, value_out, class_out, loss_out,
    joined, d_joined, values, attention, kq, d_vq, returned,
    cls, cls_in, cls_chip, cls_g, cls_meta, cls_all,
    qv_acc, qv, qv_in, qv_chip, qv_meta, qv_all,
    gp, gp_in, gp_chip, gp_all, loss_meta, loss_node,
    send_sem, recv_sem, sib_send, sib_recv,
):
    me = lax.axis_index("meta")
    node = lax.axis_index("node")
    chip, core = node // 2, lax.rem(node, 2)
    other = 1 - core
    sibling = {"node": 2 * chip + other}
    groups = [lax.rem(me + j, GROUPS) for j in range(1, GROUPS)]
    chips = [lax.rem(chip + j, CHIPS) for j in range(1, CHIPS)]

    barrier = pltpu.get_barrier_semaphore()
    for g in groups:
        pl.semaphore_signal(barrier, inc=1, device_id={"meta": g}, device_id_type=MESH)
    for k in chips:
        pl.semaphore_signal(barrier, inc=1, device_id={"node": 2 * k + core}, device_id_type=MESH)
    pl.semaphore_signal(barrier, inc=1, device_id=sibling, device_id_type=MESH)
    pl.semaphore_wait(barrier, GROUPS - 1 + CHIPS)

    def to_group(phase, g, src, dst):
        return remote(src, dst, send_sem.at[phase, g], recv_sem.at[phase, me], {"meta": g})

    def from_group(phase, g, dst):
        return remote(dst, dst, send_sem.at[phase, g], recv_sem.at[phase, g], {"meta": g})

    def to_chip(phase, k, src, dst):
        return remote(src, dst, send_sem.at[phase, k], recv_sem.at[phase, chip], {"node": 2 * k + core})

    def from_chip(phase, k, dst):
        return remote(dst, dst, send_sem.at[phase, k], recv_sem.at[phase, k], {"node": 2 * k + core})

    def to_sibling(phase, src, dst):
        return remote(src, dst, sib_send.at[phase], sib_recv.at[phase], sibling)

    meta_count, papers, width = hidden.shape
    pad = w_class.shape[0]
    key = 64
    scale = key ** (-0.5)
    side = BLOCK * meta_count
    row_paper = lax.rem(lax.broadcasted_iota(jnp.int32, (side, side), 0), BLOCK)
    col_paper = lax.rem(lax.broadcasted_iota(jnp.int32, (side, side), 1), BLOCK)
    same = row_paper == col_paper
    lane = lax.broadcasted_iota(jnp.int32, (side, 2 * key), 1)
    first = lane < key

    def forward(b, carry):
        at = pl.ds(pl.multiple_of(b * BLOCK, BLOCK), BLOCK)
        h = hidden[:, at, :].reshape(side, width)
        mixed = dot(h, w_all[...]).astype(BF16)
        v = mixed[:, :width]
        qk = mixed[:, width : width + 2 * key]
        swapped = mixed[:, width + 2 * key :]
        values[b] = v
        kq[b] = swapped
        q = jnp.where(first, qk.astype(F32), 0.0).astype(BF16)
        scores = dot_nt(q, swapped) * scale
        weights = jnp.where(same, jnp.exp(scores), 0.0)
        att = weights / jnp.sum(weights, axis=1, keepdims=True)
        attention[b] = att
        out = (dot(att.astype(BF16), v) + h.astype(F32)).astype(BF16)
        joined[:, at, :] = out.reshape(meta_count, BLOCK, width)
        return carry

    lax.fori_loop(0, papers // BLOCK, forward, 0)

    def columns(m):
        return pl.ds(pl.multiple_of(m * width, width), width)

    logits = lax.fori_loop(
        0, meta_count, lambda m, t: t + dot_nt(joined[m], w_class[:, columns(m)]), jnp.zeros((papers, pad), F32)
    )
    class_at = lax.broadcasted_iota(jnp.int32, (papers, pad), 1)
    exps = jnp.where(class_at < class_count, jnp.exp(logits), 0.0)
    total = jnp.sum(exps, axis=1, keepdims=True)
    own = pl.ds(pl.multiple_of(me * papers, papers), papers)
    onehot = (labels[own, :] == class_at).astype(F32)
    loss_rows = jnp.log(total) - jnp.sum(onehot * logits, axis=1, keepdims=True)
    loss_meta[me] = jnp.zeros((8, 128), F32) + jnp.sum(loss_rows)
    dlogits = (seed * (exps / total - onehot)).astype(BF16)

    def classes(g, carry):
        for half in range(2):
            m = 2 * g + half
            d_joined[m] = dot(dlogits, w_class[:, columns(m)]).astype(BF16)
            grad = dot_tn(dlogits, joined[m]).astype(BF16)
            for q in range(4):
                for part in range(2):
                    cls[part, 4 * half + q, g] = grad[
                        part * (pad // 2) : (part + 1) * (pad // 2), q * 128 : (q + 1) * 128
                    ]
        return carry

    lax.fori_loop(0, GROUPS, classes, 0)
    c0 = to_sibling(0, cls.at[other], cls_in)
    c0.start()

    def backward(b, carry):
        at = pl.ds(pl.multiple_of(b * BLOCK, BLOCK), BLOCK)
        dj = d_joined[:, at, :].reshape(side, width)
        att = attention[b]
        d_val = dot_tn(att.astype(BF16), dj)
        d_att = dot_nt(dj, values[b])
        mean = jnp.sum(att * d_att, axis=1, keepdims=True)
        d_scores = (att * (d_att - mean) * scale).astype(BF16)
        swapped = kq[b]
        d_qk = jnp.where(first, dot(d_scores, swapped), dot_tn(d_scores, swapped))
        d_vq[:, at, :width] = d_val.astype(BF16).reshape(meta_count, BLOCK, width)
        d_vq[:, at, width:] = d_qk.astype(BF16).reshape(meta_count, BLOCK, 2 * key)
        return carry

    lax.fori_loop(0, papers // BLOCK, backward, 0)

    qv_acc[...] = jnp.zeros_like(qv_acc)
    mixed_width = width + 2 * key
    back = joined

    def returns(j, carry):
        g = lax.rem(me + j, GROUPS)
        for half in range(2):
            m = 2 * g + half
            rows = d_vq[m]
            back[m] = (d_joined[m].astype(F32) + dot_nt(rows, w_all[:, :mixed_width])).astype(BF16)
            qv_acc[...] += dot_tn(hidden[m], rows)
        return carry

    def slot(g):
        return returned.at[:, pl.ds(pl.multiple_of(g * papers, papers), papers), :]

    def send_back(j, carry):
        returns(j, carry)
        g = lax.rem(me + j, GROUPS)
        to_group(0, g, back.at[pl.ds(2 * g, 2)], slot(me)).start()
        return carry

    lax.fori_loop(1, GROUPS, send_back, 0)
    returns(0, 0)
    for half in range(2):
        returned[half, pl.ds(pl.multiple_of(me * papers, papers), papers), :] = back[2 * me + half]

    part_rows = qv.shape[2]
    for part in range(2):
        for k in range(CHIPS):
            start = (part * CHIPS + k) * part_rows
            qv[part, k] = qv_acc[start : start + part_rows, :].astype(BF16)
    q0 = to_sibling(1, qv.at[other], qv_in)
    q0.start()

    c0.wait_recv()
    q0.wait_recv()

    def pair_sum(k, carry):
        cls_in[k] = (cls[core, k].astype(F32) + cls_in[k].astype(F32)).astype(BF16)
        qv_in[k] = (qv[core, k].astype(F32) + qv_in[k].astype(F32)).astype(BF16)
        return carry

    lax.fori_loop(0, CHIPS, pair_sum, 0)
    for k in chips:
        to_chip(1, k, cls_in.at[k], cls_chip.at[chip]).start()
        to_chip(2, k, qv_in.at[k], qv_chip.at[chip]).start()
    cls_chip[chip] = cls_in[chip]
    qv_chip[chip] = qv_in[chip]
    for k in chips:
        from_chip(1, k, cls_chip.at[k]).wait_recv()
        from_chip(2, k, qv_chip.at[k]).wait_recv()

    def chip_sum(g, carry):
        cls_g[g] = jnp.sum(cls_chip[:, g].astype(F32), axis=0).astype(BF16)
        return carry

    lax.fori_loop(0, GROUPS, chip_sum, 0)
    qv_meta[me] = jnp.sum(qv_chip[...].astype(F32), axis=0).astype(BF16)
    cls_meta[me] = cls_g[me]
    for g in groups:
        to_group(3, g, cls_g.at[g], cls_meta.at[me]).start()
        to_group(4, g, qv_meta.at[me], qv_meta.at[me]).start()
        to_group(5, g, loss_meta.at[me], loss_meta.at[me]).start()

    for g in groups:
        from_group(0, g, slot(g)).wait_recv()

    part_feat = gp.shape[2]

    def project(m):
        grad = dot_tn(gathered[m], returned[m])
        for k in range(CHIPS):
            gp[m, k] = grad[k * part_feat : (k + 1) * part_feat].astype(BF16)

    project(other)
    g0 = to_sibling(2, gp.at[other], gp_in)
    g0.start()
    project(core)

    for g in groups:
        from_group(3, g, cls_meta.at[g]).wait_recv()
        from_group(4, g, qv_meta.at[g]).wait_recv()
        from_group(5, g, loss_meta.at[g]).wait_recv()
    cls_all[core, chip] = jnp.sum(cls_meta[...].astype(F32), axis=0).astype(BF16)
    qv_all[core, chip] = jnp.sum(qv_meta[...].astype(F32), axis=0).astype(BF16)
    loss_node[core, chip] = jnp.sum(loss_meta[...], axis=0)
    for k in chips:
        to_chip(6, k, cls_all.at[core, chip], cls_all.at[core, chip]).start()
        to_chip(7, k, qv_all.at[core, chip], qv_all.at[core, chip]).start()
        to_chip(8, k, loss_node.at[core, chip], loss_node.at[core, chip]).start()

    g0.wait_recv()

    def pair_proj(k, carry):
        gp_in[k] = (gp[core, k].astype(F32) + gp_in[k].astype(F32)).astype(BF16)
        return carry

    lax.fori_loop(0, CHIPS, pair_proj, 0)
    for k in chips:
        to_chip(9, k, gp_in.at[k], gp_chip.at[chip]).start()
    gp_chip[chip] = gp_in[chip]

    for k in chips:
        from_chip(6, k, cls_all.at[core, k]).wait_recv()
        from_chip(7, k, qv_all.at[core, k]).wait_recv()
        from_chip(8, k, loss_node.at[core, k]).wait_recv()
    last = [
        to_sibling(3, cls_all.at[core], cls_all.at[core]),
        to_sibling(4, qv_all.at[core], qv_all.at[core]),
        to_sibling(5, loss_node.at[core], loss_node.at[core]),
    ]
    for copy in last:
        copy.start()

    for k in chips:
        from_chip(9, k, gp_chip.at[k]).wait_recv()
    gp_all[core, chip] = jnp.sum(gp_chip[...].astype(F32), axis=0).astype(BF16)
    for k in chips:
        to_chip(10, k, gp_all.at[core, chip], gp_all.at[core, chip]).start()

    def across(k):
        return remote(
            gp_all.at[core, k], gp_all.at[core, k], send_sem.at[11, k], recv_sem.at[11, k], sibling
        )

    def across_in(k):
        return remote(
            gp_all.at[other, k], gp_all.at[other, k], send_sem.at[11, k], recv_sem.at[11, k], sibling
        )

    across(chip).start()

    remote(cls_all.at[other], cls_all.at[other], sib_send.at[3], sib_recv.at[3], sibling).wait_recv()
    remote(qv_all.at[other], qv_all.at[other], sib_send.at[4], sib_recv.at[4], sibling).wait_recv()
    remote(loss_node.at[other], loss_node.at[other], sib_send.at[5], sib_recv.at[5], sibling).wait_recv()
    half_rows = pad // 2
    for k in range(CHIPS):
        lanes = slice(k * 128, (k + 1) * 128)
        class_out[:half_rows, lanes] = cls_all[0, k].astype(F32)
        class_out[half_rows:, lanes] = cls_all[1, k][: class_count - half_rows].astype(F32)
        for part in range(2):
            start = (part * CHIPS + k) * part_rows
            block = qv_all[part, k].astype(F32)
            value_out[start : start + part_rows, :] = block[:, :width]
            qk_out[start : start + part_rows, :] = block[:, width:]
    loss_out[...] = jnp.sum(loss_node[...].reshape(2 * CHIPS, 8, 128), axis=0)

    for k in chips:
        from_chip(10, k, gp_all.at[core, k]).wait_recv()
        across(k).start()

    def emit(part, k):
        at = pl.ds(pl.multiple_of(k * part_feat, part_feat), part_feat)
        proj_out[part, at, :] = gp_all[part, k].astype(F32)

    for k in [chip] + chips:
        emit(core, k)
    for k in [chip] + chips:
        across_in(k).wait_recv()
        emit(other, k)

    c0.wait_send()
    q0.wait_send()
    g0.wait_send()
    for copy in last:
        copy.wait_send()
    for g in groups:
        to_group(0, g, back.at[pl.ds(2 * g, 2)], slot(me)).wait_send()
        to_group(3, g, cls_g.at[g], cls_meta.at[me]).wait_send()
        to_group(4, g, qv_meta.at[me], qv_meta.at[me]).wait_send()
        to_group(5, g, loss_meta.at[me], loss_meta.at[me]).wait_send()
    for k in chips:
        to_chip(1, k, cls_in.at[k], cls_chip.at[chip]).wait_send()
        to_chip(2, k, qv_in.at[k], qv_chip.at[chip]).wait_send()
        to_chip(6, k, cls_all.at[core, chip], cls_all.at[core, chip]).wait_send()
        to_chip(7, k, qv_all.at[core, chip], qv_all.at[core, chip]).wait_send()
        to_chip(8, k, loss_node.at[core, chip], loss_node.at[core, chip]).wait_send()
        to_chip(9, k, gp_in.at[k], gp_chip.at[chip]).wait_send()
        to_chip(10, k, gp_all.at[core, chip], gp_all.at[core, chip]).wait_send()
    for k in [chip] + chips:
        across(k).wait_send()


def back_step(hidden, w_class, w_all, labels, gathered, class_count, seed):
    metas, papers, width = hidden.shape
    feat = gathered.shape[2]
    batch = gathered.shape[1]
    side = BLOCK * metas
    blocks = papers // BLOCK
    mixed = width + 128
    half = CLASS_PAD // 2
    vmem = pl.BlockSpec(memory_space=pltpu.VMEM)
    part = feat // CHIPS
    rows = width // (2 * CHIPS)
    return pl.pallas_call(
        functools.partial(back_kernel, seed, class_count),
        out_shape=(
            jax.ShapeDtypeStruct((2, feat, width), F32),
            jax.ShapeDtypeStruct((width, 128), F32),
            jax.ShapeDtypeStruct((width, width), F32),
            jax.ShapeDtypeStruct((class_count, 2 * width), F32),
            jax.ShapeDtypeStruct((8, 128), F32),
        ),
        in_specs=[vmem] * 5,
        out_specs=(vmem,) * 5,
        scratch_shapes=[
            pltpu.VMEM((metas, papers, width), BF16),
            pltpu.VMEM((metas, papers, width), BF16),
            pltpu.VMEM((blocks, side, width), BF16),
            pltpu.VMEM((blocks, side, side), F32),
            pltpu.VMEM((blocks, side, 128), BF16),
            pltpu.VMEM((metas, papers, mixed), BF16),
            pltpu.VMEM((2, batch, width), BF16),
            pltpu.VMEM((2, CHIPS, GROUPS, half, 128), BF16),
            pltpu.VMEM((CHIPS, GROUPS, half, 128), BF16),
            pltpu.VMEM((CHIPS, GROUPS, half, 128), BF16),
            pltpu.VMEM((GROUPS, half, 128), BF16),
            pltpu.VMEM((GROUPS, half, 128), BF16),
            pltpu.VMEM((2, CHIPS, half, 128), BF16),
            pltpu.VMEM((width, mixed), F32),
            pltpu.VMEM((2, CHIPS, rows, mixed), BF16),
            pltpu.VMEM((CHIPS, rows, mixed), BF16),
            pltpu.VMEM((CHIPS, rows, mixed), BF16),
            pltpu.VMEM((GROUPS, rows, mixed), BF16),
            pltpu.VMEM((2, CHIPS, rows, mixed), BF16),
            pltpu.VMEM((2, CHIPS, part, width), BF16),
            pltpu.VMEM((CHIPS, part, width), BF16),
            pltpu.VMEM((CHIPS, part, width), BF16),
            pltpu.VMEM((2, CHIPS, part, width), BF16),
            pltpu.VMEM((GROUPS, 8, 128), F32),
            pltpu.VMEM((2, CHIPS, 8, 128), F32),
            pltpu.SemaphoreType.DMA((12, 8)),
            pltpu.SemaphoreType.DMA((12, 8)),
            pltpu.SemaphoreType.DMA((6,)),
            pltpu.SemaphoreType.DMA((6,)),
        ],
        compiler_params=pltpu.CompilerParams(
            collective_id=1, has_side_effects=True, vmem_limit_bytes=60 * 1024 * 1024
        ),
    )(hidden, w_class, w_all, labels, gathered)


def local(aggregates, batch_ids, labels, w_proj, w_qk, w_value, w_class):
    batch_total = labels.shape[0] * lax.axis_size("node")
    class_count = w_class.shape[0]
    key = w_qk.shape[1] // 2
    gathered, hidden = front(batch_ids[:, None], aggregates, w_proj)
    w_all = jnp.concatenate([w_value, w_qk, w_qk[:, key:], w_qk[:, :key]], axis=1)
    w_pad = jnp.pad(w_class, ((0, CLASS_PAD - class_count), (0, 0)))
    grad_proj, grad_qk, grad_value, grad_class, loss = back_step(
        hidden, w_pad, w_all, labels[:, None], gathered, class_count, 1.0 / batch_total**0.5
    )
    return (grad_proj, grad_qk, grad_value, grad_class, loss[0, 0] / batch_total)


def solution(mesh):
    in_specs = (P("meta", "node", None), P("node"), P("node"), P("meta", None, None), P(), P(), P())
    out_specs = (P("meta", None, None), P(), P(), P(None, "meta"), P())
    return jax.shard_map(local, mesh=mesh, in_specs=in_specs, out_specs=out_specs, check_vma=False)
```

```python
import functools

import jax
import jax.numpy as jnp
from jax import lax
from jax.experimental import pallas as pl
from jax.experimental.pallas import tpu as pltpu
from jax.sharding import PartitionSpec as P

MESH = pl.DeviceIdType.MESH
F32 = jnp.float32
BF16 = jnp.bfloat16
GROUPS = 8
CHIPS = 8
PAPERS = 192
HALF = 96
BLOCK = 16
METAS = 16
KEY = 64
CLASS_PAD = 160
TAIL = CLASS_PAD - 128


def dot(a, b):
    return jnp.dot(a, b, preferred_element_type=F32)


def dot_nt(a, b):
    return lax.dot_general(a, b, (((1,), (1,)), ((), ())), preferred_element_type=F32)


def dot_tn(a, b):
    return lax.dot_general(a, b, (((0,), (0,)), ((), ())), preferred_element_type=F32)


def iota(shape, axis):
    return lax.broadcasted_iota(jnp.int32, shape, axis)


def where_one(mask):
    return mask.astype(F32).astype(BF16)


def remote(src, dst, send_sem, recv_sem, where):
    return pltpu.make_async_remote_copy(
        src_ref=src, dst_ref=dst, send_sem=send_sem, recv_sem=recv_sem, device_id=where, device_id_type=MESH
    )


def step_kernel(
    seed, class_count,
    ids_ref, labels_ref, agg_hbm, w_proj, w_qk, w_value, w_class,
    gp_all, cls_all, qv_all, loss_node,
    agg, agg_sem, ids, labels, gathered, outbox, hidden, w_all, w_mix,
    joined, d_joined, values, attention, kq, dlogits, attended, mail, mail_in, d_qk, d_qk_in, spread_x,
    cls, cls_in, cls_chip, cls_g, cls_meta,
    qv_acc, qv, qv_in, qv_chip, qv_meta,
    gp, gp_in, gp_chip, loss_acc, loss_meta,
    out_sem, in_sem, mail_send, mail_recv, send_sem, recv_sem, sib_send, sib_recv,
):
    me = lax.axis_index("meta")
    node = lax.axis_index("node")
    chip, core = node // 2, lax.rem(node, 2)
    other = 1 - core
    sibling = {"node": 2 * chip + other}
    groups = [lax.rem(me + j, GROUPS) for j in range(1, GROUPS)]
    chips = [lax.rem(chip + j, CHIPS) for j in range(1, CHIPS)]
    width = w_value.shape[0]
    rows = agg.shape[1]
    feat = agg.shape[2]

    loads = [pltpu.make_async_copy(agg_hbm.at[m], agg.at[m], agg_sem.at[m]) for m in range(2)]
    for load in loads:
        load.start()

    barrier = pltpu.get_barrier_semaphore()
    for g in groups:
        pl.semaphore_signal(barrier, inc=1, device_id={"meta": g}, device_id_type=MESH)
    for k in chips:
        pl.semaphore_signal(barrier, inc=1, device_id={"node": 2 * k + core}, device_id_type=MESH)
    pl.semaphore_signal(barrier, inc=1, device_id=sibling, device_id_type=MESH)

    def to_group(phase, g, src, dst):
        return remote(src, dst, send_sem.at[phase, g], recv_sem.at[phase, me], {"meta": g})

    def from_group(phase, g, dst):
        return remote(dst, dst, send_sem.at[phase, g], recv_sem.at[phase, g], {"meta": g})

    def to_chip(phase, k, src, dst):
        return remote(src, dst, send_sem.at[phase, k], recv_sem.at[phase, chip], {"node": 2 * k + core})

    def from_chip(phase, k, dst):
        return remote(dst, dst, send_sem.at[phase, k], recv_sem.at[phase, k], {"node": 2 * k + core})

    def to_sibling(phase, src, dst):
        return remote(src, dst, sib_send.at[phase], sib_recv.at[phase], sibling)

    eye = iota((128, 128), 0) == iota((128, 128), 1)
    for t in range(ids_ref.shape[0]):
        for src, dst in ((ids_ref, ids), (labels_ref, labels)):
            row = jnp.broadcast_to(src[t : t + 1, :].astype(F32), (128, 128))
            dst[t * 128 : (t + 1) * 128, :] = jnp.sum(jnp.where(eye, row, 0.0), axis=1, keepdims=True).astype(jnp.int32)

    loads[0].wait()
    loads[1].wait()
    pl.semaphore_wait(barrier, GROUPS - 1 + CHIPS)

    def part(h):
        return pl.ds(pl.multiple_of(h * HALF, HALF), HALF)

    def out_copy(g, h, m):
        return remote(
            outbox.at[g, m, part(h), :],
            hidden.at[2 * me + m, part(h), :],
            out_sem.at[g, 2 * h + m],
            in_sem.at[me, 2 * h + m],
            {"meta": g},
        )

    def in_copy(g, h, m):
        here = hidden.at[2 * g + m, part(h), :]
        return remote(here, here, out_sem.at[g, 2 * h + m], in_sem.at[g, 2 * h + m], {"meta": g})

    def project_pair(p, h, with_own):
        first = lax.rem(me // 2 + p + 1, 4) * 2 + lax.rem(me + p, 2)
        second = lax.rem(me // 2 + 3 - p, 4) * 2 + lax.rem(me + p + 1, 2)
        if with_own:
            second = me
        spots = [pl.ds(pl.multiple_of(g * PAPERS + h * HALF, HALF), HALF) for g in (first, second)]
        column = jnp.concatenate([ids[spot, :] for spot in spots], axis=0)
        picks = where_one(column == iota((2 * HALF, rows), 1))
        for m in range(2):
            got = dot(picks, agg[m]).astype(BF16)
            row = dot(got, w_proj[m]).astype(BF16)
            for q, g in enumerate((first, second)):
                gathered[m, spots[q], :] = got[q * HALF : (q + 1) * HALF]
                mine = row[q * HALF : (q + 1) * HALF]
                outbox[g, m, part(h), :] = mine
                if with_own and q == 1:
                    hidden[2 * me + m, part(h), :] = mine
                else:
                    out_copy(g, h, m).start()

    def project_half(h, carry):
        def one(p, c):
            project_pair(p, h, False)
            return c

        lax.fori_loop(0, 3, one, 0)
        project_pair(3, h, True)
        return carry

    lax.fori_loop(0, 2, project_half, 0)

    swap = where_one(lax.rem(iota((2 * KEY, 2 * KEY), 0) + KEY, 2 * KEY) == iota((2 * KEY, 2 * KEY), 1))
    w_all[:, :width] = w_value[...]
    w_all[:, width : width + 2 * KEY] = w_qk[...]
    w_all[:, width + 2 * KEY :] = dot(w_qk[...], swap).astype(BF16)
    tail_at = 128 * METAS
    for m in range(METAS):
        lanes = slice(m * width, (m + 1) * width)
        w_mix[128 * m : 128 * (m + 1), :] = w_class[:128, lanes]
        last = w_class[128:class_count, lanes].astype(F32)
        zeros = jnp.zeros((CLASS_PAD - class_count, width), F32)
        w_mix[tail_at + TAIL * m : tail_at + TAIL * (m + 1), :] = jnp.concatenate([last, zeros], axis=0).astype(BF16)

    def class_rows(m):
        main = w_mix[pl.ds(pl.multiple_of(128 * m, 128), 128), :]
        tail = w_mix[pl.ds(pl.multiple_of(tail_at + TAIL * m, TAIL), TAIL), :]
        return jnp.concatenate([main, tail], axis=0)

    def class_rows_wide(m):
        return jnp.concatenate([class_rows(m), jnp.zeros((256 - CLASS_PAD, width), BF16)], axis=0)

    scale = KEY ** (-0.5)
    side = BLOCK * METAS
    same = lax.rem(iota((side, side), 0), BLOCK) == lax.rem(iota((side, side), 1), BLOCK)
    first = iota((side, 2 * KEY), 1) < KEY
    by_key = where_one(iota((side, side), 0) // BLOCK == iota((side, side), 1) // BLOCK)
    by_query = iota((side, side), 0) // BLOCK == lax.rem(iota((side, side), 1), METAS)

    def mail_to(g, h):
        return remote(
            mail.at[g, part(h), :], mail_in.at[me, part(h), :], mail_send.at[g, h], mail_recv.at[me, h], {"meta": g}
        )

    def mail_from(g, h):
        here = mail_in.at[g, part(h), :]
        return remote(here, here, mail_send.at[g, h], mail_recv.at[g, h], {"meta": g})

    def keys_to(g, h):
        return remote(
            d_qk.at[pl.ds(2 * g, 2), part(h), :],
            d_qk_in.at[me, :, part(h), :],
            mail_send.at[g, 2 + h],
            mail_recv.at[me, 2 + h],
            {"meta": g},
        )

    def keys_from(g, h):
        here = d_qk_in.at[g, :, part(h), :]
        return remote(here, here, mail_send.at[g, 2 + h], mail_recv.at[g, 2 + h], {"meta": g})

    def head(h, carry):
        for g in groups:
            for m in range(2):
                in_copy(g, h, m).wait_recv()

        def forward(t, c):
            b = h * (HALF // BLOCK) + t
            at = pl.ds(pl.multiple_of(b * BLOCK, BLOCK), BLOCK)
            here = hidden[:, at, :].reshape(side, width)
            mixed = dot(here, w_all[...]).astype(BF16)
            v = mixed[:, :width]
            swapped = mixed[:, width + 2 * KEY :]
            values[b] = v
            kq[b] = swapped
            q = jnp.where(first, mixed[:, width : width + 2 * KEY].astype(F32), 0.0).astype(BF16)
            scores = dot_nt(q, swapped) * scale
            weights = jnp.where(same, jnp.exp(scores), 0.0)
            att = weights / jnp.sum(weights, axis=1, keepdims=True)
            attention[b] = att
            att = att.astype(BF16)
            out = (dot(att, v) + here.astype(F32)).astype(BF16)
            joined[:, at, :] = out.reshape(METAS, BLOCK, width)
            wide = jnp.where(by_query, dot(att, by_key), 0.0)
            attended[at, :] = jnp.sum(wide.reshape(METAS, BLOCK, side), axis=0).astype(BF16)
            return c

        lax.fori_loop(0, HALF // BLOCK, forward, 0)

        logits = lax.fori_loop(
            0,
            METAS,
            lambda m, t: t + dot_nt(joined[m, part(h), :], class_rows_wide(m)),
            jnp.zeros((HALF, 256), F32),
        )
        class_at = iota((HALF, 256), 1)
        exps = jnp.where(class_at < class_count, jnp.exp(logits), 0.0)
        total = jnp.sum(exps, axis=1, keepdims=True)
        own = pl.ds(pl.multiple_of(me * PAPERS + h * HALF, HALF), HALF)
        onehot = (labels[own, :] == class_at).astype(F32)
        loss_rows = jnp.log(total) - jnp.sum(onehot * logits, axis=1, keepdims=True)
        loss_acc[h] = jnp.zeros((8, 128), F32) + jnp.sum(loss_rows)
        dl = (seed * (exps / total - onehot)).astype(BF16)
        dlogits[part(h), :] = dl

        lane = iota((side, 128), 1)
        for j in range(GROUPS):
            g = lax.rem(me + j, GROUPS)
            choose = where_one(jnp.logical_and(iota((side, 128), 0) == lane + 2 * METAS * g - TAIL, lane >= TAIL) & (lane < TAIL + 2 * METAS))
            second = (dl[:, 128:].astype(F32) + dot(attended[part(h), :], choose)).astype(BF16)
            box = mail_in if j == 0 else mail
            box[g, part(h), :128] = dl[:, :128]
            box[g, part(h), 128:] = second
            if j:
                mail_to(g, h).start()

        def spread(m, c):
            d_joined[m, part(h), :] = dot(dl[:, :CLASS_PAD], class_rows(m)).astype(BF16)
            return c

        lax.fori_loop(0, METAS, spread, 0)

        def backward(t, c):
            b = h * (HALF // BLOCK) + t
            at = pl.ds(pl.multiple_of(b * BLOCK, BLOCK), BLOCK)
            dj = d_joined[:, at, :].reshape(side, width)
            att = attention[b]
            d_att = dot_nt(dj, values[b])
            mean = jnp.sum(att * d_att, axis=1, keepdims=True)
            d_scores = (att * (d_att - mean) * scale).astype(BF16)
            swapped = kq[b]
            grad = jnp.where(first, dot(d_scores, swapped), dot_tn(d_scores, swapped))
            d_qk[:, at, :] = grad.astype(BF16).reshape(METAS, BLOCK, 2 * KEY)
            return c

        lax.fori_loop(0, HALF // BLOCK, backward, 0)
        for g in groups:
            keys_to(g, h).start()
        for m in range(2):
            d_qk_in[me, m, part(h), :] = d_qk[2 * me + m, part(h), :]
        return carry

    lax.fori_loop(0, 2, head, 0)

    def classes(g, carry):
        for m in range(2):
            grad = dot_tn(dlogits[:, :CLASS_PAD], joined[2 * g + m]).astype(BF16)
            for q in range(4):
                for p in range(2):
                    cls[p, 4 * m + q, g] = grad[p * (CLASS_PAD // 2) : (p + 1) * (CLASS_PAD // 2), q * 128 : (q + 1) * 128]
        return carry

    lax.fori_loop(0, GROUPS, classes, 0)
    c0 = to_sibling(0, cls.at[other], cls_in)
    c0.start()

    d_values = joined
    d_hidden = d_joined
    for g in groups:
        for h in range(2):
            mail_from(g, h).wait_recv()
    tail_lane = iota((128, TAIL * METAS), 1)
    tail_row = iota((128, TAIL * METAS), 0)
    repeat = where_one((tail_row < TAIL) & (lax.rem(tail_lane, TAIL) == tail_row))
    widen = [where_one(tail_row == TAIL + METAS * j + tail_lane // TAIL) for j in range(2)]

    def home_values(j, carry):
        s = lax.rem(me + j, GROUPS)
        main = mail_in[s, :, :128].astype(F32)
        second = mail_in[s, :, 128:]
        second_f = second.astype(F32)
        tails = dot(second, repeat)
        for q in range(2):
            at = slice(q * PAPERS, (q + 1) * PAPERS)
            spread_x[at, tail_at:] = (tails * dot(second, widen[q])).astype(BF16)
            for i in range(METAS):
                lane = TAIL + METAS * q + i
                spread_x[at, 128 * i : 128 * (i + 1)] = (second_f[:, lane : lane + 1] * main).astype(BF16)
        grads = dot(spread_x[...], w_mix[...]).astype(BF16)
        for q in range(2):
            d_values[2 * s + q] = grads[q * PAPERS : (q + 1) * PAPERS]
        return carry

    lax.fori_loop(0, 2, home_values, 0)

    c0.wait_recv()

    def pair_class(k, carry):
        cls_in[k] = (cls[core, k].astype(F32) + cls_in[k].astype(F32)).astype(BF16)
        return carry

    lax.fori_loop(0, CHIPS, pair_class, 0)
    for k in chips:
        to_chip(1, k, cls_in.at[k], cls_chip.at[chip]).start()
    cls_chip[chip] = cls_in[chip]

    lax.fori_loop(2, GROUPS, home_values, 0)

    for g in groups:
        for h in range(2):
            keys_from(g, h).wait_recv()
    qv_acc[...] = jnp.zeros_like(qv_acc)

    def home_hidden(s, carry):
        letters = mail_in[s, :, :CLASS_PAD]
        for m in range(2):
            dv = d_values[2 * s + m]
            dk = d_qk_in[s, m]
            dj = dot(letters, class_rows(2 * me + m)).astype(BF16).astype(F32)
            grad = dj + dot_nt(dv, w_value[...]) + dot_nt(dk, w_qk[...])
            d_hidden[GROUPS * m + s] = grad.astype(BF16)
            qv_acc[...] += dot_tn(outbox[s, m], jnp.concatenate([dv, dk], axis=1))
        return carry

    lax.fori_loop(0, GROUPS, home_hidden, 0)

    part_feat = gp.shape[2]

    def project(m):
        back = d_hidden[pl.ds(GROUPS * m, GROUPS)].reshape(GROUPS * PAPERS, width)
        grad = dot_tn(gathered[m], back)
        for k in range(CHIPS):
            gp[m, k] = grad[k * part_feat : (k + 1) * part_feat].astype(BF16)

    project(other)
    g0 = to_sibling(2, gp.at[other], gp_in)
    g0.start()

    part_rows = qv.shape[2]
    for p in range(2):
        for k in range(CHIPS):
            start = (p * CHIPS + k) * part_rows
            qv[p, k] = qv_acc[start : start + part_rows, :].astype(BF16)
    q0 = to_sibling(1, qv.at[other], qv_in)
    q0.start()
    project(core)

    g0.wait_recv()

    def pair_proj(k, carry):
        gp_in[k] = (gp[core, k].astype(F32) + gp_in[k].astype(F32)).astype(BF16)
        return carry

    lax.fori_loop(0, CHIPS, pair_proj, 0)
    for k in chips:
        to_chip(9, k, gp_in.at[k], gp_chip.at[chip]).start()
    gp_chip[chip] = gp_in[chip]

    q0.wait_recv()

    def pair_qv(k, carry):
        qv_in[k] = (qv[core, k].astype(F32) + qv_in[k].astype(F32)).astype(BF16)
        return carry

    lax.fori_loop(0, CHIPS, pair_qv, 0)
    for k in chips:
        to_chip(2, k, qv_in.at[k], qv_chip.at[chip]).start()
    qv_chip[chip] = qv_in[chip]

    for k in chips:
        from_chip(1, k, cls_chip.at[k]).wait_recv()

    def chip_sum(g, carry):
        cls_g[g] = jnp.sum(cls_chip[:, g].astype(F32), axis=0).astype(BF16)
        return carry

    lax.fori_loop(0, GROUPS, chip_sum, 0)
    cls_meta[me] = cls_g[me]
    loss_meta[me] = loss_acc[0] + loss_acc[1]
    for g in groups:
        to_group(3, g, cls_g.at[g], cls_meta.at[me]).start()
        to_group(5, g, loss_meta.at[me], loss_meta.at[me]).start()

    for k in chips:
        from_chip(2, k, qv_chip.at[k]).wait_recv()
    qv_meta[me] = jnp.sum(qv_chip[...].astype(F32), axis=0).astype(BF16)
    for g in groups:
        to_group(4, g, qv_meta.at[me], qv_meta.at[me]).start()

    for k in chips:
        from_chip(9, k, gp_chip.at[k]).wait_recv()
    gp_all[core, chip] = jnp.sum(gp_chip[...].astype(F32), axis=0).astype(BF16)
    for k in chips:
        to_chip(10, k, gp_all.at[core, chip], gp_all.at[core, chip]).start()

    def across(k):
        here = gp_all.at[core, k]
        return remote(here, here, send_sem.at[11, k], recv_sem.at[11, k], sibling)

    def across_in(k):
        here = gp_all.at[other, k]
        return remote(here, here, send_sem.at[11, k], recv_sem.at[11, k], sibling)

    across(chip).start()

    for g in groups:
        from_group(3, g, cls_meta.at[g]).wait_recv()
        from_group(4, g, qv_meta.at[g]).wait_recv()
        from_group(5, g, loss_meta.at[g]).wait_recv()
    cls_all[core, chip] = jnp.sum(cls_meta[...].astype(F32), axis=0).astype(BF16)
    qv_all[core, chip] = jnp.sum(qv_meta[...].astype(F32), axis=0).astype(BF16)
    loss_node[core, chip] = jnp.sum(loss_meta[...], axis=0)
    for k in chips:
        to_chip(6, k, cls_all.at[core, chip], cls_all.at[core, chip]).start()
        to_chip(7, k, qv_all.at[core, chip], qv_all.at[core, chip]).start()
        to_chip(8, k, loss_node.at[core, chip], loss_node.at[core, chip]).start()

    for k in chips:
        from_chip(10, k, gp_all.at[core, k]).wait_recv()
        across(k).start()

    for k in chips:
        from_chip(6, k, cls_all.at[core, k]).wait_recv()
        from_chip(7, k, qv_all.at[core, k]).wait_recv()
        from_chip(8, k, loss_node.at[core, k]).wait_recv()
    finals = [
        to_sibling(3, cls_all.at[core], cls_all.at[core]),
        to_sibling(4, qv_all.at[core], qv_all.at[core]),
        to_sibling(5, loss_node.at[core], loss_node.at[core]),
    ]
    for copy in finals:
        copy.start()

    for k in [chip] + chips:
        across_in(k).wait_recv()
    remote(cls_all.at[other], cls_all.at[other], sib_send.at[3], sib_recv.at[3], sibling).wait_recv()
    remote(qv_all.at[other], qv_all.at[other], sib_send.at[4], sib_recv.at[4], sibling).wait_recv()
    remote(loss_node.at[other], loss_node.at[other], sib_send.at[5], sib_recv.at[5], sibling).wait_recv()

    c0.wait_send()
    q0.wait_send()
    g0.wait_send()
    for copy in finals:
        copy.wait_send()
    for g in groups:
        for h in range(2):
            for m in range(2):
                out_copy(g, h, m).wait_send()
            mail_to(g, h).wait_send()
            keys_to(g, h).wait_send()
        to_group(3, g, cls_g.at[g], cls_meta.at[me]).wait_send()
        to_group(4, g, qv_meta.at[me], qv_meta.at[me]).wait_send()
        to_group(5, g, loss_meta.at[me], loss_meta.at[me]).wait_send()
    for k in chips:
        to_chip(1, k, cls_in.at[k], cls_chip.at[chip]).wait_send()
        to_chip(2, k, qv_in.at[k], qv_chip.at[chip]).wait_send()
        to_chip(6, k, cls_all.at[core, chip], cls_all.at[core, chip]).wait_send()
        to_chip(7, k, qv_all.at[core, chip], qv_all.at[core, chip]).wait_send()
        to_chip(8, k, loss_node.at[core, chip], loss_node.at[core, chip]).wait_send()
        to_chip(9, k, gp_in.at[k], gp_chip.at[chip]).wait_send()
        to_chip(10, k, gp_all.at[core, chip], gp_all.at[core, chip]).wait_send()
    for k in [chip] + chips:
        across(k).wait_send()


def finish_kernel(batch_total, class_count, gp, cls, qv, loss, proj_out, qk_out, value_out, class_out, loss_out):
    part_feat, width = gp.shape[2], gp.shape[3]
    part_rows = qv.shape[2]
    half_rows = cls.shape[2]
    for p in range(2):
        for k in range(CHIPS):
            proj_out[p, k * part_feat : (k + 1) * part_feat, :] = gp[p, k].astype(F32)
            start = (p * CHIPS + k) * part_rows
            block = qv[p, k].astype(F32)
            value_out[start : start + part_rows, :] = block[:, :width]
            qk_out[start : start + part_rows, :] = block[:, width:]
            lanes = slice(k * 128, (k + 1) * 128)
            if p == 0:
                class_out[:half_rows, lanes] = cls[0, k].astype(F32)
            else:
                class_out[half_rows:, lanes] = cls[1, k].astype(F32)[: class_count - half_rows]
    loss_out[0, 0] = jnp.sum(loss[...].reshape(2 * CHIPS, 8, 128), axis=0)[0, 0] / batch_total


def local(aggregates, batch_ids, labels, w_proj, w_qk, w_value, w_class):
    batch_total = labels.shape[0] * lax.axis_size("node")
    class_count = w_class.shape[0]
    count, rows, feat = aggregates.shape
    batch = batch_ids.shape[0]
    width = w_value.shape[0]
    side = BLOCK * METAS
    blocks = PAPERS // BLOCK
    mixed = width + 2 * KEY
    half = CLASS_PAD // 2
    part = feat // CHIPS
    part_rows = width // (2 * CHIPS)
    vmem = pl.BlockSpec(memory_space=pltpu.VMEM)
    sums = pl.pallas_call(
        functools.partial(step_kernel, 1.0 / batch_total**0.5, class_count),
        out_shape=(
            jax.ShapeDtypeStruct((2, CHIPS, part, width), BF16),
            jax.ShapeDtypeStruct((2, CHIPS, half, 128), BF16),
            jax.ShapeDtypeStruct((2, CHIPS, part_rows, mixed), BF16),
            jax.ShapeDtypeStruct((2, CHIPS, 8, 128), F32),
        ),
        in_specs=[vmem, vmem, pl.BlockSpec(memory_space=pl.ANY)] + [vmem] * 4,
        out_specs=(vmem,) * 4,
        scratch_shapes=[
            pltpu.VMEM((count, rows, feat), BF16),
            pltpu.SemaphoreType.DMA((2,)),
            pltpu.VMEM((batch, 1), jnp.int32),
            pltpu.VMEM((batch, 1), jnp.int32),
            pltpu.VMEM((count, batch, feat), BF16),
            pltpu.VMEM((GROUPS, count, PAPERS, width), BF16),
            pltpu.VMEM((METAS, PAPERS, width), BF16),
            pltpu.VMEM((width, width + 4 * KEY), BF16),
            pltpu.VMEM((METAS * CLASS_PAD, width), BF16),
            pltpu.VMEM((METAS, PAPERS, width), BF16),
            pltpu.VMEM((METAS, PAPERS, width), BF16),
            pltpu.VMEM((blocks, side, width), BF16),
            pltpu.VMEM((blocks, side, side), F32),
            pltpu.VMEM((blocks, side, 2 * KEY), BF16),
            pltpu.VMEM((PAPERS, 256), BF16),
            pltpu.VMEM((PAPERS, side), BF16),
            pltpu.VMEM((GROUPS, PAPERS, 256), BF16),
            pltpu.VMEM((GROUPS, PAPERS, 256), BF16),
            pltpu.VMEM((METAS, PAPERS, 2 * KEY), BF16),
            pltpu.VMEM((GROUPS, count, PAPERS, 2 * KEY), BF16),
            pltpu.VMEM((2 * PAPERS, METAS * CLASS_PAD), BF16),
            pltpu.VMEM((2, CHIPS, GROUPS, half, 128), BF16),
            pltpu.VMEM((CHIPS, GROUPS, half, 128), BF16),
            pltpu.VMEM((CHIPS, GROUPS, half, 128), BF16),
            pltpu.VMEM((GROUPS, half, 128), BF16),
            pltpu.VMEM((GROUPS, half, 128), BF16),
            pltpu.VMEM((width, mixed), F32),
            pltpu.VMEM((2, CHIPS, part_rows, mixed), BF16),
            pltpu.VMEM((CHIPS, part_rows, mixed), BF16),
            pltpu.VMEM((CHIPS, part_rows, mixed), BF16),
            pltpu.VMEM((GROUPS, part_rows, mixed), BF16),
            pltpu.VMEM((2, CHIPS, part, width), BF16),
            pltpu.VMEM((CHIPS, part, width), BF16),
            pltpu.VMEM((CHIPS, part, width), BF16),
            pltpu.VMEM((2, 8, 128), F32),
            pltpu.VMEM((GROUPS, 8, 128), F32),
            pltpu.SemaphoreType.DMA((GROUPS, 4)),
            pltpu.SemaphoreType.DMA((GROUPS, 4)),
            pltpu.SemaphoreType.DMA((GROUPS, 4)),
            pltpu.SemaphoreType.DMA((GROUPS, 4)),
            pltpu.SemaphoreType.DMA((12, 8)),
            pltpu.SemaphoreType.DMA((12, 8)),
            pltpu.SemaphoreType.DMA((6,)),
            pltpu.SemaphoreType.DMA((6,)),
        ],
        compiler_params=pltpu.CompilerParams(
            collective_id=1, has_side_effects=True, vmem_limit_bytes=62 * 1024 * 1024
        ),
    )(
        batch_ids.reshape(batch // 128, 128), labels.reshape(batch // 128, 128), aggregates, w_proj, w_qk, w_value, w_class
    )
    grad_proj, grad_qk, grad_value, grad_class, loss = pl.pallas_call(
        functools.partial(finish_kernel, batch_total, class_count),
        out_shape=(
            jax.ShapeDtypeStruct((count, feat, width), F32),
            jax.ShapeDtypeStruct((width, 2 * KEY), F32),
            jax.ShapeDtypeStruct((width, width), F32),
            jax.ShapeDtypeStruct((class_count, count * width), F32),
            jax.ShapeDtypeStruct((1, 1), F32),
        ),
        in_specs=[vmem] * 4,
        out_specs=(vmem,) * 4 + (pl.BlockSpec(memory_space=pltpu.SMEM),),
        compiler_params=pltpu.CompilerParams(vmem_limit_bytes=32 * 1024 * 1024),
    )(*sums)
    return (grad_proj, grad_qk, grad_value, grad_class, loss.reshape(()))


def solution(mesh):
    in_specs = (P("meta", "node", None), P("node"), P("node"), P("meta", None, None), P(), P(), P())
    out_specs = (P("meta", None, None), P(), P(), P(None, "meta"), P())
    return jax.shard_map(local, mesh=mesh, in_specs=in_specs, out_specs=out_specs, check_vma=False)
```

```python
import functools

import jax
import jax.numpy as jnp
from jax import lax
from jax.experimental import pallas as pl
from jax.experimental.pallas import tpu as pltpu
from jax.sharding import PartitionSpec as P

MESH = pl.DeviceIdType.MESH
F32 = jnp.float32
BF16 = jnp.bfloat16
GROUPS = 8
CHIPS = 8
PAPERS = 192
HALF = 96
BLOCK = 16
METAS = 16
KEY = 64
CLASS_PAD = 160
TAIL = CLASS_PAD - 128
UNROLL = 2


def dot(a, b):
    return jnp.dot(a, b, preferred_element_type=F32)


def dot_nt(a, b):
    return lax.dot_general(a, b, (((1,), (1,)), ((), ())), preferred_element_type=F32)


def dot_tn(a, b):
    return lax.dot_general(a, b, (((0,), (0,)), ((), ())), preferred_element_type=F32)


def iota(shape, axis):
    return lax.broadcasted_iota(jnp.int32, shape, axis)


def where_one(mask):
    return mask.astype(F32).astype(BF16)


def remote(src, dst, send_sem, recv_sem, where):
    return pltpu.make_async_remote_copy(
        src_ref=src, dst_ref=dst, send_sem=send_sem, recv_sem=recv_sem, device_id=where, device_id_type=MESH
    )


def step_kernel(
    seed, class_count,
    ids_ref, labels_ref, agg_hbm, w_proj_hbm, w_qk, w_value, w_class_hbm,
    gp_all, cls_all, qv_all, loss_node,
    load_sem, labels, gathered, outbox, hidden, w_all, w_back, w_mix,
    joined, d_joined, values, attention, kq, dlogits, attended, mail, mail_in, d_qk, d_vk,
    cls, cls_in, cls_meta, cls_k, cls_chip,
    qv, qv_in, qv_chip, qv_meta,
    gp, gp_in, gp_chip, loss_acc, loss_meta,
    out_sem, in_sem, mail_send, mail_recv, send_sem, recv_sem, sib_send, sib_recv,
):
    me = lax.axis_index("meta")
    node = lax.axis_index("node")
    chip, core = node // 2, lax.rem(node, 2)
    other = 1 - core
    sibling = {"node": 2 * chip + other}
    groups = [lax.rem(me + j, GROUPS) for j in range(1, GROUPS)]
    chips = [lax.rem(chip + j, CHIPS) for j in range(1, CHIPS)]
    width = w_value.shape[0]
    rows, feat = agg_hbm.shape[1:]
    tail_at = 128 * METAS

    barrier = pltpu.get_barrier_semaphore()
    for g in groups:
        pl.semaphore_signal(barrier, inc=1, device_id={"meta": g}, device_id_type=MESH)
    for k in chips:
        pl.semaphore_signal(barrier, inc=1, device_id={"node": 2 * k + core}, device_id_type=MESH)
    pl.semaphore_signal(barrier, inc=1, device_id=sibling, device_id_type=MESH)

    def to_group(phase, g, src, dst):
        return remote(src, dst, send_sem.at[phase, g], recv_sem.at[phase, me], {"meta": g})

    def from_group(phase, g, dst):
        return remote(dst, dst, send_sem.at[phase, g], recv_sem.at[phase, g], {"meta": g})

    def to_chip(phase, k, src, dst):
        return remote(src, dst, send_sem.at[phase, k], recv_sem.at[phase, chip], {"node": 2 * k + core})

    def from_chip(phase, k, dst):
        return remote(dst, dst, send_sem.at[phase, k], recv_sem.at[phase, k], {"node": 2 * k + core})

    def to_sibling(phase, src, dst):
        return remote(src, dst, sib_send.at[phase], sib_recv.at[phase], sibling)

    def to_column(src, dst):
        eye = iota((128, 128), 0) == iota((128, 128), 1)
        for t in range(src.shape[0]):
            row = jnp.broadcast_to(src[t : t + 1, :].astype(F32), (128, 128))
            dst[t * 128 : (t + 1) * 128, :] = jnp.sum(jnp.where(eye, row, 0.0), axis=1, keepdims=True).astype(jnp.int32)

    def part(h):
        return pl.ds(pl.multiple_of(h * HALF, HALF), HALF)

    def out_copy(g, h, m):
        return remote(
            outbox.at[m, g, part(h), :],
            hidden.at[2 * me + m, part(h), :],
            out_sem.at[g, 2 * h + m],
            in_sem.at[me, 2 * h + m],
            {"meta": g},
        )

    def in_copy(g, h, m):
        here = hidden.at[2 * g + m, part(h), :]
        return remote(here, here, out_sem.at[g, 2 * h + m], in_sem.at[g, 2 * h + m], {"meta": g})

    def front(agg, w_proj, w_class, ids):
        loads = []
        step = rows // 4
        for m in range(2):
            for q in range(4):
                at = pl.ds(q * step, step)
                loads.append(pltpu.make_async_copy(agg_hbm.at[m, at, :], agg.at[m, at, :], load_sem.at[4 * m + q]))
        loads.append(pltpu.make_async_copy(w_proj_hbm, w_proj, load_sem.at[8]))
        loads.append(pltpu.make_async_copy(w_class_hbm, w_class, load_sem.at[9]))
        for load in loads:
            load.start()
        to_column(ids_ref, ids)
        for load in loads[:9]:
            load.wait()
        pl.semaphore_wait(barrier, GROUPS - 1 + CHIPS)

        def project_pair(p, h, with_own):
            first = lax.rem(me // 2 + p + 1, 4) * 2 + lax.rem(me + p, 2)
            second = lax.rem(me // 2 + 3 - p, 4) * 2 + lax.rem(me + p + 1, 2)
            if with_own:
                second = me
            spots = [pl.ds(pl.multiple_of(g * PAPERS + h * HALF, HALF), HALF) for g in (first, second)]
            column = jnp.concatenate([ids[spot, :] for spot in spots], axis=0)
            picks = where_one(column == iota((2 * HALF, rows), 1))
            for m in range(2):
                got = dot(picks, agg[m]).astype(BF16)
                row = dot(got, w_proj[m]).astype(BF16)
                for q, g in enumerate((first, second)):
                    gathered[m, spots[q], :] = got[q * HALF : (q + 1) * HALF]
                    mine = row[q * HALF : (q + 1) * HALF]
                    outbox[m, g, part(h), :] = mine
                    if with_own and q == 1:
                        hidden[2 * me + m, part(h), :] = mine
                    else:
                        out_copy(g, h, m).start()

        def project_half(h, carry):
            def one(p, c):
                project_pair(p, h, False)
                return c

            lax.fori_loop(0, 3, one, 0)
            project_pair(3, h, True)
            return carry

        lax.fori_loop(0, 2, project_half, 0)

        swap = where_one(lax.rem(iota((2 * KEY, 2 * KEY), 0) + KEY, 2 * KEY) == iota((2 * KEY, 2 * KEY), 1))
        w_all[:, :width] = w_value[...]
        w_all[:, width : width + 2 * KEY] = w_qk[...]
        w_all[:, width + 2 * KEY :] = dot(w_qk[...], swap).astype(BF16)
        w_back[:width, :] = w_value[...].astype(F32).T.astype(BF16)
        w_back[width:, :] = w_qk[...].astype(F32).T.astype(BF16)
        loads[9].wait()
        for m in range(METAS):
            lanes = slice(m * width, (m + 1) * width)
            w_mix[128 * m : 128 * (m + 1), :] = w_class[:128, lanes]
            last = w_class[128:class_count, lanes].astype(F32)
            zeros = jnp.zeros((CLASS_PAD - class_count, width), F32)
            w_mix[tail_at + TAIL * m : tail_at + TAIL * (m + 1), :] = jnp.concatenate([last, zeros], axis=0).astype(BF16)

    pl.run_scoped(
        front,
        pltpu.VMEM(agg_hbm.shape, BF16),
        pltpu.VMEM(w_proj_hbm.shape, BF16),
        pltpu.VMEM(w_class_hbm.shape, BF16),
        pltpu.VMEM((GROUPS * PAPERS, 1), jnp.int32),
    )
    to_column(labels_ref, labels)

    def class_rows(m):
        main = w_mix[pl.ds(pl.multiple_of(128 * m, 128), 128), :]
        tail = w_mix[pl.ds(pl.multiple_of(tail_at + TAIL * m, TAIL), TAIL), :]
        return jnp.concatenate([main, tail], axis=0)

    def class_rows_wide(m):
        return jnp.concatenate([class_rows(m), jnp.zeros((256 - CLASS_PAD, width), BF16)], axis=0)

    scale = KEY ** (-0.5)
    side = BLOCK * METAS
    same = lax.rem(iota((side, side), 0), BLOCK) == lax.rem(iota((side, side), 1), BLOCK)
    first = iota((side, 2 * KEY), 1) < KEY
    by_key = where_one(iota((side, side), 0) // BLOCK == iota((side, side), 1) // BLOCK)
    by_query = iota((side, side), 0) // BLOCK == lax.rem(iota((side, side), 1), METAS)

    def mail_to(g, h):
        return remote(
            mail.at[g, part(h), :], mail_in.at[me, part(h), :], mail_send.at[g, h], mail_recv.at[me, h], {"meta": g}
        )

    def mail_from(g, h):
        here = mail_in.at[g, part(h), :]
        return remote(here, here, mail_send.at[g, h], mail_recv.at[g, h], {"meta": g})

    def key_rows(g, h):
        return pl.ds(pl.multiple_of(g * PAPERS + h * HALF, HALF), HALF)

    def keys_to(g, h):
        return remote(
            d_qk.at[pl.ds(2 * g, 2), part(h), :],
            d_vk.at[:, key_rows(me, h), pl.ds(width, 2 * KEY)],
            mail_send.at[g, 2 + h],
            mail_recv.at[me, 2 + h],
            {"meta": g},
        )

    def keys_from(g, h):
        here = d_vk.at[:, key_rows(g, h), pl.ds(width, 2 * KEY)]
        return remote(here, here, mail_send.at[g, 2 + h], mail_recv.at[g, 2 + h], {"meta": g})

    def head(h, carry):
        for g in groups:
            for m in range(2):
                in_copy(g, h, m).wait_recv()

        def forward(t, c):
            b = h * (HALF // BLOCK) + t
            at = pl.ds(pl.multiple_of(b * BLOCK, BLOCK), BLOCK)
            here = hidden[:, at, :].reshape(side, width)
            mixed = dot(here, w_all[...]).astype(BF16)
            v = mixed[:, :width]
            swapped = mixed[:, width + 2 * KEY :]
            values[b] = v
            kq[b] = swapped
            q = jnp.where(first, mixed[:, width : width + 2 * KEY].astype(F32), 0.0).astype(BF16)
            scores = dot_nt(q, swapped) * scale
            weights = jnp.where(same, jnp.exp(scores), 0.0)
            att = weights * (1.0 / jnp.sum(weights, axis=1, keepdims=True))
            attention[b] = att
            att = att.astype(BF16)
            out = (dot(att, v) + here.astype(F32)).astype(BF16)
            joined[:, at, :] = out.reshape(METAS, BLOCK, width)
            wide = jnp.where(by_query, dot(att, by_key), 0.0)
            attended[at, :] = jnp.sum(wide.reshape(METAS, BLOCK, side), axis=0).astype(BF16)
            return c

        lax.fori_loop(0, HALF // BLOCK, forward, 0, unroll=UNROLL)

        logits = lax.fori_loop(
            0,
            METAS,
            lambda m, t: t + dot_nt(joined[m, part(h), :], class_rows_wide(m)),
            jnp.zeros((HALF, 256), F32),
        )
        class_at = iota((HALF, 256), 1)
        exps = jnp.where(class_at < class_count, jnp.exp(logits), 0.0)
        total = jnp.sum(exps, axis=1, keepdims=True)
        own = pl.ds(pl.multiple_of(me * PAPERS + h * HALF, HALF), HALF)
        onehot = (labels[own, :] == class_at).astype(F32)
        loss_rows = jnp.log(total) - jnp.sum(onehot * logits, axis=1, keepdims=True)
        loss_acc[h] = jnp.zeros((8, 128), F32) + jnp.sum(loss_rows)
        dl = (seed * (exps / total - onehot)).astype(BF16)
        dlogits[part(h), :] = dl

        lane = iota((side, 128), 1)
        for j in range(GROUPS):
            g = lax.rem(me + j, GROUPS)
            choose = where_one(jnp.logical_and(iota((side, 128), 0) == lane + 2 * METAS * g - TAIL, lane >= TAIL) & (lane < TAIL + 2 * METAS))
            second = (dl[:, 128:].astype(F32) + dot(attended[part(h), :], choose)).astype(BF16)
            box = mail_in if j == 0 else mail
            box[g, part(h), :128] = dl[:, :128]
            box[g, part(h), 128:] = second
            if j:
                mail_to(g, h).start()

        def spread(m, c):
            d_joined[m, part(h), :] = dot(dl[:, :CLASS_PAD], class_rows(m)).astype(BF16)
            return c

        lax.fori_loop(0, METAS, spread, 0)

        def backward(t, c):
            b = h * (HALF // BLOCK) + t
            at = pl.ds(pl.multiple_of(b * BLOCK, BLOCK), BLOCK)
            dj = d_joined[:, at, :].reshape(side, width)
            att = attention[b]
            d_att = dot_nt(dj, values[b])
            mean = jnp.sum(att * d_att, axis=1, keepdims=True)
            d_scores = (att * (d_att - mean) * scale).astype(BF16)
            swapped = kq[b]
            grad = jnp.where(first, dot(d_scores, swapped), dot_tn(d_scores, swapped))
            d_qk[:, at, :] = grad.astype(BF16).reshape(METAS, BLOCK, 2 * KEY)
            return c

        lax.fori_loop(0, HALF // BLOCK, backward, 0, unroll=UNROLL)
        for g in groups:
            keys_to(g, h).start()
        for m in range(2):
            d_vk[m, key_rows(me, h), width:] = d_qk[2 * me + m, part(h), :]
        return carry

    lax.fori_loop(0, 2, head, 0)

    def classes(g, carry):
        for m in range(2):
            grad = dot_tn(dlogits[:, :CLASS_PAD], joined[2 * g + m]).astype(BF16)
            for q in range(4):
                for p in range(2):
                    cls[p, g, 4 * m + q] = grad[p * (CLASS_PAD // 2) : (p + 1) * (CLASS_PAD // 2), q * 128 : (q + 1) * 128]
        return carry

    lax.fori_loop(0, GROUPS, classes, 0)
    c0 = to_sibling(0, cls.at[other], cls_in)
    c0.start()

    for g in groups:
        for h in range(2):
            mail_from(g, h).wait_recv()
    c0.wait_recv()

    def pair_class(g, carry):
        cls_in[g] = (cls[core, g].astype(F32) + cls_in[g].astype(F32)).astype(BF16)
        return carry

    lax.fori_loop(0, GROUPS, pair_class, 0)
    for g in groups:
        to_group(1, g, cls_in.at[g], cls_meta.at[me]).start()
    cls_meta[me] = cls_in[me]

    tail_lane = iota((128, TAIL * METAS), 1)
    tail_row = iota((128, TAIL * METAS), 0)
    repeat = where_one((tail_row < TAIL) & (lax.rem(tail_lane, TAIL) == tail_row))
    widen = [where_one(tail_row == TAIL + METAS * j + tail_lane // TAIL) for j in range(2)]

    def home_values(x_even, x_odd):
        def build(j, x):
            s = lax.rem(me + j, GROUPS)
            main = mail_in[s, :, :128].astype(F32)
            second = mail_in[s, :, 128:]
            second_f = second.astype(F32)
            tails = dot(second, repeat)
            for q in range(2):
                at = slice(q * PAPERS, (q + 1) * PAPERS)
                x[at, tail_at:] = (tails * dot(second, widen[q])).astype(BF16)
                for i in range(METAS):
                    lane = TAIL + METAS * q + i
                    x[at, 128 * i : 128 * (i + 1)] = (second_f[:, lane : lane + 1] * main).astype(BF16)

        def multiply(j, x):
            s = lax.rem(me + j, GROUPS)
            grads = dot(x[...], w_mix[...]).astype(BF16)
            for q in range(2):
                at = pl.ds(pl.multiple_of(s * PAPERS, PAPERS), PAPERS)
                d_vk[q, at, :width] = grads[q * PAPERS : (q + 1) * PAPERS]

        build(0, x_even)

        def two(t, carry):
            build(2 * t + 1, x_odd)
            multiply(2 * t, x_even)
            build(2 * t + 2, x_even)
            multiply(2 * t + 1, x_odd)
            return carry

        lax.fori_loop(0, GROUPS // 2, two, 0)

    spread_shape = pltpu.VMEM((2 * PAPERS, METAS * CLASS_PAD), BF16)
    pl.run_scoped(home_values, spread_shape, spread_shape)

    for g in groups:
        for h in range(2):
            keys_from(g, h).wait_recv()

    batch = GROUPS * PAPERS
    part_rows = qv.shape[2]
    for c in range(4):
        cols = slice(c * 128, (c + 1) * 128)
        grad = sum(dot_tn(outbox[m].reshape(batch, width)[:, cols], d_vk[m]) for m in range(2)).astype(BF16)
        for r in range(128 // part_rows):
            piece = c * (128 // part_rows) + r
            qv[piece // CHIPS, piece % CHIPS] = grad[r * part_rows : (r + 1) * part_rows]
    q0 = to_sibling(1, qv.at[other], qv_in)
    q0.start()

    d_hidden = d_joined

    def home_hidden(m):
        def some(r, carry):
            at = pl.ds(pl.multiple_of(r * 2 * PAPERS, 2 * PAPERS), 2 * PAPERS)
            letters = mail_in[pl.ds(2 * r, 2)].reshape(2 * PAPERS, 256)[:, :CLASS_PAD]
            grad = dot(letters, class_rows(2 * me + m)) + dot(d_vk[m, at, :], w_back[...])
            d_hidden[pl.ds(GROUPS * m + 2 * r, 2)] = grad.astype(BF16).reshape(2, PAPERS, width)
            return carry

        lax.fori_loop(0, GROUPS // 2, some, 0)

    part_feat = gp.shape[3]

    def project(m):
        back = d_hidden[GROUPS * m : GROUPS * (m + 1)].reshape(batch, width)
        grad = dot_tn(gathered[m], back)
        for p in range(2):
            for k in range(CHIPS):
                start = (p * CHIPS + k) * part_feat
                gp[m, p, k] = grad[start : start + part_feat].astype(BF16)

    def pair_proj(m):
        def one(k, carry):
            gp_in[m, k] = (gp[m, core, k].astype(F32) + gp_in[m, k].astype(F32)).astype(BF16)
            return carry

        lax.fori_loop(0, CHIPS, one, 0)
        for k in chips:
            to_chip(9 + m, k, gp_in.at[m, k], gp_chip.at[m, chip]).start()
        gp_chip[m, chip] = gp_in[m, chip]

    def across(m, k):
        here = gp_all.at[m, core, k]
        return remote(here, here, send_sem.at[13 + m, k], recv_sem.at[13 + m, k], sibling)

    def across_in(m, k):
        here = gp_all.at[m, other, k]
        return remote(here, here, send_sem.at[13 + m, k], recv_sem.at[13 + m, k], sibling)

    def chip_proj(m):
        for k in chips:
            from_chip(9 + m, k, gp_chip.at[m, k]).wait_recv()
        gp_all[m, core, chip] = jnp.sum(gp_chip[m].astype(F32), axis=0).astype(BF16)
        for k in chips:
            to_chip(11 + m, k, gp_all.at[m, core, chip], gp_all.at[m, core, chip]).start()
        across(m, chip).start()

    def pass_on(m):
        for k in chips:
            from_chip(11 + m, k, gp_all.at[m, core, k]).wait_recv()
            across(m, k).start()

    home_hidden(0)

    q0.wait_recv()

    def pair_qv(k, carry):
        qv_in[k] = (qv[core, k].astype(F32) + qv_in[k].astype(F32)).astype(BF16)
        return carry

    lax.fori_loop(0, CHIPS, pair_qv, 0)
    for k in chips:
        to_chip(2, k, qv_in.at[k], qv_chip.at[chip]).start()
    qv_chip[chip] = qv_in[chip]

    project(0)
    g0 = [to_sibling(2 + 4 * m, gp.at[m, other], gp_in.at[m]) for m in range(2)]
    g0[0].start()
    home_hidden(1)
    g0[0].wait_recv()
    pair_proj(0)
    project(1)
    g0[1].start()

    for k in chips:
        from_chip(2, k, qv_chip.at[k]).wait_recv()
    qv_meta[me] = jnp.sum(qv_chip[...].astype(F32), axis=0).astype(BF16)
    loss_meta[me] = loss_acc[0] + loss_acc[1]
    for g in groups:
        to_group(4, g, qv_meta.at[me], qv_meta.at[me]).start()
        to_group(5, g, loss_meta.at[me], loss_meta.at[me]).start()

    g0[1].wait_recv()
    pair_proj(1)

    for g in groups:
        from_group(1, g, cls_meta.at[g]).wait_recv()

    def meta_sum(k, carry):
        cls_k[k] = jnp.sum(cls_meta[:, k].astype(F32), axis=0).astype(BF16)
        return carry

    lax.fori_loop(0, CHIPS, meta_sum, 0)
    for k in chips:
        to_chip(3, k, cls_k.at[k], cls_chip.at[chip]).start()
    cls_chip[chip] = cls_k[chip]

    chip_proj(0)

    for g in groups:
        from_group(4, g, qv_meta.at[g]).wait_recv()
        from_group(5, g, loss_meta.at[g]).wait_recv()
    qv_all[core, chip] = jnp.sum(qv_meta[...].astype(F32), axis=0).astype(BF16)
    loss_node[core, chip] = jnp.sum(loss_meta[...], axis=0)
    for k in chips:
        to_chip(7, k, qv_all.at[core, chip], qv_all.at[core, chip]).start()
        to_chip(8, k, loss_node.at[core, chip], loss_node.at[core, chip]).start()

    chip_proj(1)

    for k in chips:
        from_chip(3, k, cls_chip.at[k]).wait_recv()
    cls_all[core, chip] = jnp.sum(cls_chip[...].astype(F32), axis=0).astype(BF16)
    for k in chips:
        to_chip(6, k, cls_all.at[core, chip], cls_all.at[core, chip]).start()

    pass_on(0)

    for k in chips:
        from_chip(6, k, cls_all.at[core, k]).wait_recv()
        from_chip(7, k, qv_all.at[core, k]).wait_recv()
        from_chip(8, k, loss_node.at[core, k]).wait_recv()
    finals = [
        to_sibling(3, cls_all.at[core], cls_all.at[core]),
        to_sibling(4, qv_all.at[core], qv_all.at[core]),
        to_sibling(5, loss_node.at[core], loss_node.at[core]),
    ]
    for copy in finals:
        copy.start()

    pass_on(1)

    for m in range(2):
        for k in [chip] + chips:
            across_in(m, k).wait_recv()
    remote(cls_all.at[other], cls_all.at[other], sib_send.at[3], sib_recv.at[3], sibling).wait_recv()
    remote(qv_all.at[other], qv_all.at[other], sib_send.at[4], sib_recv.at[4], sibling).wait_recv()
    remote(loss_node.at[other], loss_node.at[other], sib_send.at[5], sib_recv.at[5], sibling).wait_recv()

    c0.wait_send()
    q0.wait_send()
    for copy in g0 + finals:
        copy.wait_send()
    for g in groups:
        for h in range(2):
            for m in range(2):
                out_copy(g, h, m).wait_send()
            mail_to(g, h).wait_send()
            keys_to(g, h).wait_send()
        to_group(1, g, cls_in.at[g], cls_meta.at[me]).wait_send()
        to_group(4, g, qv_meta.at[me], qv_meta.at[me]).wait_send()
        to_group(5, g, loss_meta.at[me], loss_meta.at[me]).wait_send()
    for k in chips:
        to_chip(2, k, qv_in.at[k], qv_chip.at[chip]).wait_send()
        to_chip(3, k, cls_k.at[k], cls_chip.at[chip]).wait_send()
        to_chip(6, k, cls_all.at[core, chip], cls_all.at[core, chip]).wait_send()
        to_chip(7, k, qv_all.at[core, chip], qv_all.at[core, chip]).wait_send()
        to_chip(8, k, loss_node.at[core, chip], loss_node.at[core, chip]).wait_send()
    for m in range(2):
        for k in chips:
            to_chip(9 + m, k, gp_in.at[m, k], gp_chip.at[m, chip]).wait_send()
            to_chip(11 + m, k, gp_all.at[m, core, chip], gp_all.at[m, core, chip]).wait_send()
        for k in [chip] + chips:
            across(m, k).wait_send()


def finish_kernel(
    batch_total, class_count,
    gp_hbm, cls_hbm, qv_hbm, loss_hbm, proj_hbm, qk_out, value_out, class_out, loss_out,
    gp, cls, qv, loss, proj, in_sem, out_sem,
):
    part_feat, width = gp.shape[3:]
    part_rows = qv.shape[2]
    half_rows = cls.shape[2]
    loads = [pltpu.make_async_copy(gp_hbm.at[m], gp.at[m], in_sem.at[m]) for m in range(2)]
    for q, (src, dst) in enumerate(((cls_hbm, cls), (qv_hbm, qv), (loss_hbm, loss))):
        loads.append(pltpu.make_async_copy(src, dst, in_sem.at[2 + q]))
    for load in loads:
        load.start()
    stores = []
    for m in range(2):
        loads[m].wait()
        for p in range(2):
            for k in range(CHIPS):
                start = (p * CHIPS + k) * part_feat
                proj[m, start : start + part_feat, :] = gp[m, p, k].astype(F32)
        stores.append(pltpu.make_async_copy(proj.at[m], proj_hbm.at[m], out_sem.at[m]))
        stores[m].start()
    for load in loads[2:]:
        load.wait()
    for p in range(2):
        for k in range(CHIPS):
            start = (p * CHIPS + k) * part_rows
            block = qv[p, k].astype(F32)
            value_out[start : start + part_rows, :] = block[:, :width]
            qk_out[start : start + part_rows, :] = block[:, width:]
            lanes = slice(k * 128, (k + 1) * 128)
            if p == 0:
                class_out[:half_rows, lanes] = cls[0, k].astype(F32)
            else:
                class_out[half_rows:, lanes] = cls[1, k].astype(F32)[: class_count - half_rows]
    loss_out[0, 0] = jnp.sum(loss[...].reshape(2 * CHIPS, 8, 128), axis=0)[0, 0] / batch_total
    for store in stores:
        store.wait()


def local(aggregates, batch_ids, labels, w_proj, w_qk, w_value, w_class):
    batch_total = labels.shape[0] * lax.axis_size("node")
    class_count = w_class.shape[0]
    count, rows, feat = aggregates.shape
    batch = batch_ids.shape[0]
    width = w_value.shape[0]
    side = BLOCK * METAS
    blocks = PAPERS // BLOCK
    mixed = width + 2 * KEY
    half = CLASS_PAD // 2
    part = feat // (2 * CHIPS)
    part_rows = width // (2 * CHIPS)
    vmem = pl.BlockSpec(memory_space=pltpu.VMEM)
    anywhere = pl.BlockSpec(memory_space=pl.ANY)
    sums = pl.pallas_call(
        functools.partial(step_kernel, 1.0 / batch_total**0.5, class_count),
        out_shape=(
            jax.ShapeDtypeStruct((count, 2, CHIPS, part, width), BF16),
            jax.ShapeDtypeStruct((2, CHIPS, half, 128), BF16),
            jax.ShapeDtypeStruct((2, CHIPS, part_rows, mixed), BF16),
            jax.ShapeDtypeStruct((2, CHIPS, 8, 128), F32),
        ),
        in_specs=[vmem, vmem, anywhere, anywhere, vmem, vmem, anywhere],
        out_specs=(vmem,) * 4,
        scratch_shapes=[
            pltpu.SemaphoreType.DMA((10,)),
            pltpu.VMEM((batch, 1), jnp.int32),
            pltpu.VMEM((count, batch, feat), BF16),
            pltpu.VMEM((count, GROUPS, PAPERS, width), BF16),
            pltpu.VMEM((METAS, PAPERS, width), BF16),
            pltpu.VMEM((width, width + 4 * KEY), BF16),
            pltpu.VMEM((mixed, width), BF16),
            pltpu.VMEM((METAS * CLASS_PAD, width), BF16),
            pltpu.VMEM((METAS, PAPERS, width), BF16),
            pltpu.VMEM((METAS, PAPERS, width), BF16),
            pltpu.VMEM((blocks, side, width), BF16),
            pltpu.VMEM((blocks, side, side), F32),
            pltpu.VMEM((blocks, side, 2 * KEY), BF16),
            pltpu.VMEM((PAPERS, 256), BF16),
            pltpu.VMEM((PAPERS, side), BF16),
            pltpu.VMEM((GROUPS, PAPERS, 256), BF16),
            pltpu.VMEM((GROUPS, PAPERS, 256), BF16),
            pltpu.VMEM((METAS, PAPERS, 2 * KEY), BF16),
            pltpu.VMEM((count, batch, mixed), BF16),
            pltpu.VMEM((2, GROUPS, CHIPS, half, 128), BF16),
            pltpu.VMEM((GROUPS, CHIPS, half, 128), BF16),
            pltpu.VMEM((GROUPS, CHIPS, half, 128), BF16),
            pltpu.VMEM((CHIPS, half, 128), BF16),
            pltpu.VMEM((CHIPS, half, 128), BF16),
            pltpu.VMEM((2, CHIPS, part_rows, mixed), BF16),
            pltpu.VMEM((CHIPS, part_rows, mixed), BF16),
            pltpu.VMEM((CHIPS, part_rows, mixed), BF16),
            pltpu.VMEM((GROUPS, part_rows, mixed), BF16),
            pltpu.VMEM((count, 2, CHIPS, part, width), BF16),
            pltpu.VMEM((count, CHIPS, part, width), BF16),
            pltpu.VMEM((count, CHIPS, part, width), BF16),
            pltpu.VMEM((2, 8, 128), F32),
            pltpu.VMEM((GROUPS, 8, 128), F32),
            pltpu.SemaphoreType.DMA((GROUPS, 4)),
            pltpu.SemaphoreType.DMA((GROUPS, 4)),
            pltpu.SemaphoreType.DMA((GROUPS, 4)),
            pltpu.SemaphoreType.DMA((GROUPS, 4)),
            pltpu.SemaphoreType.DMA((15, 8)),
            pltpu.SemaphoreType.DMA((15, 8)),
            pltpu.SemaphoreType.DMA((7,)),
            pltpu.SemaphoreType.DMA((7,)),
        ],
        compiler_params=pltpu.CompilerParams(
            collective_id=1, has_side_effects=True, vmem_limit_bytes=62 * 1024 * 1024
        ),
    )(
        batch_ids.reshape(batch // 128, 128), labels.reshape(batch // 128, 128), aggregates, w_proj, w_qk, w_value, w_class
    )
    grad_proj, grad_qk, grad_value, grad_class, loss = pl.pallas_call(
        functools.partial(finish_kernel, batch_total, class_count),
        out_shape=(
            jax.ShapeDtypeStruct((count, feat, width), F32),
            jax.ShapeDtypeStruct((width, 2 * KEY), F32),
            jax.ShapeDtypeStruct((width, width), F32),
            jax.ShapeDtypeStruct((class_count, count * width), F32),
            jax.ShapeDtypeStruct((1, 1), F32),
        ),
        in_specs=[anywhere] * 4,
        out_specs=(anywhere,) + (vmem,) * 3 + (pl.BlockSpec(memory_space=pltpu.SMEM),),
        scratch_shapes=[
            pltpu.VMEM((count, 2, CHIPS, part, width), BF16),
            pltpu.VMEM((2, CHIPS, half, 128), BF16),
            pltpu.VMEM((2, CHIPS, part_rows, mixed), BF16),
            pltpu.VMEM((2, CHIPS, 8, 128), F32),
            pltpu.VMEM((count, feat, width), F32),
            pltpu.SemaphoreType.DMA((5,)),
            pltpu.SemaphoreType.DMA((2,)),
        ],
        compiler_params=pltpu.CompilerParams(vmem_limit_bytes=32 * 1024 * 1024),
    )(*sums)
    return (grad_proj, grad_qk, grad_value, grad_class, loss.reshape(()))


def solution(mesh):
    in_specs = (P("meta", "node", None), P("node"), P("node"), P("meta", None, None), P(), P(), P())
    out_specs = (P("meta", None, None), P(), P(), P(None, "meta"), P())
    return jax.shard_map(local, mesh=mesh, in_specs=in_specs, out_specs=out_specs, check_vma=False)
```

```python
import functools

import jax
import jax.numpy as jnp
from jax import lax
from jax.experimental import pallas as pl
from jax.experimental.pallas import tpu as pltpu
from jax.sharding import PartitionSpec as P

MESH = pl.DeviceIdType.MESH
F32 = jnp.float32
BF16 = jnp.bfloat16
GROUPS = 8
CHIPS = 8
PAPERS = 192
HALF = 96
BLOCK = 16
METAS = 16
KEY = 64
CLASS_PAD = 160
TAIL = CLASS_PAD - 128
META_ROWS = 48
UNROLL = 6


def dot(a, b):
    return jnp.dot(a, b, preferred_element_type=F32)


def dot_nt(a, b):
    return lax.dot_general(a, b, (((1,), (1,)), ((), ())), preferred_element_type=F32)


def dot_tn(a, b):
    return lax.dot_general(a, b, (((0,), (0,)), ((), ())), preferred_element_type=F32)


def iota(shape, axis):
    return lax.broadcasted_iota(jnp.int32, shape, axis)


def where_one(mask):
    return mask.astype(F32).astype(BF16)


def remote(src, dst, send_sem, recv_sem, where):
    return pltpu.make_async_remote_copy(
        src_ref=src, dst_ref=dst, send_sem=send_sem, recv_sem=recv_sem, device_id=where, device_id_type=MESH
    )


def step_kernel(
    seed, class_count,
    ids_ref, labels_ref, agg_hbm, w_proj_hbm, w_qk, w_value, w_class_hbm,
    gp_all, cls_all, qv_all, loss_node,
    load_sem, labels, gathered, outbox, hidden, w_all, w_back, w_mix,
    joined, d_joined, dlogits, attended, mail, mail_in, d_vq, d_vk,
    cx, cx_in, cx_meta, cx_sum, cx_chip, cy, cy_in, cy_chip, cy_sum, cy_meta,
    qv, qv_in, qv_chip, qv_meta,
    gp, gp_in, gp_chip, loss_acc, loss_meta,
    out_sem, in_sem, mail_send, mail_recv, send_sem, recv_sem, sib_send, sib_recv,
):
    me = lax.axis_index("meta")
    node = lax.axis_index("node")
    chip, core = node // 2, lax.rem(node, 2)
    other = 1 - core
    sibling = {"node": 2 * chip + other}
    groups = [lax.rem(me + j, GROUPS) for j in range(1, GROUPS)]
    chips = [lax.rem(chip + j, CHIPS) for j in range(1, CHIPS)]
    width = w_value.shape[0]
    rows, feat = agg_hbm.shape[1:]
    tail_at = 128 * METAS

    barrier = pltpu.get_barrier_semaphore()
    for g in groups:
        pl.semaphore_signal(barrier, inc=1, device_id={"meta": g}, device_id_type=MESH)
    for k in chips:
        pl.semaphore_signal(barrier, inc=1, device_id={"node": 2 * k + core}, device_id_type=MESH)
    pl.semaphore_signal(barrier, inc=1, device_id=sibling, device_id_type=MESH)

    def to_group(phase, g, src, dst):
        return remote(src, dst, send_sem.at[phase, g], recv_sem.at[phase, me], {"meta": g})

    def from_group(phase, g, dst):
        return remote(dst, dst, send_sem.at[phase, g], recv_sem.at[phase, g], {"meta": g})

    def to_chip(phase, k, src, dst):
        return remote(src, dst, send_sem.at[phase, k], recv_sem.at[phase, chip], {"node": 2 * k + core})

    def from_chip(phase, k, dst):
        return remote(dst, dst, send_sem.at[phase, k], recv_sem.at[phase, k], {"node": 2 * k + core})

    def to_sibling(phase, src, dst):
        return remote(src, dst, sib_send.at[phase], sib_recv.at[phase], sibling)

    def to_column(src, dst):
        eye = iota((128, 128), 0) == iota((128, 128), 1)
        for t in range(src.shape[0]):
            row = jnp.broadcast_to(src[t : t + 1, :].astype(F32), (128, 128))
            dst[t * 128 : (t + 1) * 128, :] = jnp.sum(jnp.where(eye, row, 0.0), axis=1, keepdims=True).astype(jnp.int32)

    def part(h):
        return pl.ds(pl.multiple_of(h * HALF, HALF), HALF)

    def out_copy(g, h, m):
        return remote(
            outbox.at[m, g, part(h), :],
            hidden.at[2 * me + m, part(h), :],
            out_sem.at[g, 2 * h + m],
            in_sem.at[me, 2 * h + m],
            {"meta": g},
        )

    def in_copy(g, h, m):
        here = hidden.at[2 * g + m, part(h), :]
        return remote(here, here, out_sem.at[g, 2 * h + m], in_sem.at[g, 2 * h + m], {"meta": g})

    def front(agg, w_proj, w_class, ids):
        loads = []
        step = rows // 4
        for m in range(2):
            for q in range(4):
                at = pl.ds(q * step, step)
                loads.append(pltpu.make_async_copy(agg_hbm.at[m, at, :], agg.at[m, at, :], load_sem.at[4 * m + q]))
        loads.append(pltpu.make_async_copy(w_proj_hbm, w_proj, load_sem.at[8]))
        loads.append(pltpu.make_async_copy(w_class_hbm, w_class, load_sem.at[9]))
        for load in loads:
            load.start()
        to_column(ids_ref, ids)
        for load in loads[:9]:
            load.wait()
        pl.semaphore_wait(barrier, GROUPS - 1 + CHIPS)

        def project_pair(p, h, with_own):
            first = lax.rem(me // 2 + p + 1, 4) * 2 + lax.rem(me + p, 2)
            second = lax.rem(me // 2 + 3 - p, 4) * 2 + lax.rem(me + p + 1, 2)
            if with_own:
                second = me
            spots = [pl.ds(pl.multiple_of(g * PAPERS + h * HALF, HALF), HALF) for g in (first, second)]
            column = jnp.concatenate([ids[spot, :] for spot in spots], axis=0)
            picks = where_one(column == iota((2 * HALF, rows), 1))
            for m in range(2):
                got = dot(picks, agg[m]).astype(BF16)
                row = dot(got, w_proj[m]).astype(BF16)
                for q, g in enumerate((first, second)):
                    gathered[m, spots[q], :] = got[q * HALF : (q + 1) * HALF]
                    mine = row[q * HALF : (q + 1) * HALF]
                    outbox[m, g, part(h), :] = mine
                    if with_own and q == 1:
                        hidden[2 * me + m, part(h), :] = mine
                    else:
                        out_copy(g, h, m).start()

        def project_half(h, carry):
            def one(p, c):
                project_pair(p, h, False)
                return c

            lax.fori_loop(0, 3, one, 0)
            project_pair(3, h, True)
            return carry

        lax.fori_loop(0, 2, project_half, 0)

        to_column(labels_ref, ids)
        labels[...] = ids[pl.ds(pl.multiple_of(me * PAPERS, PAPERS), PAPERS), :]

        swap = where_one(lax.rem(iota((2 * KEY, 2 * KEY), 0) + KEY, 2 * KEY) == iota((2 * KEY, 2 * KEY), 1))
        w_all[:, :width] = w_value[...]
        w_all[:, width : width + 2 * KEY] = w_qk[...]
        w_all[:, width + 2 * KEY :] = dot(w_qk[...], swap).astype(BF16)
        w_back[:width, :] = w_value[...].astype(F32).T.astype(BF16)
        w_back[width:, :] = w_qk[...].astype(F32).T.astype(BF16)
        loads[9].wait()
        for m in range(METAS):
            lanes = slice(m * width, (m + 1) * width)
            w_mix[128 * m : 128 * (m + 1), :] = w_class[:128, lanes]
            last = w_class[128:class_count, lanes].astype(F32)
            zeros = jnp.zeros((CLASS_PAD - class_count, width), F32)
            w_mix[tail_at + TAIL * m : tail_at + TAIL * (m + 1), :] = jnp.concatenate([last, zeros], axis=0).astype(BF16)

    pl.run_scoped(
        front,
        pltpu.VMEM(agg_hbm.shape, BF16),
        pltpu.VMEM(w_proj_hbm.shape, BF16),
        pltpu.VMEM(w_class_hbm.shape, BF16),
        pltpu.VMEM((GROUPS * PAPERS, 1), jnp.int32),
    )
    def class_rows(m):
        main = w_mix[pl.ds(pl.multiple_of(128 * m, 128), 128), :]
        tail = w_mix[pl.ds(pl.multiple_of(tail_at + TAIL * m, TAIL), TAIL), :]
        return jnp.concatenate([main, tail], axis=0)

    def class_rows_wide(m):
        return jnp.concatenate([class_rows(m), jnp.zeros((256 - CLASS_PAD, width), BF16)], axis=0)

    scale = KEY ** (-0.5)
    side = BLOCK * METAS
    same = lax.rem(iota((side, side), 0), BLOCK) == lax.rem(iota((side, side), 1), BLOCK)
    first = iota((side, 2 * KEY), 1) < KEY
    by_key = where_one(iota((side, side), 0) // BLOCK == iota((side, side), 1) // BLOCK)
    by_query = iota((side, side), 0) // BLOCK == lax.rem(iota((side, side), 1), METAS)

    def mail_to(g, h):
        return remote(
            mail.at[g, part(h), :], mail_in.at[me, part(h), :], mail_send.at[g, h], mail_recv.at[me, h], {"meta": g}
        )

    def mail_from(g, h):
        here = mail_in.at[g, part(h), :]
        return remote(here, here, mail_send.at[g, h], mail_recv.at[g, h], {"meta": g})

    def key_rows(g, h):
        return pl.ds(pl.multiple_of(g * PAPERS + h * HALF, HALF), HALF)

    def keys_to(g, h):
        return remote(
            d_vq.at[pl.ds(2 * g, 2), part(h), pl.ds(width, 2 * KEY)],
            d_vk.at[:, key_rows(me, h), pl.ds(width, 2 * KEY)],
            mail_send.at[g, 2 + h],
            mail_recv.at[me, 2 + h],
            {"meta": g},
        )

    def keys_from(g, h):
        here = d_vk.at[:, key_rows(g, h), pl.ds(width, 2 * KEY)]
        return remote(here, here, mail_send.at[g, 2 + h], mail_recv.at[g, 2 + h], {"meta": g})

    def head(values, attention, kq, h, carry):
        for g in groups:
            for m in range(2):
                in_copy(g, h, m).wait_recv()

        def forward(t, c):
            b = h * (HALF // BLOCK) + t
            at = pl.ds(pl.multiple_of(b * BLOCK, BLOCK), BLOCK)
            here = hidden[:, at, :].reshape(side, width)
            mixed = dot(here, w_all[...]).astype(BF16)
            v = mixed[:, :width]
            swapped = mixed[:, width + 2 * KEY :]
            values[b] = v
            kq[b] = swapped
            q = jnp.where(first, mixed[:, width : width + 2 * KEY].astype(F32), 0.0).astype(BF16)
            scores = dot_nt(q, swapped) * scale
            weights = jnp.where(same, jnp.exp(scores), 0.0)
            att = weights * (1.0 / jnp.sum(weights, axis=1, keepdims=True))
            attention[b] = att
            att = att.astype(BF16)
            out = (dot(att, v) + here.astype(F32)).astype(BF16)
            joined[:, at, :] = out.reshape(METAS, BLOCK, width)
            wide = jnp.where(by_query, dot(att, by_key), 0.0)
            attended[at, :] = jnp.sum(wide.reshape(METAS, BLOCK, side), axis=0).astype(BF16)
            return c

        lax.fori_loop(0, HALF // BLOCK, forward, 0, unroll=UNROLL)

        logits = lax.fori_loop(
            0,
            METAS,
            lambda m, t: t + dot_nt(joined[m, part(h), :], class_rows_wide(m)),
            jnp.zeros((HALF, 256), F32),
        )
        class_at = iota((HALF, 256), 1)
        exps = jnp.where(class_at < class_count, jnp.exp(logits), 0.0)
        total = jnp.sum(exps, axis=1, keepdims=True)
        onehot = (labels[part(h), :] == class_at).astype(F32)
        loss_rows = jnp.log(total) - jnp.sum(onehot * logits, axis=1, keepdims=True)
        loss_acc[h] = jnp.zeros((8, 128), F32) + jnp.sum(loss_rows)
        dl = (seed * (exps / total - onehot)).astype(BF16)
        dlogits[part(h), :] = dl

        lane = iota((side, 128), 1)
        for j in range(GROUPS):
            g = lax.rem(me + j, GROUPS)
            choose = where_one(jnp.logical_and(iota((side, 128), 0) == lane + 2 * METAS * g - TAIL, lane >= TAIL) & (lane < TAIL + 2 * METAS))
            second = (dl[:, 128:].astype(F32) + dot(attended[part(h), :], choose)).astype(BF16)
            box = mail_in if j == 0 else mail
            box[g, part(h), :128] = dl[:, :128]
            box[g, part(h), 128:] = second
            if j:
                mail_to(g, h).start()

        def spread(m, c):
            d_joined[m, part(h), :] = dot(dl[:, :CLASS_PAD], class_rows(m)).astype(BF16)
            return c

        lax.fori_loop(0, METAS, spread, 0)

        def backward(t, c):
            b = h * (HALF // BLOCK) + t
            at = pl.ds(pl.multiple_of(b * BLOCK, BLOCK), BLOCK)
            dj = d_joined[:, at, :].reshape(side, width)
            att = attention[b]
            d_att = dot_nt(dj, values[b])
            mean = jnp.sum(att * d_att, axis=1, keepdims=True)
            d_scores = (att * (d_att - mean) * scale).astype(BF16)
            swapped = kq[b]
            grad = jnp.where(first, dot(d_scores, swapped), dot_tn(d_scores, swapped))
            d_vq[:, at, width:] = grad.astype(BF16).reshape(METAS, BLOCK, 2 * KEY)
            d_val = dot_tn(att.astype(BF16), dj)
            d_vq[:, at, :width] = d_val.astype(BF16).reshape(METAS, BLOCK, width)
            return c

        lax.fori_loop(0, HALF // BLOCK, backward, 0, unroll=UNROLL)
        for g in groups:
            keys_to(g, h).start()
        for m in range(2):
            d_vk[m, key_rows(me, h), width:] = d_vq[2 * me + m, part(h), width:]
        return carry

    def heads(*held):
        lax.fori_loop(0, 2, functools.partial(head, *held), 0)

    blocks = PAPERS // BLOCK
    pl.run_scoped(
        heads,
        pltpu.VMEM((blocks, side, width), BF16),
        pltpu.VMEM((blocks, side, side), F32),
        pltpu.VMEM((blocks, side, 2 * KEY), BF16),
    )

    def classes(g, carry):
        for m in range(2):
            grad = dot_tn(dlogits[:, :CLASS_PAD], joined[2 * g + m]).astype(BF16)
            for q in range(4):
                lanes = slice(q * 128, (q + 1) * 128)
                for p in range(2):
                    top = p * (CLASS_PAD // 2)
                    cx[p, g, 4 * m + q] = grad[top : top + META_ROWS, lanes]
                    cy[p, 4 * m + q, g] = grad[top + META_ROWS : top + CLASS_PAD // 2, lanes]
        return carry

    lax.fori_loop(0, GROUPS, classes, 0)
    c0 = [to_sibling(0, cx.at[other], cx_in), to_sibling(7, cy.at[other], cy_in)]
    for copy in c0:
        copy.start()

    batch = GROUPS * PAPERS
    part_rows = qv.shape[2]
    for c in range(4):
        cols = slice(c * 128, (c + 1) * 128)
        grad = dot_tn(
            hidden[:, :, cols].reshape(METAS * PAPERS, 128), d_vq[...].reshape(METAS * PAPERS, width + 2 * KEY)
        ).astype(BF16)
        for r in range(128 // part_rows):
            piece = c * (128 // part_rows) + r
            qv[piece // CHIPS, piece % CHIPS] = grad[r * part_rows : (r + 1) * part_rows]
    q0 = to_sibling(1, qv.at[other], qv_in)
    q0.start()

    for copy in c0:
        copy.wait_recv()

    def pair_class(g, carry):
        cx_in[g] = (cx[core, g].astype(F32) + cx_in[g].astype(F32)).astype(BF16)
        cy_in[g] = (cy[core, g].astype(F32) + cy_in[g].astype(F32)).astype(BF16)
        return carry

    lax.fori_loop(0, GROUPS, pair_class, 0)
    for k in chips:
        to_chip(0, k, cy_in.at[k], cy_chip.at[chip]).start()
    for g in groups:
        to_group(1, g, cx_in.at[g], cx_meta.at[me]).start()
    cx_meta[me] = cx_in[me]
    cy_chip[chip] = cy_in[chip]

    q0.wait_recv()

    def pair_qv(k, carry):
        qv_in[k] = (qv[core, k].astype(F32) + qv_in[k].astype(F32)).astype(BF16)
        return carry

    lax.fori_loop(0, CHIPS, pair_qv, 0)
    for k in chips:
        to_chip(2, k, qv_in.at[k], qv_chip.at[chip]).start()
    qv_chip[chip] = qv_in[chip]

    for g in groups:
        for h in range(2):
            mail_from(g, h).wait_recv()
    tail_lane = iota((128, TAIL * METAS), 1)
    tail_row = iota((128, TAIL * METAS), 0)
    repeat = where_one((tail_row < TAIL) & (lax.rem(tail_lane, TAIL) == tail_row))
    widen = [where_one(tail_row == TAIL + METAS * j + tail_lane // TAIL) for j in range(2)]

    def home_values(q, x_even, x_odd):
        def build(j, x):
            for u in range(2):
                s = lax.rem(2 * j + u, GROUPS)
                at = slice(u * PAPERS, (u + 1) * PAPERS)
                main = mail_in[s, :, :128].astype(F32)
                second = mail_in[s, :, 128:]
                second_f = second.astype(F32)
                x[at, tail_at:] = (dot(second, repeat) * dot(second, widen[q])).astype(BF16)
                for i in range(METAS):
                    lane = TAIL + METAS * q + i
                    x[at, 128 * i : 128 * (i + 1)] = (second_f[:, lane : lane + 1] * main).astype(BF16)

        def multiply(j, x):
            at = pl.ds(pl.multiple_of(2 * j * PAPERS, 2 * PAPERS), 2 * PAPERS)
            d_vk[q, at, :width] = dot(x[...], w_mix[...]).astype(BF16)

        build(0, x_even)

        def two(t, carry):
            build(2 * t + 1, x_odd)
            multiply(2 * t, x_even)
            build(2 * t + 2, x_even)
            multiply(2 * t + 1, x_odd)
            return carry

        lax.fori_loop(0, GROUPS // 4, two, 0)

    spread_shape = pltpu.VMEM((2 * PAPERS, METAS * CLASS_PAD), BF16)

    d_hidden = d_joined

    def home_hidden(m):
        def some(r, carry):
            at = pl.ds(pl.multiple_of(r * 2 * PAPERS, 2 * PAPERS), 2 * PAPERS)
            letters = mail_in[pl.ds(2 * r, 2)].reshape(2 * PAPERS, 256)[:, :CLASS_PAD]
            grad = dot(letters, class_rows(2 * me + m)) + dot(d_vk[m, at, :], w_back[...])
            d_hidden[pl.ds(GROUPS * m + 2 * r, 2)] = grad.astype(BF16).reshape(2, PAPERS, width)
            return carry

        lax.fori_loop(0, GROUPS // 2, some, 0)

    part_feat = gp.shape[3]

    def project(m, p):
        back = d_hidden[GROUPS * m : GROUPS * (m + 1)].reshape(batch, width)
        cols = pl.ds(pl.multiple_of(p * CHIPS * part_feat, 128), CHIPS * part_feat)
        grad = dot_tn(gathered[m, :, cols], back).astype(BF16)
        for k in range(CHIPS):
            gp[m, p, k] = grad[k * part_feat : (k + 1) * part_feat]

    def pair_proj(m):
        def one(k, carry):
            gp_in[m, k] = (gp[m, core, k].astype(F32) + gp_in[m, k].astype(F32)).astype(BF16)
            return carry

        lax.fori_loop(0, CHIPS, one, 0)
        for k in chips:
            to_chip(9 + m, k, gp_in.at[m, k], gp_chip.at[m, chip]).start()
        gp_chip[m, chip] = gp_in[m, chip]

    def across(m, k):
        here = gp_all.at[m, core, k]
        return remote(here, here, send_sem.at[13 + m, k], recv_sem.at[13 + m, k], sibling)

    def across_in(m, k):
        here = gp_all.at[m, other, k]
        return remote(here, here, send_sem.at[13 + m, k], recv_sem.at[13 + m, k], sibling)

    def chip_proj(m):
        for k in chips:
            from_chip(9 + m, k, gp_chip.at[m, k]).wait_recv()
        gp_all[m, core, chip] = jnp.sum(gp_chip[m].astype(F32), axis=0).astype(BF16)
        for k in chips:
            to_chip(11 + m, k, gp_all.at[m, core, chip], gp_all.at[m, core, chip]).start()
        across(m, chip).start()

    def pass_on(m):
        for k in chips:
            from_chip(11 + m, k, gp_all.at[m, core, k]).wait_recv()
            across(m, k).start()

    g0 = [to_sibling(2 + 4 * m, gp.at[m, other], gp_in.at[m]) for m in range(2)]

    def first_sum(m):
        project(m, other)
        g0[m].start()
        project(m, core)
        g0[m].wait_recv()
        pair_proj(m)

    pl.run_scoped(functools.partial(home_values, 0), spread_shape, spread_shape)
    for g in groups:
        for h in range(2):
            keys_from(g, h).wait_recv()
    home_hidden(0)
    first_sum(0)
    pl.run_scoped(functools.partial(home_values, 1), spread_shape, spread_shape)

    for k in chips:
        from_chip(0, k, cy_chip.at[k]).wait_recv()

    def chip_sum(g, carry):
        cy_sum[g] = jnp.sum(cy_chip[:, g].astype(F32), axis=0).astype(BF16)
        return carry

    lax.fori_loop(0, GROUPS, chip_sum, 0)
    for g in groups:
        to_group(15, g, cy_sum.at[g], cy_meta.at[me]).start()
    cy_meta[me] = cy_sum[me]

    for k in chips:
        from_chip(2, k, qv_chip.at[k]).wait_recv()
    qv_meta[me] = jnp.sum(qv_chip[...].astype(F32), axis=0).astype(BF16)
    loss_meta[me] = loss_acc[0] + loss_acc[1]
    for g in groups:
        to_group(4, g, qv_meta.at[me], qv_meta.at[me]).start()
        to_group(5, g, loss_meta.at[me], loss_meta.at[me]).start()

    home_hidden(1)
    chip_proj(0)
    first_sum(1)

    for g in groups:
        from_group(1, g, cx_meta.at[g]).wait_recv()

    def meta_sum(k, carry):
        cx_sum[k] = jnp.sum(cx_meta[:, k].astype(F32), axis=0).astype(BF16)
        return carry

    lax.fori_loop(0, CHIPS, meta_sum, 0)
    for k in chips:
        to_chip(3, k, cx_sum.at[k], cx_chip.at[chip]).start()
    cx_chip[chip] = cx_sum[chip]

    for g in groups:
        from_group(4, g, qv_meta.at[g]).wait_recv()
        from_group(5, g, loss_meta.at[g]).wait_recv()
        from_group(15, g, cy_meta.at[g]).wait_recv()
    qv_all[core, chip] = jnp.sum(qv_meta[...].astype(F32), axis=0).astype(BF16)
    loss_node[core, chip] = jnp.sum(loss_meta[...], axis=0)
    cls_all[core, chip, META_ROWS:, :] = jnp.sum(cy_meta[...].astype(F32), axis=0).astype(BF16)
    for k in chips:
        to_chip(7, k, qv_all.at[core, chip], qv_all.at[core, chip]).start()
        to_chip(8, k, loss_node.at[core, chip], loss_node.at[core, chip]).start()

    pass_on(0)

    for k in chips:
        from_chip(3, k, cx_chip.at[k]).wait_recv()
    cls_all[core, chip, :META_ROWS, :] = jnp.sum(cx_chip[...].astype(F32), axis=0).astype(BF16)
    for k in chips:
        to_chip(6, k, cls_all.at[core, chip], cls_all.at[core, chip]).start()

    chip_proj(1)

    for k in chips:
        from_chip(6, k, cls_all.at[core, k]).wait_recv()
        from_chip(7, k, qv_all.at[core, k]).wait_recv()
        from_chip(8, k, loss_node.at[core, k]).wait_recv()
    finals = [
        to_sibling(3, cls_all.at[core], cls_all.at[core]),
        to_sibling(4, qv_all.at[core], qv_all.at[core]),
        to_sibling(5, loss_node.at[core], loss_node.at[core]),
    ]
    for copy in finals:
        copy.start()

    pass_on(1)

    for m in range(2):
        for k in [chip] + chips:
            across_in(m, k).wait_recv()
    remote(cls_all.at[other], cls_all.at[other], sib_send.at[3], sib_recv.at[3], sibling).wait_recv()
    remote(qv_all.at[other], qv_all.at[other], sib_send.at[4], sib_recv.at[4], sibling).wait_recv()
    remote(loss_node.at[other], loss_node.at[other], sib_send.at[5], sib_recv.at[5], sibling).wait_recv()

    q0.wait_send()
    for copy in c0 + g0 + finals:
        copy.wait_send()
    for g in groups:
        for h in range(2):
            for m in range(2):
                out_copy(g, h, m).wait_send()
            mail_to(g, h).wait_send()
            keys_to(g, h).wait_send()
        to_group(1, g, cx_in.at[g], cx_meta.at[me]).wait_send()
        to_group(15, g, cy_sum.at[g], cy_meta.at[me]).wait_send()
        to_group(4, g, qv_meta.at[me], qv_meta.at[me]).wait_send()
        to_group(5, g, loss_meta.at[me], loss_meta.at[me]).wait_send()
    for k in chips:
        to_chip(2, k, qv_in.at[k], qv_chip.at[chip]).wait_send()
        to_chip(0, k, cy_in.at[k], cy_chip.at[chip]).wait_send()
        to_chip(3, k, cx_sum.at[k], cx_chip.at[chip]).wait_send()
        to_chip(6, k, cls_all.at[core, chip], cls_all.at[core, chip]).wait_send()
        to_chip(7, k, qv_all.at[core, chip], qv_all.at[core, chip]).wait_send()
        to_chip(8, k, loss_node.at[core, chip], loss_node.at[core, chip]).wait_send()
    for m in range(2):
        for k in chips:
            to_chip(9 + m, k, gp_in.at[m, k], gp_chip.at[m, chip]).wait_send()
            to_chip(11 + m, k, gp_all.at[m, core, chip], gp_all.at[m, core, chip]).wait_send()
        for k in [chip] + chips:
            across(m, k).wait_send()


def finish_kernel(
    batch_total, class_count,
    gp_hbm, cls_hbm, qv_hbm, loss_hbm, proj_hbm, qk_out, value_out, class_out, loss_out,
    gp, cls, qv, loss, proj, in_sem, out_sem,
):
    part_feat, width = gp.shape[3:]
    part_rows = qv.shape[2]
    half_rows = cls.shape[2]
    loads = [pltpu.make_async_copy(gp_hbm.at[m], gp.at[m], in_sem.at[m]) for m in range(2)]
    for q, (src, dst) in enumerate(((cls_hbm, cls), (qv_hbm, qv), (loss_hbm, loss))):
        loads.append(pltpu.make_async_copy(src, dst, in_sem.at[2 + q]))
    for load in loads:
        load.start()
    stores = []
    for m in range(2):
        loads[m].wait()
        for p in range(2):
            for k in range(CHIPS):
                start = (p * CHIPS + k) * part_feat
                proj[m, start : start + part_feat, :] = gp[m, p, k].astype(F32)
        stores.append(pltpu.make_async_copy(proj.at[m], proj_hbm.at[m], out_sem.at[m]))
        stores[m].start()
    for load in loads[2:]:
        load.wait()
    for p in range(2):
        for k in range(CHIPS):
            start = (p * CHIPS + k) * part_rows
            block = qv[p, k].astype(F32)
            value_out[start : start + part_rows, :] = block[:, :width]
            qk_out[start : start + part_rows, :] = block[:, width:]
            lanes = slice(k * 128, (k + 1) * 128)
            if p == 0:
                class_out[:half_rows, lanes] = cls[0, k].astype(F32)
            else:
                class_out[half_rows:, lanes] = cls[1, k].astype(F32)[: class_count - half_rows]
    loss_out[0, 0] = jnp.sum(loss[...].reshape(2 * CHIPS, 8, 128), axis=0)[0, 0] / batch_total
    for store in stores:
        store.wait()


def local(aggregates, batch_ids, labels, w_proj, w_qk, w_value, w_class):
    batch_total = labels.shape[0] * lax.axis_size("node")
    class_count = w_class.shape[0]
    count, rows, feat = aggregates.shape
    batch = batch_ids.shape[0]
    width = w_value.shape[0]
    side = BLOCK * METAS
    mixed = width + 2 * KEY
    half = CLASS_PAD // 2
    part = feat // (2 * CHIPS)
    part_rows = width // (2 * CHIPS)
    vmem = pl.BlockSpec(memory_space=pltpu.VMEM)
    anywhere = pl.BlockSpec(memory_space=pl.ANY)
    sums = pl.pallas_call(
        functools.partial(step_kernel, 1.0 / batch_total**0.5, class_count),
        out_shape=(
            jax.ShapeDtypeStruct((count, 2, CHIPS, part, width), BF16),
            jax.ShapeDtypeStruct((2, CHIPS, half, 128), BF16),
            jax.ShapeDtypeStruct((2, CHIPS, part_rows, mixed), BF16),
            jax.ShapeDtypeStruct((2, CHIPS, 8, 128), F32),
        ),
        in_specs=[vmem, vmem, anywhere, anywhere, vmem, vmem, anywhere],
        out_specs=(vmem,) * 4,
        scratch_shapes=[
            pltpu.SemaphoreType.DMA((10,)),
            pltpu.VMEM((PAPERS, 1), jnp.int32),
            pltpu.VMEM((count, batch, feat), BF16),
            pltpu.VMEM((count, GROUPS, PAPERS, width), BF16),
            pltpu.VMEM((METAS, PAPERS, width), BF16),
            pltpu.VMEM((width, width + 4 * KEY), BF16),
            pltpu.VMEM((mixed, width), BF16),
            pltpu.VMEM((METAS * CLASS_PAD, width), BF16),
            pltpu.VMEM((METAS, PAPERS, width), BF16),
            pltpu.VMEM((METAS, PAPERS, width), BF16),
            pltpu.VMEM((PAPERS, 256), BF16),
            pltpu.VMEM((PAPERS, side), BF16),
            pltpu.VMEM((GROUPS, PAPERS, 256), BF16),
            pltpu.VMEM((GROUPS, PAPERS, 256), BF16),
            pltpu.VMEM((METAS, PAPERS, mixed), BF16),
            pltpu.VMEM((count, batch, mixed), BF16),
            pltpu.VMEM((2, GROUPS, CHIPS, META_ROWS, 128), BF16),
            pltpu.VMEM((GROUPS, CHIPS, META_ROWS, 128), BF16),
            pltpu.VMEM((GROUPS, CHIPS, META_ROWS, 128), BF16),
            pltpu.VMEM((CHIPS, META_ROWS, 128), BF16),
            pltpu.VMEM((CHIPS, META_ROWS, 128), BF16),
            pltpu.VMEM((2, CHIPS, GROUPS, half - META_ROWS, 128), BF16),
            pltpu.VMEM((CHIPS, GROUPS, half - META_ROWS, 128), BF16),
            pltpu.VMEM((CHIPS, GROUPS, half - META_ROWS, 128), BF16),
            pltpu.VMEM((GROUPS, half - META_ROWS, 128), BF16),
            pltpu.VMEM((GROUPS, half - META_ROWS, 128), BF16),
            pltpu.VMEM((2, CHIPS, part_rows, mixed), BF16),
            pltpu.VMEM((CHIPS, part_rows, mixed), BF16),
            pltpu.VMEM((CHIPS, part_rows, mixed), BF16),
            pltpu.VMEM((GROUPS, part_rows, mixed), BF16),
            pltpu.VMEM((count, 2, CHIPS, part, width), BF16),
            pltpu.VMEM((count, CHIPS, part, width), BF16),
            pltpu.VMEM((count, CHIPS, part, width), BF16),
            pltpu.VMEM((2, 8, 128), F32),
            pltpu.VMEM((GROUPS, 8, 128), F32),
            pltpu.SemaphoreType.DMA((GROUPS, 4)),
            pltpu.SemaphoreType.DMA((GROUPS, 4)),
            pltpu.SemaphoreType.DMA((GROUPS, 4)),
            pltpu.SemaphoreType.DMA((GROUPS, 4)),
            pltpu.SemaphoreType.DMA((16, 8)),
            pltpu.SemaphoreType.DMA((16, 8)),
            pltpu.SemaphoreType.DMA((8,)),
            pltpu.SemaphoreType.DMA((8,)),
        ],
        compiler_params=pltpu.CompilerParams(
            collective_id=1, has_side_effects=True, vmem_limit_bytes=62 * 1024 * 1024
        ),
    )(
        batch_ids.reshape(batch // 128, 128), labels.reshape(batch // 128, 128), aggregates, w_proj, w_qk, w_value, w_class
    )
    grad_proj, grad_qk, grad_value, grad_class, loss = pl.pallas_call(
        functools.partial(finish_kernel, batch_total, class_count),
        out_shape=(
            jax.ShapeDtypeStruct((count, feat, width), F32),
            jax.ShapeDtypeStruct((width, 2 * KEY), F32),
            jax.ShapeDtypeStruct((width, width), F32),
            jax.ShapeDtypeStruct((class_count, count * width), F32),
            jax.ShapeDtypeStruct((1, 1), F32),
        ),
        in_specs=[anywhere] * 4,
        out_specs=(anywhere,) + (vmem,) * 3 + (pl.BlockSpec(memory_space=pltpu.SMEM),),
        scratch_shapes=[
            pltpu.VMEM((count, 2, CHIPS, part, width), BF16),
            pltpu.VMEM((2, CHIPS, half, 128), BF16),
            pltpu.VMEM((2, CHIPS, part_rows, mixed), BF16),
            pltpu.VMEM((2, CHIPS, 8, 128), F32),
            pltpu.VMEM((count, feat, width), F32),
            pltpu.SemaphoreType.DMA((5,)),
            pltpu.SemaphoreType.DMA((2,)),
        ],
        compiler_params=pltpu.CompilerParams(vmem_limit_bytes=62 * 1024 * 1024),
    )(*sums)
    return (grad_proj, grad_qk, grad_value, grad_class, loss.reshape(()))


def solution(mesh):
    in_specs = (P("meta", "node", None), P("node"), P("node"), P("meta", None, None), P(), P(), P())
    out_specs = (P("meta", None, None), P(), P(), P(None, "meta"), P())
    return jax.shard_map(local, mesh=mesh, in_specs=in_specs, out_specs=out_specs, check_vma=False)
```

```python
import functools

import jax
import jax.numpy as jnp
from jax import lax
from jax.experimental import pallas as pl
from jax.experimental.pallas import tpu as pltpu
from jax.sharding import PartitionSpec as P

MESH = pl.DeviceIdType.MESH
F32 = jnp.float32
BF16 = jnp.bfloat16
GROUPS = 8
CHIPS = 8
PAPERS = 192
HALF = 96
BLOCK = 16
METAS = 16
KEY = 64
CLASS_PAD = 160
TAIL = CLASS_PAD - 128
META_ROWS = 48
UNROLL = 6


def dot(a, b):
    return jnp.dot(a, b, preferred_element_type=F32)


def dot_nt(a, b):
    return lax.dot_general(a, b, (((1,), (1,)), ((), ())), preferred_element_type=F32)


def dot_tn(a, b):
    return lax.dot_general(a, b, (((0,), (0,)), ((), ())), preferred_element_type=F32)


def iota(shape, axis):
    return lax.broadcasted_iota(jnp.int32, shape, axis)


def where_one(mask):
    return mask.astype(F32).astype(BF16)


def remote(src, dst, send_sem, recv_sem, where):
    return pltpu.make_async_remote_copy(
        src_ref=src, dst_ref=dst, send_sem=send_sem, recv_sem=recv_sem, device_id=where, device_id_type=MESH
    )


def step_kernel(
    seed, class_count,
    ids_ref, labels_hbm, agg_hbm, w_proj_hbm, w_qk_hbm, w_value_hbm, w_class_hbm,
    gp_all, fin,
    load_sem, labels, gathered, outbox, hidden, w_all, w_back, w_mix,
    joined, d_joined, dlogits, attended, mail, mail_in, d_vq, d_vk,
    sx, sx_in, sx_meta, sx_sum, sx_chip, sy, sy_in, sy_chip, sy_sum, sy_meta,
    gp, gp_in, gp_chip, loss_acc,
    out_sem, in_sem, mail_send, mail_recv, send_sem, recv_sem, sib_send, sib_recv,
):
    me = lax.axis_index("meta")
    node = lax.axis_index("node")
    chip, core = node // 2, lax.rem(node, 2)
    other = 1 - core
    sibling = {"node": 2 * chip + other}
    groups = [lax.rem(me + j, GROUPS) for j in range(1, GROUPS)]
    chips = [lax.rem(chip + j, CHIPS) for j in range(1, CHIPS)]
    width = w_value_hbm.shape[0]
    rows, feat = agg_hbm.shape[1:]
    tail_at = 128 * METAS

    barrier = pltpu.get_barrier_semaphore()
    for g in groups:
        pl.semaphore_signal(barrier, inc=1, device_id={"meta": g}, device_id_type=MESH)
    for k in chips:
        pl.semaphore_signal(barrier, inc=1, device_id={"node": 2 * k + core}, device_id_type=MESH)
    pl.semaphore_signal(barrier, inc=1, device_id=sibling, device_id_type=MESH)

    def to_group(phase, g, src, dst):
        return remote(src, dst, send_sem.at[phase, g], recv_sem.at[phase, me], {"meta": g})

    def from_group(phase, g, dst):
        return remote(dst, dst, send_sem.at[phase, g], recv_sem.at[phase, g], {"meta": g})

    def to_chip(phase, k, src, dst):
        return remote(src, dst, send_sem.at[phase, k], recv_sem.at[phase, chip], {"node": 2 * k + core})

    def from_chip(phase, k, dst):
        return remote(dst, dst, send_sem.at[phase, k], recv_sem.at[phase, k], {"node": 2 * k + core})

    def to_sibling(phase, src, dst):
        return remote(src, dst, sib_send.at[phase], sib_recv.at[phase], sibling)

    def to_column(src, dst):
        eye = iota((128, 128), 0) == iota((128, 128), 1)
        for t in range(src.shape[0]):
            row = jnp.broadcast_to(src[t : t + 1, :].astype(F32), (128, 128))
            dst[t * 128 : (t + 1) * 128, :] = jnp.sum(jnp.where(eye, row, 0.0), axis=1, keepdims=True).astype(jnp.int32)

    def part(h):
        return pl.ds(pl.multiple_of(h * HALF, HALF), HALF)

    def out_copy(g, h, m):
        return remote(
            outbox.at[m, g, part(h), :],
            hidden.at[2 * me + m, part(h), :],
            out_sem.at[g, 2 * h + m],
            in_sem.at[me, 2 * h + m],
            {"meta": g},
        )

    def in_copy(g, h, m):
        here = hidden.at[2 * g + m, part(h), :]
        return remote(here, here, out_sem.at[g, 2 * h + m], in_sem.at[g, 2 * h + m], {"meta": g})

    def front(agg, w_proj, w_class, ids, labels_ref, w_qk, w_value):
        loads = []
        step = rows // 4
        for m in range(2):
            for q in range(4):
                at = pl.ds(q * step, step)
                loads.append(pltpu.make_async_copy(agg_hbm.at[m, at, :], agg.at[m, at, :], load_sem.at[4 * m + q]))
            loads.append(pltpu.make_async_copy(w_proj_hbm.at[m], w_proj.at[m], load_sem.at[8 + m]))
        later = [
            pltpu.make_async_copy(src, dst, load_sem.at[10 + q])
            for q, (src, dst) in enumerate(
                ((w_class_hbm, w_class), (labels_hbm, labels_ref), (w_qk_hbm, w_qk), (w_value_hbm, w_value))
            )
        ]
        for load in loads + later:
            load.start()
        to_column(ids_ref, ids)

        def project_pair(p, h, with_own):
            first = lax.rem(me // 2 + p + 1, 4) * 2 + lax.rem(me + p, 2)
            second = lax.rem(me // 2 + 3 - p, 4) * 2 + lax.rem(me + p + 1, 2)
            if with_own:
                second = me
            spots = [pl.ds(pl.multiple_of(g * PAPERS + h * HALF, HALF), HALF) for g in (first, second)]
            column = jnp.concatenate([ids[spot, :] for spot in spots], axis=0)
            picks = where_one(column == iota((2 * HALF, rows), 1))
            for m in range(2):
                if not with_own:

                    @pl.when(h + p == 0)
                    def _():
                        for load in loads[5 * m : 5 * m + 5]:
                            load.wait()

                got = dot(picks, agg[m]).astype(BF16)
                row = dot(got, w_proj[m]).astype(BF16)
                if m == 0 and not with_own:

                    @pl.when(h + p == 0)
                    def _():
                        pl.semaphore_wait(barrier, GROUPS - 1 + CHIPS)

                for q, g in enumerate((first, second)):
                    gathered[m, spots[q], :] = got[q * HALF : (q + 1) * HALF]
                    mine = row[q * HALF : (q + 1) * HALF]
                    outbox[m, g, part(h), :] = mine
                    if with_own and q == 1:
                        hidden[2 * me + m, part(h), :] = mine
                    else:
                        out_copy(g, h, m).start()

        def project_half(h, carry):
            def one(p, c):
                project_pair(p, h, False)
                return c

            lax.fori_loop(0, 3, one, 0)
            project_pair(3, h, True)
            return carry

        lax.fori_loop(0, 2, project_half, 0)

        for load in later:
            load.wait()
        to_column(labels_ref, ids)
        labels[...] = ids[pl.ds(pl.multiple_of(me * PAPERS, PAPERS), PAPERS), :]

        swap = where_one(lax.rem(iota((2 * KEY, 2 * KEY), 0) + KEY, 2 * KEY) == iota((2 * KEY, 2 * KEY), 1))
        w_all[:, :width] = w_value[...]
        w_all[:, width : width + 2 * KEY] = w_qk[...]
        w_all[:, width + 2 * KEY :] = dot(w_qk[...], swap).astype(BF16)
        w_back[:width, :] = w_value[...].astype(F32).T.astype(BF16)
        w_back[width:, :] = w_qk[...].astype(F32).T.astype(BF16)
        for m in range(METAS):
            lanes = slice(m * width, (m + 1) * width)
            w_mix[128 * m : 128 * (m + 1), :] = w_class[:128, lanes]
            last = w_class[128:class_count, lanes].astype(F32)
            zeros = jnp.zeros((CLASS_PAD - class_count, width), F32)
            w_mix[tail_at + TAIL * m : tail_at + TAIL * (m + 1), :] = jnp.concatenate([last, zeros], axis=0).astype(BF16)

    pl.run_scoped(
        front,
        pltpu.VMEM(agg_hbm.shape, BF16),
        pltpu.VMEM(w_proj_hbm.shape, BF16),
        pltpu.VMEM(w_class_hbm.shape, BF16),
        pltpu.VMEM((GROUPS * PAPERS, 1), jnp.int32),
        pltpu.VMEM(labels_hbm.shape, jnp.int32),
        pltpu.VMEM(w_qk_hbm.shape, BF16),
        pltpu.VMEM(w_value_hbm.shape, BF16),
    )
    def class_rows(m):
        main = w_mix[pl.ds(pl.multiple_of(128 * m, 128), 128), :]
        tail = w_mix[pl.ds(pl.multiple_of(tail_at + TAIL * m, TAIL), TAIL), :]
        return jnp.concatenate([main, tail], axis=0)

    def class_rows_wide(m):
        return jnp.concatenate([class_rows(m), jnp.zeros((256 - CLASS_PAD, width), BF16)], axis=0)

    scale = KEY ** (-0.5)
    side = BLOCK * METAS
    same = lax.rem(iota((side, side), 0), BLOCK) == lax.rem(iota((side, side), 1), BLOCK)
    first = iota((side, 2 * KEY), 1) < KEY
    by_key = where_one(iota((side, side), 0) // BLOCK == iota((side, side), 1) // BLOCK)
    by_query = iota((side, side), 0) // BLOCK == lax.rem(iota((side, side), 1), METAS)

    def mail_to(g, h):
        return remote(
            mail.at[g, part(h), :], mail_in.at[me, part(h), :], mail_send.at[g, h], mail_recv.at[me, h], {"meta": g}
        )

    def mail_from(g, h):
        here = mail_in.at[g, part(h), :]
        return remote(here, here, mail_send.at[g, h], mail_recv.at[g, h], {"meta": g})

    def head(values, attention, kq, h, carry):
        for g in groups:
            for m in range(2):
                in_copy(g, h, m).wait_recv()

        def forward(t, c):
            b = h * (HALF // BLOCK) + t
            at = pl.ds(pl.multiple_of(b * BLOCK, BLOCK), BLOCK)
            here = hidden[:, at, :].reshape(side, width)
            mixed = dot(here, w_all[...]).astype(BF16)
            v = mixed[:, :width]
            swapped = mixed[:, width + 2 * KEY :]
            values[b] = v
            kq[b] = swapped
            q = jnp.where(first, mixed[:, width : width + 2 * KEY].astype(F32), 0.0).astype(BF16)
            scores = dot_nt(q, swapped) * scale
            weights = jnp.where(same, jnp.exp(scores), 0.0)
            att = weights * (1.0 / jnp.sum(weights, axis=1, keepdims=True))
            attention[b] = att
            att = att.astype(BF16)
            out = (dot(att, v) + here.astype(F32)).astype(BF16)
            joined[:, at, :] = out.reshape(METAS, BLOCK, width)
            wide = jnp.where(by_query, dot(att, by_key), 0.0)
            attended[at, :] = jnp.sum(wide.reshape(METAS, BLOCK, side), axis=0).astype(BF16)
            return c

        lax.fori_loop(0, HALF // BLOCK, forward, 0, unroll=UNROLL)

        logits = lax.fori_loop(
            0,
            METAS,
            lambda m, t: t + dot_nt(joined[m, part(h), :], class_rows_wide(m)),
            jnp.zeros((HALF, 256), F32),
        )
        class_at = iota((HALF, 256), 1)
        exps = jnp.where(class_at < class_count, jnp.exp(logits), 0.0)
        total = jnp.sum(exps, axis=1, keepdims=True)
        onehot = (labels[part(h), :] == class_at).astype(F32)
        loss_rows = jnp.log(total) - jnp.sum(onehot * logits, axis=1, keepdims=True)
        loss_acc[h] = jnp.zeros((8, 128), F32) + jnp.sum(loss_rows)
        dl = (seed * (exps / total - onehot)).astype(BF16)
        dlogits[part(h), :] = dl

        lane = iota((side, 128), 1)
        for j in range(GROUPS):
            g = lax.rem(me + j, GROUPS)
            choose = where_one(jnp.logical_and(iota((side, 128), 0) == lane + 2 * METAS * g - TAIL, lane >= TAIL) & (lane < TAIL + 2 * METAS))
            second = (dl[:, 128:].astype(F32) + dot(attended[part(h), :], choose)).astype(BF16)
            box = mail_in if j == 0 else mail
            box[g, part(h), :128] = dl[:, :128]
            box[g, part(h), 128:256] = second

        def spread(m, c):
            d_joined[m, part(h), :] = dot(dl[:, :CLASS_PAD], class_rows(m)).astype(BF16)
            return c

        lax.fori_loop(0, METAS, spread, 0)

        def backward(t, c):
            b = h * (HALF // BLOCK) + t
            at = pl.ds(pl.multiple_of(b * BLOCK, BLOCK), BLOCK)
            dj = d_joined[:, at, :].reshape(side, width)
            att = attention[b]
            d_att = dot_nt(dj, values[b])
            mean = jnp.sum(att * d_att, axis=1, keepdims=True)
            d_scores = (att * (d_att - mean) * scale).astype(BF16)
            swapped = kq[b]
            grad = jnp.where(first, dot(d_scores, swapped), dot_tn(d_scores, swapped))
            d_vq[:, at, width:] = grad.astype(BF16).reshape(METAS, BLOCK, 2 * KEY)
            d_val = dot_tn(att.astype(BF16), dj)
            d_vq[:, at, :width] = d_val.astype(BF16).reshape(METAS, BLOCK, width)
            return c

        lax.fori_loop(0, HALF // BLOCK, backward, 0, unroll=UNROLL)
        for j in range(GROUPS):
            g = lax.rem(me + j, GROUPS)
            box = mail_in if j == 0 else mail
            for m in range(2):
                lanes = slice(256 + 2 * KEY * m, 256 + 2 * KEY * (m + 1))
                box[g, part(h), lanes] = d_vq[2 * g + m, part(h), width:]
            if j:
                mail_to(g, h).start()
        return carry

    def heads(*held):
        lax.fori_loop(0, 2, functools.partial(head, *held), 0)

    blocks = PAPERS // BLOCK
    pl.run_scoped(
        heads,
        pltpu.VMEM((blocks, side, width), BF16),
        pltpu.VMEM((blocks, side, side), F32),
        pltpu.VMEM((blocks, side, 2 * KEY), BF16),
    )

    node_rows = CLASS_PAD // 2 - META_ROWS
    loss_part = loss_acc[0][:1, :1] + loss_acc[1][:1, :1]

    def classes(g, carry):
        for m in range(2):
            grad = dot_tn(dlogits[:, :CLASS_PAD], joined[2 * g + m])
            grad = jnp.where(iota((CLASS_PAD, width), 0) == class_count, loss_part, grad).astype(BF16)
            for q in range(4):
                lanes = slice(q * 128, (q + 1) * 128)
                for p in range(2):
                    top = p * (CLASS_PAD // 2)
                    sx[p, g, 4 * m + q] = grad[top : top + META_ROWS, lanes]
                    sy[p, 4 * m + q, pl.ds(pl.multiple_of(g * node_rows, node_rows), node_rows), :] = grad[top + META_ROWS : top + CLASS_PAD // 2, lanes]
        return carry

    lax.fori_loop(0, GROUPS, classes, 0)
    c0 = [to_sibling(0, sx.at[other], sx_in), to_sibling(1, sy.at[other], sy_in)]
    c0[0].start()

    batch = GROUPS * PAPERS
    qv_at = GROUPS * node_rows
    qv_rows = width // (2 * CHIPS)
    tiles = (width + 2 * KEY) // 128
    for c in range(4):
        cols = slice(c * 128, (c + 1) * 128)
        grad = dot_tn(
            hidden[:, :, cols].reshape(METAS * PAPERS, 128), d_vq[...].reshape(METAS * PAPERS, width + 2 * KEY)
        ).astype(BF16)
        for r in range(128 // qv_rows):
            piece = c * (128 // qv_rows) + r
            for t in range(tiles):
                sy[piece // CHIPS, piece % CHIPS, qv_at + t * qv_rows : qv_at + (t + 1) * qv_rows, :] = grad[
                    r * qv_rows : (r + 1) * qv_rows, t * 128 : (t + 1) * 128
                ]
    c0[1].start()

    c0[0].wait_recv()

    def pair_x(g, carry):
        sx_in[g] = (sx[core, g].astype(F32) + sx_in[g].astype(F32)).astype(BF16)
        return carry

    lax.fori_loop(0, GROUPS, pair_x, 0)
    for g in groups:
        to_group(1, g, sx_in.at[g], sx_meta.at[me]).start()
    sx_meta[me] = sx_in[me]

    c0[1].wait_recv()

    def pair_y(k, carry):
        sy_in[k] = (sy[core, k].astype(F32) + sy_in[k].astype(F32)).astype(BF16)
        return carry

    lax.fori_loop(0, CHIPS, pair_y, 0)
    for k in chips:
        to_chip(2, k, sy_in.at[k], sy_chip.at[chip]).start()
    sy_chip[chip] = sy_in[chip]

    for g in groups:
        for h in range(2):
            mail_from(g, h).wait_recv()
    tail_lane = iota((128, TAIL * METAS), 1)
    tail_row = iota((128, TAIL * METAS), 0)
    repeat = where_one((tail_row < TAIL) & (lax.rem(tail_lane, TAIL) == tail_row))
    widen = [where_one(tail_row == TAIL + METAS * j + tail_lane // TAIL) for j in range(2)]

    def home_values(q, x_even, x_odd):
        def build(j, x):
            for u in range(2):
                s = lax.rem(2 * j + u, GROUPS)
                at = slice(u * PAPERS, (u + 1) * PAPERS)
                main = mail_in[s, :, :128].astype(F32)
                second = mail_in[s, :, 128:256]
                second_f = second.astype(F32)
                x[at, tail_at:] = (dot(second, repeat) * dot(second, widen[q])).astype(BF16)
                for i in range(METAS):
                    lane = TAIL + METAS * q + i
                    x[at, 128 * i : 128 * (i + 1)] = (second_f[:, lane : lane + 1] * main).astype(BF16)

        def multiply(j, x):
            at = pl.ds(pl.multiple_of(2 * j * PAPERS, 2 * PAPERS), 2 * PAPERS)
            d_vk[q, at, :] = dot(x[...], w_mix[...]).astype(BF16)

        build(0, x_even)

        def two(t, carry):
            build(2 * t + 1, x_odd)
            multiply(2 * t, x_even)
            build(2 * t + 2, x_even)
            multiply(2 * t + 1, x_odd)
            return carry

        lax.fori_loop(0, GROUPS // 4, two, 0)

    spread_shape = pltpu.VMEM((2 * PAPERS, METAS * CLASS_PAD), BF16)

    d_hidden = d_joined

    def home_hidden(m):
        def some(r, carry):
            at = pl.ds(pl.multiple_of(r * 2 * PAPERS, 2 * PAPERS), 2 * PAPERS)
            letters = mail_in[pl.ds(2 * r, 2)].reshape(2 * PAPERS, 512)
            keys = letters[:, 256 + 2 * KEY * m : 256 + 2 * KEY * (m + 1)]
            both = jnp.concatenate([d_vk[m, at, :], keys], axis=1)
            grad = dot(letters[:, :CLASS_PAD], class_rows(2 * me + m)) + dot(both, w_back[...])
            d_hidden[pl.ds(GROUPS * m + 2 * r, 2)] = grad.astype(BF16).reshape(2, PAPERS, width)
            return carry

        lax.fori_loop(0, GROUPS // 2, some, 0)

    part_feat = gp.shape[3]

    def project(m, p):
        back = d_hidden[GROUPS * m : GROUPS * (m + 1)].reshape(batch, width)
        cols = pl.ds(pl.multiple_of(p * CHIPS * part_feat, 128), CHIPS * part_feat)
        grad = dot_tn(gathered[m, :, cols], back).astype(BF16)
        for k in range(CHIPS):
            gp[m, p, k] = grad[k * part_feat : (k + 1) * part_feat]

    def pair_proj(m):
        def one(k, carry):
            gp_in[m, k] = (gp[m, core, k].astype(F32) + gp_in[m, k].astype(F32)).astype(BF16)
            return carry

        lax.fori_loop(0, CHIPS, one, 0)
        for k in chips:
            to_chip(9 + m, k, gp_in.at[m, k], gp_chip.at[m, chip]).start()
        gp_chip[m, chip] = gp_in[m, chip]

    def across(m):
        return to_sibling(3 + m, gp_all.at[m, core], gp_all.at[m, core])

    def across_in(m):
        here = gp_all.at[m, other]
        return remote(here, here, sib_send.at[3 + m], sib_recv.at[3 + m], sibling)

    def chip_proj(m):
        for k in chips:
            from_chip(9 + m, k, gp_chip.at[m, k]).wait_recv()
        gp_all[m, core, chip] = jnp.sum(gp_chip[m].astype(F32), axis=0).astype(BF16)
        for k in chips:
            to_chip(11 + m, k, gp_all.at[m, core, chip], gp_all.at[m, core, chip]).start()

    def pass_on(m):
        for k in chips:
            from_chip(11 + m, k, gp_all.at[m, core, k]).wait_recv()
        across(m).start()

    g0 = [to_sibling(5 + m, gp.at[m, other], gp_in.at[m]) for m in range(2)]

    def first_sum(m):
        project(m, other)
        g0[m].start()
        project(m, core)
        g0[m].wait_recv()
        pair_proj(m)

    pl.run_scoped(functools.partial(home_values, 0), spread_shape, spread_shape)
    home_hidden(0)
    first_sum(0)

    for k in chips:
        from_chip(2, k, sy_chip.at[k]).wait_recv()
    qv_sum = jnp.sum(sy_chip[:, qv_at:, :].astype(F32), axis=0).astype(BF16)

    def chip_sum(g, carry):
        at = pl.ds(pl.multiple_of(g * node_rows, node_rows), node_rows)
        sy_sum[g, :node_rows, :] = jnp.sum(sy_chip[:, at, :].astype(F32), axis=0).astype(BF16)
        return carry

    lax.fori_loop(0, GROUPS, chip_sum, 0)
    for g in range(GROUPS):
        sy_sum[g, node_rows:, :] = qv_sum
    for g in groups:
        to_group(3, g, sy_sum.at[g], sy_meta.at[me]).start()
    sy_meta[me] = sy_sum[me]

    pl.run_scoped(functools.partial(home_values, 1), spread_shape, spread_shape)

    for g in groups:
        from_group(1, g, sx_meta.at[g]).wait_recv()

    def meta_sum(k, carry):
        sx_sum[k] = jnp.sum(sx_meta[:, k].astype(F32), axis=0).astype(BF16)
        return carry

    lax.fori_loop(0, CHIPS, meta_sum, 0)
    for k in chips:
        to_chip(4, k, sx_sum.at[k], sx_chip.at[chip]).start()
    sx_chip[chip] = sx_sum[chip]

    home_hidden(1)
    chip_proj(0)
    first_sum(1)

    for g in groups:
        from_group(3, g, sy_meta.at[g]).wait_recv()
    fin[core, chip, META_ROWS:, :] = jnp.sum(sy_meta[...].astype(F32), axis=0).astype(BF16)
    for k in chips:
        from_chip(4, k, sx_chip.at[k]).wait_recv()
    fin[core, chip, :META_ROWS, :] = jnp.sum(sx_chip[...].astype(F32), axis=0).astype(BF16)
    for k in chips:
        to_chip(6, k, fin.at[core, chip], fin.at[core, chip]).start()

    pass_on(0)

    chip_proj(1)

    for k in chips:
        from_chip(6, k, fin.at[core, k]).wait_recv()
    last = to_sibling(2, fin.at[core], fin.at[core])
    last.start()

    pass_on(1)

    for m in range(2):
        across_in(m).wait_recv()
    remote(fin.at[other], fin.at[other], sib_send.at[2], sib_recv.at[2], sibling).wait_recv()

    last.wait_send()
    for copy in c0 + g0:
        copy.wait_send()
    for g in groups:
        for h in range(2):
            for m in range(2):
                out_copy(g, h, m).wait_send()
            mail_to(g, h).wait_send()
        to_group(1, g, sx_in.at[g], sx_meta.at[me]).wait_send()
        to_group(3, g, sy_sum.at[g], sy_meta.at[me]).wait_send()
    for k in chips:
        to_chip(2, k, sy_in.at[k], sy_chip.at[chip]).wait_send()
        to_chip(4, k, sx_sum.at[k], sx_chip.at[chip]).wait_send()
        to_chip(6, k, fin.at[core, chip], fin.at[core, chip]).wait_send()
    for m in range(2):
        for k in chips:
            to_chip(9 + m, k, gp_in.at[m, k], gp_chip.at[m, chip]).wait_send()
            to_chip(11 + m, k, gp_all.at[m, core, chip], gp_all.at[m, core, chip]).wait_send()
        across(m).wait_send()


def finish_kernel(
    batch_total, class_count,
    gp_hbm, fin_hbm, proj_hbm, qk_out, value_out, class_out, loss_out,
    gp, fin, proj, in_sem, out_sem,
):
    part_feat, width = gp.shape[3:]
    qv_rows = width // (2 * CHIPS)
    half_rows = CLASS_PAD // 2
    loads = [pltpu.make_async_copy(gp_hbm.at[m], gp.at[m], in_sem.at[m]) for m in range(2)]
    loads.append(pltpu.make_async_copy(fin_hbm, fin, in_sem.at[2]))
    for load in loads:
        load.start()
    stores = []
    for m in range(2):
        loads[m].wait()
        for p in range(2):
            for k in range(CHIPS):
                start = (p * CHIPS + k) * part_feat
                proj[m, start : start + part_feat, :] = gp[m, p, k].astype(F32)
        stores.append(pltpu.make_async_copy(proj.at[m], proj_hbm.at[m], out_sem.at[m]))
        stores[m].start()
    loads[2].wait()
    left = class_count - half_rows
    for p in range(2):
        for k in range(CHIPS):
            start = (p * CHIPS + k) * qv_rows
            for t in range(width // 128 + 1):
                block = fin[p, k, half_rows + t * qv_rows : half_rows + (t + 1) * qv_rows, :].astype(F32)
                if t < width // 128:
                    value_out[start : start + qv_rows, t * 128 : (t + 1) * 128] = block
                else:
                    qk_out[start : start + qv_rows, :] = block
            lanes = slice(k * 128, (k + 1) * 128)
            block = fin[p, k, :half_rows, :].astype(F32)
            if p == 0:
                class_out[:half_rows, lanes] = block
            else:
                class_out[half_rows:, lanes] = block[:left]
    loss_out[0, 0] = fin[1, 0, :half_rows, :].astype(F32)[left, 0] / batch_total
    for store in stores:
        store.wait()


def local(aggregates, batch_ids, labels, w_proj, w_qk, w_value, w_class):
    batch_total = labels.shape[0] * lax.axis_size("node")
    class_count = w_class.shape[0]
    count, rows, feat = aggregates.shape
    batch = batch_ids.shape[0]
    width = w_value.shape[0]
    side = BLOCK * METAS
    mixed = width + 2 * KEY
    half = CLASS_PAD // 2
    part = feat // (2 * CHIPS)
    node_rows = half - META_ROWS
    qv_rows = width // (2 * CHIPS) * (mixed // 128)
    fin_rows = half + qv_rows
    vmem = pl.BlockSpec(memory_space=pltpu.VMEM)
    anywhere = pl.BlockSpec(memory_space=pl.ANY)
    sums = pl.pallas_call(
        functools.partial(step_kernel, 1.0 / batch_total**0.5, class_count),
        out_shape=(
            jax.ShapeDtypeStruct((count, 2, CHIPS, part, width), BF16),
            jax.ShapeDtypeStruct((2, CHIPS, fin_rows, 128), BF16),
        ),
        in_specs=[vmem] + [anywhere] * 6,
        out_specs=(vmem,) * 2,
        scratch_shapes=[
            pltpu.SemaphoreType.DMA((14,)),
            pltpu.VMEM((PAPERS, 1), jnp.int32),
            pltpu.VMEM((count, batch, feat), BF16),
            pltpu.VMEM((count, GROUPS, PAPERS, width), BF16),
            pltpu.VMEM((METAS, PAPERS, width), BF16),
            pltpu.VMEM((width, width + 4 * KEY), BF16),
            pltpu.VMEM((mixed, width), BF16),
            pltpu.VMEM((METAS * CLASS_PAD, width), BF16),
            pltpu.VMEM((METAS, PAPERS, width), BF16),
            pltpu.VMEM((METAS, PAPERS, width), BF16),
            pltpu.VMEM((PAPERS, 256), BF16),
            pltpu.VMEM((PAPERS, side), BF16),
            pltpu.VMEM((GROUPS, PAPERS, 512), BF16),
            pltpu.VMEM((GROUPS, PAPERS, 512), BF16),
            pltpu.VMEM((METAS, PAPERS, mixed), BF16),
            pltpu.VMEM((count, batch, width), BF16),
            pltpu.VMEM((2, GROUPS, CHIPS, META_ROWS, 128), BF16),
            pltpu.VMEM((GROUPS, CHIPS, META_ROWS, 128), BF16),
            pltpu.VMEM((GROUPS, CHIPS, META_ROWS, 128), BF16),
            pltpu.VMEM((CHIPS, META_ROWS, 128), BF16),
            pltpu.VMEM((CHIPS, META_ROWS, 128), BF16),
            pltpu.VMEM((2, CHIPS, GROUPS * node_rows + qv_rows, 128), BF16),
            pltpu.VMEM((CHIPS, GROUPS * node_rows + qv_rows, 128), BF16),
            pltpu.VMEM((CHIPS, GROUPS * node_rows + qv_rows, 128), BF16),
            pltpu.VMEM((GROUPS, node_rows + qv_rows, 128), BF16),
            pltpu.VMEM((GROUPS, node_rows + qv_rows, 128), BF16),
            pltpu.VMEM((count, 2, CHIPS, part, width), BF16),
            pltpu.VMEM((count, CHIPS, part, width), BF16),
            pltpu.VMEM((count, CHIPS, part, width), BF16),
            pltpu.VMEM((2, 8, 128), F32),
            pltpu.SemaphoreType.DMA((GROUPS, 4)),
            pltpu.SemaphoreType.DMA((GROUPS, 4)),
            pltpu.SemaphoreType.DMA((GROUPS, 2)),
            pltpu.SemaphoreType.DMA((GROUPS, 2)),
            pltpu.SemaphoreType.DMA((16, 8)),
            pltpu.SemaphoreType.DMA((16, 8)),
            pltpu.SemaphoreType.DMA((8,)),
            pltpu.SemaphoreType.DMA((8,)),
        ],
        compiler_params=pltpu.CompilerParams(
            collective_id=1, has_side_effects=True, vmem_limit_bytes=62 * 1024 * 1024
        ),
    )(
        batch_ids.reshape(batch // 128, 128), labels.reshape(batch // 128, 128), aggregates, w_proj, w_qk, w_value, w_class
    )
    grad_proj, grad_qk, grad_value, grad_class, loss = pl.pallas_call(
        functools.partial(finish_kernel, batch_total, class_count),
        out_shape=(
            jax.ShapeDtypeStruct((count, feat, width), F32),
            jax.ShapeDtypeStruct((width, 2 * KEY), F32),
            jax.ShapeDtypeStruct((width, width), F32),
            jax.ShapeDtypeStruct((class_count, count * width), F32),
            jax.ShapeDtypeStruct((1, 1), F32),
        ),
        in_specs=[anywhere] * 2,
        out_specs=(anywhere,) + (vmem,) * 3 + (pl.BlockSpec(memory_space=pltpu.SMEM),),
        scratch_shapes=[
            pltpu.VMEM((count, 2, CHIPS, part, width), BF16),
            pltpu.VMEM((2, CHIPS, fin_rows, 128), BF16),
            pltpu.VMEM((count, feat, width), F32),
            pltpu.SemaphoreType.DMA((3,)),
            pltpu.SemaphoreType.DMA((2,)),
        ],
        compiler_params=pltpu.CompilerParams(vmem_limit_bytes=62 * 1024 * 1024),
    )(*sums)
    return (grad_proj, grad_qk, grad_value, grad_class, loss.reshape(()))


def solution(mesh):
    in_specs = (P("meta", "node", None), P("node"), P("node"), P("meta", None, None), P(), P(), P())
    out_specs = (P("meta", None, None), P(), P(), P(None, "meta"), P())
    return jax.shard_map(local, mesh=mesh, in_specs=in_specs, out_specs=out_specs, check_vma=False)
```

```python
import functools

import jax
import jax.numpy as jnp
from jax import lax
from jax.experimental import pallas as pl
from jax.experimental.pallas import tpu as pltpu
from jax.sharding import PartitionSpec as P

MESH = pl.DeviceIdType.MESH
F32 = jnp.float32
BF16 = jnp.bfloat16
GROUPS = 8
CHIPS = 8
PAPERS = 192
HALF = 96
BLOCK = 16
METAS = 16
KEY = 64
CLASS_PAD = 160
TAIL = CLASS_PAD - 128
META_ROWS = 48
UNROLL = 6


def dot(a, b):
    return jnp.dot(a, b, preferred_element_type=F32)


def dot_nt(a, b):
    return lax.dot_general(a, b, (((1,), (1,)), ((), ())), preferred_element_type=F32)


def dot_tn(a, b):
    return lax.dot_general(a, b, (((0,), (0,)), ((), ())), preferred_element_type=F32)


def iota(shape, axis):
    return lax.broadcasted_iota(jnp.int32, shape, axis)


def where_one(mask):
    return mask.astype(F32).astype(BF16)


def remote(src, dst, send_sem, recv_sem, where):
    return pltpu.make_async_remote_copy(
        src_ref=src, dst_ref=dst, send_sem=send_sem, recv_sem=recv_sem, device_id=where, device_id_type=MESH
    )


def step_kernel(
    seed, class_count,
    ids_ref, labels_ref, agg_hbm, w_proj_hbm, w_qk, w_value, w_class_hbm,
    gp_all, cls_all, qv_all, loss_node,
    load_sem, labels, gathered, outbox, hidden, w_all, w_back, w_mix,
    joined, d_joined, dlogits, attended, mail, mail_in, d_vq, d_vk,
    cx, cx_in, cx_meta, cx_sum, cx_chip, cy, cy_in, cy_chip, cy_sum, cy_meta,
    qv, qv_in, qv_chip, qv_meta,
    gp, gp_in, gp_chip, loss_acc, loss_meta,
    out_sem, in_sem, mail_send, mail_recv, send_sem, recv_sem, sib_send, sib_recv,
):
    me = lax.axis_index("meta")
    node = lax.axis_index("node")
    chip, core = node // 2, lax.rem(node, 2)
    other = 1 - core
    sibling = {"node": 2 * chip + other}
    groups = [lax.rem(me + j, GROUPS) for j in range(1, GROUPS)]
    chips = [lax.rem(chip + j, CHIPS) for j in range(1, CHIPS)]
    width = w_value.shape[0]
    rows, feat = agg_hbm.shape[1:]
    tail_at = 128 * METAS

    barrier = pltpu.get_barrier_semaphore()
    for g in groups:
        pl.semaphore_signal(barrier, inc=1, device_id={"meta": g}, device_id_type=MESH)
    for k in chips:
        pl.semaphore_signal(barrier, inc=1, device_id={"node": 2 * k + core}, device_id_type=MESH)
    pl.semaphore_signal(barrier, inc=1, device_id=sibling, device_id_type=MESH)

    def to_group(phase, g, src, dst):
        return remote(src, dst, send_sem.at[phase, g], recv_sem.at[phase, me], {"meta": g})

    def from_group(phase, g, dst):
        return remote(dst, dst, send_sem.at[phase, g], recv_sem.at[phase, g], {"meta": g})

    def to_chip(phase, k, src, dst):
        return remote(src, dst, send_sem.at[phase, k], recv_sem.at[phase, chip], {"node": 2 * k + core})

    def from_chip(phase, k, dst):
        return remote(dst, dst, send_sem.at[phase, k], recv_sem.at[phase, k], {"node": 2 * k + core})

    def to_sibling(phase, src, dst):
        return remote(src, dst, sib_send.at[phase], sib_recv.at[phase], sibling)

    def to_column(src, dst):
        eye = iota((128, 128), 0) == iota((128, 128), 1)
        for t in range(src.shape[0]):
            row = jnp.broadcast_to(src[t : t + 1, :].astype(F32), (128, 128))
            dst[t * 128 : (t + 1) * 128, :] = jnp.sum(jnp.where(eye, row, 0.0), axis=1, keepdims=True).astype(jnp.int32)

    def part(h):
        return pl.ds(pl.multiple_of(h * HALF, HALF), HALF)

    def out_copy(g, h, m):
        return remote(
            outbox.at[m, g, part(h), :],
            hidden.at[2 * me + m, part(h), :],
            out_sem.at[g, 2 * h + m],
            in_sem.at[me, 2 * h + m],
            {"meta": g},
        )

    def in_copy(g, h, m):
        here = hidden.at[2 * g + m, part(h), :]
        return remote(here, here, out_sem.at[g, 2 * h + m], in_sem.at[g, 2 * h + m], {"meta": g})

    def front(agg, w_proj, w_class, ids):
        loads = []
        step = rows // 4
        for m in range(2):
            for q in range(4):
                at = pl.ds(q * step, step)
                loads.append(pltpu.make_async_copy(agg_hbm.at[m, at, :], agg.at[m, at, :], load_sem.at[4 * m + q]))
        loads.append(pltpu.make_async_copy(w_proj_hbm, w_proj, load_sem.at[8]))
        loads.append(pltpu.make_async_copy(w_class_hbm, w_class, load_sem.at[9]))
        for load in loads:
            load.start()
        to_column(ids_ref, ids)
        for load in loads[:9]:
            load.wait()
        pl.semaphore_wait(barrier, GROUPS - 1 + CHIPS)

        def project_pair(p, h, with_own):
            first = lax.rem(me // 2 + p + 1, 4) * 2 + lax.rem(me + p, 2)
            second = lax.rem(me // 2 + 3 - p, 4) * 2 + lax.rem(me + p + 1, 2)
            if with_own:
                second = me
            spots = [pl.ds(pl.multiple_of(g * PAPERS + h * HALF, HALF), HALF) for g in (first, second)]
            column = jnp.concatenate([ids[spot, :] for spot in spots], axis=0)
            picks = where_one(column == iota((2 * HALF, rows), 1))
            for m in range(2):
                got = dot(picks, agg[m]).astype(BF16)
                row = dot(got, w_proj[m]).astype(BF16)
                for q, g in enumerate((first, second)):
                    gathered[m, spots[q], :] = got[q * HALF : (q + 1) * HALF]
                    mine = row[q * HALF : (q + 1) * HALF]
                    outbox[m, g, part(h), :] = mine
                    if with_own and q == 1:
                        hidden[2 * me + m, part(h), :] = mine
                    else:
                        out_copy(g, h, m).start()

        def project_half(h, carry):
            def one(p, c):
                project_pair(p, h, False)
                return c

            lax.fori_loop(0, 3, one, 0)
            project_pair(3, h, True)
            return carry

        lax.fori_loop(0, 2, project_half, 0)

        to_column(labels_ref, ids)
        labels[...] = ids[pl.ds(pl.multiple_of(me * PAPERS, PAPERS), PAPERS), :]

        swap = where_one(lax.rem(iota((2 * KEY, 2 * KEY), 0) + KEY, 2 * KEY) == iota((2 * KEY, 2 * KEY), 1))
        w_all[:, :width] = w_value[...]
        w_all[:, width : width + 2 * KEY] = w_qk[...]
        w_all[:, width + 2 * KEY :] = dot(w_qk[...], swap).astype(BF16)
        w_back[:width, :] = w_value[...].astype(F32).T.astype(BF16)
        w_back[width:, :] = w_qk[...].astype(F32).T.astype(BF16)
        loads[9].wait()
        for m in range(METAS):
            lanes = slice(m * width, (m + 1) * width)
            w_mix[128 * m : 128 * (m + 1), :] = w_class[:128, lanes]
            last = w_class[128:class_count, lanes].astype(F32)
            zeros = jnp.zeros((CLASS_PAD - class_count, width), F32)
            w_mix[tail_at + TAIL * m : tail_at + TAIL * (m + 1), :] = jnp.concatenate([last, zeros], axis=0).astype(BF16)

    pl.run_scoped(
        front,
        pltpu.VMEM(agg_hbm.shape, BF16),
        pltpu.VMEM(w_proj_hbm.shape, BF16),
        pltpu.VMEM(w_class_hbm.shape, BF16),
        pltpu.VMEM((GROUPS * PAPERS, 1), jnp.int32),
    )
    def class_rows(m):
        main = w_mix[pl.ds(pl.multiple_of(128 * m, 128), 128), :]
        tail = w_mix[pl.ds(pl.multiple_of(tail_at + TAIL * m, TAIL), TAIL), :]
        return jnp.concatenate([main, tail], axis=0)

    def class_rows_wide(m):
        return jnp.concatenate([class_rows(m), jnp.zeros((256 - CLASS_PAD, width), BF16)], axis=0)

    scale = KEY ** (-0.5)
    side = BLOCK * METAS
    same = lax.rem(iota((side, side), 0), BLOCK) == lax.rem(iota((side, side), 1), BLOCK)
    first = iota((side, 2 * KEY), 1) < KEY
    by_key = where_one(iota((side, side), 0) // BLOCK == iota((side, side), 1) // BLOCK)
    by_query = iota((side, side), 0) // BLOCK == lax.rem(iota((side, side), 1), METAS)

    def mail_to(g, h):
        return remote(
            mail.at[g, part(h), :], mail_in.at[me, part(h), :], mail_send.at[g, h], mail_recv.at[me, h], {"meta": g}
        )

    def mail_from(g, h):
        here = mail_in.at[g, part(h), :]
        return remote(here, here, mail_send.at[g, h], mail_recv.at[g, h], {"meta": g})

    def key_rows(g, h):
        return pl.ds(pl.multiple_of(g * PAPERS + h * HALF, HALF), HALF)

    def keys_to(g, h):
        return remote(
            d_vq.at[pl.ds(2 * g, 2), part(h), pl.ds(width, 2 * KEY)],
            d_vk.at[:, key_rows(me, h), pl.ds(width, 2 * KEY)],
            mail_send.at[g, 2 + h],
            mail_recv.at[me, 2 + h],
            {"meta": g},
        )

    def keys_from(g, h):
        here = d_vk.at[:, key_rows(g, h), pl.ds(width, 2 * KEY)]
        return remote(here, here, mail_send.at[g, 2 + h], mail_recv.at[g, 2 + h], {"meta": g})

    def head(values, attention, kq, h, carry):
        for g in groups:
            for m in range(2):
                in_copy(g, h, m).wait_recv()

        @pl.when(h == 1)
        def _():
            for g in groups:
                mail_to(g, 0).start()
            for g in groups:
                keys_to(g, 0).start()

        def forward(t, c):
            b = h * (HALF // BLOCK) + t
            at = pl.ds(pl.multiple_of(b * BLOCK, BLOCK), BLOCK)
            here = hidden[:, at, :].reshape(side, width)
            mixed = dot(here, w_all[...]).astype(BF16)
            v = mixed[:, :width]
            swapped = mixed[:, width + 2 * KEY :]
            values[b] = v
            kq[b] = swapped
            q = jnp.where(first, mixed[:, width : width + 2 * KEY].astype(F32), 0.0).astype(BF16)
            scores = dot_nt(q, swapped) * scale
            weights = jnp.where(same, jnp.exp(scores), 0.0)
            att = weights * (1.0 / jnp.sum(weights, axis=1, keepdims=True))
            attention[b] = att
            att = att.astype(BF16)
            out = (dot(att, v) + here.astype(F32)).astype(BF16)
            joined[:, at, :] = out.reshape(METAS, BLOCK, width)
            wide = jnp.where(by_query, dot(att, by_key), 0.0)
            attended[at, :] = jnp.sum(wide.reshape(METAS, BLOCK, side), axis=0).astype(BF16)
            return c

        lax.fori_loop(0, HALF // BLOCK, forward, 0, unroll=UNROLL)

        logits = lax.fori_loop(
            0,
            METAS,
            lambda m, t: t + dot_nt(joined[m, part(h), :], class_rows_wide(m)),
            jnp.zeros((HALF, 256), F32),
        )
        class_at = iota((HALF, 256), 1)
        exps = jnp.where(class_at < class_count, jnp.exp(logits), 0.0)
        total = jnp.sum(exps, axis=1, keepdims=True)
        onehot = (labels[part(h), :] == class_at).astype(F32)
        loss_rows = jnp.log(total) - jnp.sum(onehot * logits, axis=1, keepdims=True)
        loss_acc[h] = jnp.zeros((8, 128), F32) + jnp.sum(loss_rows)
        dl = (seed * (exps / total - onehot)).astype(BF16)
        dlogits[part(h), :] = dl

        lane = iota((side, 128), 1)
        for j in range(GROUPS):
            g = lax.rem(me + j, GROUPS)
            choose = where_one(jnp.logical_and(iota((side, 128), 0) == lane + 2 * METAS * g - TAIL, lane >= TAIL) & (lane < TAIL + 2 * METAS))
            second = (dl[:, 128:].astype(F32) + dot(attended[part(h), :], choose)).astype(BF16)
            box = mail_in if j == 0 else mail
            box[g, part(h), :128] = dl[:, :128]
            box[g, part(h), 128:] = second

        @pl.when(h == 1)
        def _():
            for g in groups:
                mail_to(g, 1).start()

        def spread(m, c):
            d_joined[m, part(h), :] = dot(dl[:, :CLASS_PAD], class_rows(m)).astype(BF16)
            return c

        lax.fori_loop(0, METAS, spread, 0)

        def backward(t, c):
            b = h * (HALF // BLOCK) + t
            at = pl.ds(pl.multiple_of(b * BLOCK, BLOCK), BLOCK)
            dj = d_joined[:, at, :].reshape(side, width)
            att = attention[b]
            d_att = dot_nt(dj, values[b])
            mean = jnp.sum(att * d_att, axis=1, keepdims=True)
            d_scores = (att * (d_att - mean) * scale).astype(BF16)
            swapped = kq[b]
            grad = jnp.where(first, dot(d_scores, swapped), dot_tn(d_scores, swapped))
            d_vq[:, at, width:] = grad.astype(BF16).reshape(METAS, BLOCK, 2 * KEY)
            d_val = dot_tn(att.astype(BF16), dj)
            d_vq[:, at, :width] = d_val.astype(BF16).reshape(METAS, BLOCK, width)
            return c

        lax.fori_loop(0, HALF // BLOCK, backward, 0, unroll=UNROLL)

        @pl.when(h == 1)
        def _():
            for g in groups:
                keys_to(g, 1).start()

        for m in range(2):
            d_vk[m, key_rows(me, h), width:] = d_vq[2 * me + m, part(h), width:]
        return carry

    def heads(*held):
        lax.fori_loop(0, 2, functools.partial(head, *held), 0)

    blocks = PAPERS // BLOCK
    pl.run_scoped(
        heads,
        pltpu.VMEM((blocks, side, width), BF16),
        pltpu.VMEM((blocks, side, side), F32),
        pltpu.VMEM((blocks, side, 2 * KEY), BF16),
    )

    def classes(g, carry):
        for m in range(2):
            grad = dot_tn(dlogits[:, :CLASS_PAD], joined[2 * g + m]).astype(BF16)
            for q in range(4):
                lanes = slice(q * 128, (q + 1) * 128)
                for p in range(2):
                    top = p * (CLASS_PAD // 2)
                    cx[p, g, 4 * m + q] = grad[top : top + META_ROWS, lanes]
                    cy[p, 4 * m + q, g] = grad[top + META_ROWS : top + CLASS_PAD // 2, lanes]
        return carry

    lax.fori_loop(0, GROUPS, classes, 0)
    c0 = [to_sibling(0, cx.at[other], cx_in), to_sibling(7, cy.at[other], cy_in)]
    for copy in c0:
        copy.start()

    batch = GROUPS * PAPERS
    part_rows = qv.shape[2]
    for c in range(4):
        cols = slice(c * 128, (c + 1) * 128)
        grad = dot_tn(
            hidden[:, :, cols].reshape(METAS * PAPERS, 128), d_vq[...].reshape(METAS * PAPERS, width + 2 * KEY)
        ).astype(BF16)
        for r in range(128 // part_rows):
            piece = c * (128 // part_rows) + r
            qv[piece // CHIPS, piece % CHIPS] = grad[r * part_rows : (r + 1) * part_rows]
    q0 = to_sibling(1, qv.at[other], qv_in)
    q0.start()

    for copy in c0:
        copy.wait_recv()

    def pair_class(g, carry):
        cx_in[g] = (cx[core, g].astype(F32) + cx_in[g].astype(F32)).astype(BF16)
        cy_in[g] = (cy[core, g].astype(F32) + cy_in[g].astype(F32)).astype(BF16)
        return carry

    lax.fori_loop(0, GROUPS, pair_class, 0)
    for k in chips:
        to_chip(0, k, cy_in.at[k], cy_chip.at[chip]).start()
    for g in groups:
        to_group(1, g, cx_in.at[g], cx_meta.at[me]).start()
    cx_meta[me] = cx_in[me]
    cy_chip[chip] = cy_in[chip]

    q0.wait_recv()

    def pair_qv(k, carry):
        qv_in[k] = (qv[core, k].astype(F32) + qv_in[k].astype(F32)).astype(BF16)
        return carry

    lax.fori_loop(0, CHIPS, pair_qv, 0)
    for k in chips:
        to_chip(2, k, qv_in.at[k], qv_chip.at[chip]).start()
    qv_chip[chip] = qv_in[chip]

    for g in groups:
        for h in range(2):
            mail_from(g, h).wait_recv()
    tail_lane = iota((128, TAIL * METAS), 1)
    tail_row = iota((128, TAIL * METAS), 0)
    repeat = where_one((tail_row < TAIL) & (lax.rem(tail_lane, TAIL) == tail_row))
    widen = [where_one(tail_row == TAIL + METAS * j + tail_lane // TAIL) for j in range(2)]

    def home_values(q, x_even, x_odd):
        def build(j, x):
            for u in range(2):
                s = lax.rem(2 * j + u, GROUPS)
                at = slice(u * PAPERS, (u + 1) * PAPERS)
                main = mail_in[s, :, :128].astype(F32)
                second = mail_in[s, :, 128:]
                second_f = second.astype(F32)
                x[at, tail_at:] = (dot(second, repeat) * dot(second, widen[q])).astype(BF16)
                for i in range(METAS):
                    lane = TAIL + METAS * q + i
                    x[at, 128 * i : 128 * (i + 1)] = (second_f[:, lane : lane + 1] * main).astype(BF16)

        def multiply(j, x):
            at = pl.ds(pl.multiple_of(2 * j * PAPERS, 2 * PAPERS), 2 * PAPERS)
            d_vk[q, at, :width] = dot(x[...], w_mix[...]).astype(BF16)

        build(0, x_even)

        def two(t, carry):
            build(2 * t + 1, x_odd)
            multiply(2 * t, x_even)
            build(2 * t + 2, x_even)
            multiply(2 * t + 1, x_odd)
            return carry

        lax.fori_loop(0, GROUPS // 4, two, 0)

    spread_shape = pltpu.VMEM((2 * PAPERS, METAS * CLASS_PAD), BF16)

    d_hidden = d_joined

    def home_hidden(m):
        def some(r, carry):
            at = pl.ds(pl.multiple_of(r * 2 * PAPERS, 2 * PAPERS), 2 * PAPERS)
            letters = mail_in[pl.ds(2 * r, 2)].reshape(2 * PAPERS, 256)[:, :CLASS_PAD]
            grad = dot(letters, class_rows(2 * me + m)) + dot(d_vk[m, at, :], w_back[...])
            d_hidden[pl.ds(GROUPS * m + 2 * r, 2)] = grad.astype(BF16).reshape(2, PAPERS, width)
            return carry

        lax.fori_loop(0, GROUPS // 2, some, 0)

    part_feat = gp.shape[3]

    def project(m, p):
        back = d_hidden[GROUPS * m : GROUPS * (m + 1)].reshape(batch, width)
        cols = pl.ds(pl.multiple_of(p * CHIPS * part_feat, 128), CHIPS * part_feat)
        grad = dot_tn(gathered[m, :, cols], back).astype(BF16)
        for k in range(CHIPS):
            gp[m, p, k] = grad[k * part_feat : (k + 1) * part_feat]

    def pair_proj(m):
        def one(k, carry):
            gp_in[m, k] = (gp[m, core, k].astype(F32) + gp_in[m, k].astype(F32)).astype(BF16)
            return carry

        lax.fori_loop(0, CHIPS, one, 0)
        for k in chips:
            to_chip(9 + m, k, gp_in.at[m, k], gp_chip.at[m, chip]).start()
        gp_chip[m, chip] = gp_in[m, chip]

    def across(m, k):
        here = gp_all.at[m, core, k]
        return remote(here, here, send_sem.at[13 + m, k], recv_sem.at[13 + m, k], sibling)

    def across_in(m, k):
        here = gp_all.at[m, other, k]
        return remote(here, here, send_sem.at[13 + m, k], recv_sem.at[13 + m, k], sibling)

    def chip_proj(m):
        for k in chips:
            from_chip(9 + m, k, gp_chip.at[m, k]).wait_recv()
        gp_all[m, core, chip] = jnp.sum(gp_chip[m].astype(F32), axis=0).astype(BF16)
        for k in chips:
            to_chip(11 + m, k, gp_all.at[m, core, chip], gp_all.at[m, core, chip]).start()
        across(m, chip).start()

    def pass_on(m):
        for k in chips:
            from_chip(11 + m, k, gp_all.at[m, core, k]).wait_recv()
            across(m, k).start()

    g0 = [to_sibling(2 + 4 * m, gp.at[m, other], gp_in.at[m]) for m in range(2)]

    def first_sum(m):
        project(m, other)
        g0[m].start()
        project(m, core)
        g0[m].wait_recv()
        pair_proj(m)

    pl.run_scoped(functools.partial(home_values, 0), spread_shape, spread_shape)
    for g in groups:
        for h in range(2):
            keys_from(g, h).wait_recv()
    home_hidden(0)
    first_sum(0)
    pl.run_scoped(functools.partial(home_values, 1), spread_shape, spread_shape)

    for k in chips:
        from_chip(0, k, cy_chip.at[k]).wait_recv()

    def chip_sum(g, carry):
        cy_sum[g] = jnp.sum(cy_chip[:, g].astype(F32), axis=0).astype(BF16)
        return carry

    lax.fori_loop(0, GROUPS, chip_sum, 0)
    for g in groups:
        to_group(15, g, cy_sum.at[g], cy_meta.at[me]).start()
    cy_meta[me] = cy_sum[me]

    for k in chips:
        from_chip(2, k, qv_chip.at[k]).wait_recv()
    qv_meta[me] = jnp.sum(qv_chip[...].astype(F32), axis=0).astype(BF16)
    loss_meta[me] = loss_acc[0] + loss_acc[1]
    for g in groups:
        to_group(4, g, qv_meta.at[me], qv_meta.at[me]).start()
        to_group(5, g, loss_meta.at[me], loss_meta.at[me]).start()

    home_hidden(1)
    chip_proj(0)
    first_sum(1)

    for g in groups:
        from_group(1, g, cx_meta.at[g]).wait_recv()

    def meta_sum(k, carry):
        cx_sum[k] = jnp.sum(cx_meta[:, k].astype(F32), axis=0).astype(BF16)
        return carry

    lax.fori_loop(0, CHIPS, meta_sum, 0)
    for k in chips:
        to_chip(3, k, cx_sum.at[k], cx_chip.at[chip]).start()
    cx_chip[chip] = cx_sum[chip]

    for g in groups:
        from_group(4, g, qv_meta.at[g]).wait_recv()
        from_group(5, g, loss_meta.at[g]).wait_recv()
        from_group(15, g, cy_meta.at[g]).wait_recv()
    qv_all[core, chip] = jnp.sum(qv_meta[...].astype(F32), axis=0).astype(BF16)
    loss_node[core, chip] = jnp.sum(loss_meta[...], axis=0)
    cls_all[core, chip, META_ROWS:, :] = jnp.sum(cy_meta[...].astype(F32), axis=0).astype(BF16)
    for k in chips:
        to_chip(7, k, qv_all.at[core, chip], qv_all.at[core, chip]).start()
        to_chip(8, k, loss_node.at[core, chip], loss_node.at[core, chip]).start()

    pass_on(0)

    for k in chips:
        from_chip(3, k, cx_chip.at[k]).wait_recv()
    cls_all[core, chip, :META_ROWS, :] = jnp.sum(cx_chip[...].astype(F32), axis=0).astype(BF16)
    for k in chips:
        to_chip(6, k, cls_all.at[core, chip], cls_all.at[core, chip]).start()

    chip_proj(1)

    for k in chips:
        from_chip(6, k, cls_all.at[core, k]).wait_recv()
        from_chip(7, k, qv_all.at[core, k]).wait_recv()
        from_chip(8, k, loss_node.at[core, k]).wait_recv()
    finals = [
        to_sibling(3, cls_all.at[core], cls_all.at[core]),
        to_sibling(4, qv_all.at[core], qv_all.at[core]),
        to_sibling(5, loss_node.at[core], loss_node.at[core]),
    ]
    for copy in finals:
        copy.start()

    pass_on(1)

    for m in range(2):
        for k in [chip] + chips:
            across_in(m, k).wait_recv()
    remote(cls_all.at[other], cls_all.at[other], sib_send.at[3], sib_recv.at[3], sibling).wait_recv()
    remote(qv_all.at[other], qv_all.at[other], sib_send.at[4], sib_recv.at[4], sibling).wait_recv()
    remote(loss_node.at[other], loss_node.at[other], sib_send.at[5], sib_recv.at[5], sibling).wait_recv()

    q0.wait_send()
    for copy in c0 + g0 + finals:
        copy.wait_send()
    for g in groups:
        for h in range(2):
            for m in range(2):
                out_copy(g, h, m).wait_send()
            mail_to(g, h).wait_send()
            keys_to(g, h).wait_send()
        to_group(1, g, cx_in.at[g], cx_meta.at[me]).wait_send()
        to_group(15, g, cy_sum.at[g], cy_meta.at[me]).wait_send()
        to_group(4, g, qv_meta.at[me], qv_meta.at[me]).wait_send()
        to_group(5, g, loss_meta.at[me], loss_meta.at[me]).wait_send()
    for k in chips:
        to_chip(2, k, qv_in.at[k], qv_chip.at[chip]).wait_send()
        to_chip(0, k, cy_in.at[k], cy_chip.at[chip]).wait_send()
        to_chip(3, k, cx_sum.at[k], cx_chip.at[chip]).wait_send()
        to_chip(6, k, cls_all.at[core, chip], cls_all.at[core, chip]).wait_send()
        to_chip(7, k, qv_all.at[core, chip], qv_all.at[core, chip]).wait_send()
        to_chip(8, k, loss_node.at[core, chip], loss_node.at[core, chip]).wait_send()
    for m in range(2):
        for k in chips:
            to_chip(9 + m, k, gp_in.at[m, k], gp_chip.at[m, chip]).wait_send()
            to_chip(11 + m, k, gp_all.at[m, core, chip], gp_all.at[m, core, chip]).wait_send()
        for k in [chip] + chips:
            across(m, k).wait_send()


def finish_kernel(
    batch_total, class_count,
    gp_hbm, cls_hbm, qv_hbm, loss_hbm, proj_hbm, qk_out, value_out, class_out, loss_out,
    gp, cls, qv, loss, proj, in_sem, out_sem,
):
    part_feat, width = gp.shape[3:]
    part_rows = qv.shape[2]
    half_rows = cls.shape[2]
    loads = [pltpu.make_async_copy(gp_hbm.at[m], gp.at[m], in_sem.at[m]) for m in range(2)]
    for q, (src, dst) in enumerate(((cls_hbm, cls), (qv_hbm, qv), (loss_hbm, loss))):
        loads.append(pltpu.make_async_copy(src, dst, in_sem.at[2 + q]))
    for load in loads:
        load.start()
    stores = []
    for m in range(2):
        loads[m].wait()
        for p in range(2):
            for k in range(CHIPS):
                start = (p * CHIPS + k) * part_feat
                proj[m, start : start + part_feat, :] = gp[m, p, k].astype(F32)
        stores.append(pltpu.make_async_copy(proj.at[m], proj_hbm.at[m], out_sem.at[m]))
        stores[m].start()
    for load in loads[2:]:
        load.wait()
    for p in range(2):
        for k in range(CHIPS):
            start = (p * CHIPS + k) * part_rows
            block = qv[p, k].astype(F32)
            value_out[start : start + part_rows, :] = block[:, :width]
            qk_out[start : start + part_rows, :] = block[:, width:]
            lanes = slice(k * 128, (k + 1) * 128)
            if p == 0:
                class_out[:half_rows, lanes] = cls[0, k].astype(F32)
            else:
                class_out[half_rows:, lanes] = cls[1, k].astype(F32)[: class_count - half_rows]
    loss_out[0, 0] = jnp.sum(loss[...].reshape(2 * CHIPS, 8, 128), axis=0)[0, 0] / batch_total
    for store in stores:
        store.wait()


def local(aggregates, batch_ids, labels, w_proj, w_qk, w_value, w_class):
    batch_total = labels.shape[0] * lax.axis_size("node")
    class_count = w_class.shape[0]
    count, rows, feat = aggregates.shape
    batch = batch_ids.shape[0]
    width = w_value.shape[0]
    side = BLOCK * METAS
    mixed = width + 2 * KEY
    half = CLASS_PAD // 2
    part = feat // (2 * CHIPS)
    part_rows = width // (2 * CHIPS)
    vmem = pl.BlockSpec(memory_space=pltpu.VMEM)
    anywhere = pl.BlockSpec(memory_space=pl.ANY)
    sums = pl.pallas_call(
        functools.partial(step_kernel, 1.0 / batch_total**0.5, class_count),
        out_shape=(
            jax.ShapeDtypeStruct((count, 2, CHIPS, part, width), BF16),
            jax.ShapeDtypeStruct((2, CHIPS, half, 128), BF16),
            jax.ShapeDtypeStruct((2, CHIPS, part_rows, mixed), BF16),
            jax.ShapeDtypeStruct((2, CHIPS, 8, 128), F32),
        ),
        in_specs=[vmem, vmem, anywhere, anywhere, vmem, vmem, anywhere],
        out_specs=(vmem,) * 4,
        scratch_shapes=[
            pltpu.SemaphoreType.DMA((10,)),
            pltpu.VMEM((PAPERS, 1), jnp.int32),
            pltpu.VMEM((count, batch, feat), BF16),
            pltpu.VMEM((count, GROUPS, PAPERS, width), BF16),
            pltpu.VMEM((METAS, PAPERS, width), BF16),
            pltpu.VMEM((width, width + 4 * KEY), BF16),
            pltpu.VMEM((mixed, width), BF16),
            pltpu.VMEM((METAS * CLASS_PAD, width), BF16),
            pltpu.VMEM((METAS, PAPERS, width), BF16),
            pltpu.VMEM((METAS, PAPERS, width), BF16),
            pltpu.VMEM((PAPERS, 256), BF16),
            pltpu.VMEM((PAPERS, side), BF16),
            pltpu.VMEM((GROUPS, PAPERS, 256), BF16),
            pltpu.VMEM((GROUPS, PAPERS, 256), BF16),
            pltpu.VMEM((METAS, PAPERS, mixed), BF16),
            pltpu.VMEM((count, batch, mixed), BF16),
            pltpu.VMEM((2, GROUPS, CHIPS, META_ROWS, 128), BF16),
            pltpu.VMEM((GROUPS, CHIPS, META_ROWS, 128), BF16),
            pltpu.VMEM((GROUPS, CHIPS, META_ROWS, 128), BF16),
            pltpu.VMEM((CHIPS, META_ROWS, 128), BF16),
            pltpu.VMEM((CHIPS, META_ROWS, 128), BF16),
            pltpu.VMEM((2, CHIPS, GROUPS, half - META_ROWS, 128), BF16),
            pltpu.VMEM((CHIPS, GROUPS, half - META_ROWS, 128), BF16),
            pltpu.VMEM((CHIPS, GROUPS, half - META_ROWS, 128), BF16),
            pltpu.VMEM((GROUPS, half - META_ROWS, 128), BF16),
            pltpu.VMEM((GROUPS, half - META_ROWS, 128), BF16),
            pltpu.VMEM((2, CHIPS, part_rows, mixed), BF16),
            pltpu.VMEM((CHIPS, part_rows, mixed), BF16),
            pltpu.VMEM((CHIPS, part_rows, mixed), BF16),
            pltpu.VMEM((GROUPS, part_rows, mixed), BF16),
            pltpu.VMEM((count, 2, CHIPS, part, width), BF16),
            pltpu.VMEM((count, CHIPS, part, width), BF16),
            pltpu.VMEM((count, CHIPS, part, width), BF16),
            pltpu.VMEM((2, 8, 128), F32),
            pltpu.VMEM((GROUPS, 8, 128), F32),
            pltpu.SemaphoreType.DMA((GROUPS, 4)),
            pltpu.SemaphoreType.DMA((GROUPS, 4)),
            pltpu.SemaphoreType.DMA((GROUPS, 4)),
            pltpu.SemaphoreType.DMA((GROUPS, 4)),
            pltpu.SemaphoreType.DMA((16, 8)),
            pltpu.SemaphoreType.DMA((16, 8)),
            pltpu.SemaphoreType.DMA((8,)),
            pltpu.SemaphoreType.DMA((8,)),
        ],
        compiler_params=pltpu.CompilerParams(
            collective_id=1, has_side_effects=True, vmem_limit_bytes=62 * 1024 * 1024
        ),
    )(
        batch_ids.reshape(batch // 128, 128), labels.reshape(batch // 128, 128), aggregates, w_proj, w_qk, w_value, w_class
    )
    grad_proj, grad_qk, grad_value, grad_class, loss = pl.pallas_call(
        functools.partial(finish_kernel, batch_total, class_count),
        out_shape=(
            jax.ShapeDtypeStruct((count, feat, width), F32),
            jax.ShapeDtypeStruct((width, 2 * KEY), F32),
            jax.ShapeDtypeStruct((width, width), F32),
            jax.ShapeDtypeStruct((class_count, count * width), F32),
            jax.ShapeDtypeStruct((1, 1), F32),
        ),
        in_specs=[anywhere] * 4,
        out_specs=(anywhere,) + (vmem,) * 3 + (pl.BlockSpec(memory_space=pltpu.SMEM),),
        scratch_shapes=[
            pltpu.VMEM((count, 2, CHIPS, part, width), BF16),
            pltpu.VMEM((2, CHIPS, half, 128), BF16),
            pltpu.VMEM((2, CHIPS, part_rows, mixed), BF16),
            pltpu.VMEM((2, CHIPS, 8, 128), F32),
            pltpu.VMEM((count, feat, width), F32),
            pltpu.SemaphoreType.DMA((5,)),
            pltpu.SemaphoreType.DMA((2,)),
        ],
        compiler_params=pltpu.CompilerParams(vmem_limit_bytes=62 * 1024 * 1024),
    )(*sums)
    return (grad_proj, grad_qk, grad_value, grad_class, loss.reshape(()))


def solution(mesh):
    in_specs = (P("meta", "node", None), P("node"), P("node"), P("meta", None, None), P(), P(), P())
    out_specs = (P("meta", None, None), P(), P(), P(None, "meta"), P())
    return jax.shard_map(local, mesh=mesh, in_specs=in_specs, out_specs=out_specs, check_vma=False)
```

```python
import functools

import jax
import jax.numpy as jnp
from jax import lax
from jax.experimental import pallas as pl
from jax.experimental.pallas import tpu as pltpu
from jax.sharding import PartitionSpec as P

MESH = pl.DeviceIdType.MESH
F32 = jnp.float32
BF16 = jnp.bfloat16
GROUPS = 8
CHIPS = 8
PAPERS = 192
HALF = 96
BLOCK = 16
METAS = 16
KEY = 64
CLASS_PAD = 160
TAIL = CLASS_PAD - 128
META_ROWS = 48
UNROLL = 6


def dot(a, b):
    return jnp.dot(a, b, preferred_element_type=F32)


def dot_nt(a, b):
    return lax.dot_general(a, b, (((1,), (1,)), ((), ())), preferred_element_type=F32)


def dot_tn(a, b):
    return lax.dot_general(a, b, (((0,), (0,)), ((), ())), preferred_element_type=F32)


def iota(shape, axis):
    return lax.broadcasted_iota(jnp.int32, shape, axis)


def where_one(mask):
    return mask.astype(F32).astype(BF16)


def remote(src, dst, send_sem, recv_sem, where):
    return pltpu.make_async_remote_copy(
        src_ref=src, dst_ref=dst, send_sem=send_sem, recv_sem=recv_sem, device_id=where, device_id_type=MESH
    )


def step_kernel(
    seed, class_count,
    ids_ref, labels_ref, agg_hbm, w_proj_hbm, w_qk, w_value, w_class_hbm,
    gp_all, cls_all, qv_all, loss_node,
    load_sem, labels, gathered, outbox, hidden, w_all, w_back, w_mix,
    joined, d_joined, dlogits, attended, mail, mail_in, d_vq, d_vk,
    cx, cx_in, cx_meta, cx_sum, cx_chip, cy, cy_in, cy_chip, cy_sum, cy_meta,
    qv, qv_in, qv_chip, qv_meta,
    gp, gp_in, gp_chip, loss_acc, loss_meta,
    out_sem, in_sem, mail_send, mail_recv, send_sem, recv_sem, sib_send, sib_recv,
):
    me = lax.axis_index("meta")
    node = lax.axis_index("node")
    chip, core = node // 2, lax.rem(node, 2)
    other = 1 - core
    sibling = {"node": 2 * chip + other}
    groups = [lax.rem(me + j, GROUPS) for j in range(1, GROUPS)]
    chips = [lax.rem(chip + j, CHIPS) for j in range(1, CHIPS)]
    width = w_value.shape[0]
    rows, feat = agg_hbm.shape[1:]
    tail_at = 128 * METAS

    barrier = pltpu.get_barrier_semaphore()
    for g in groups:
        pl.semaphore_signal(barrier, inc=1, device_id={"meta": g}, device_id_type=MESH)
    for k in chips:
        pl.semaphore_signal(barrier, inc=1, device_id={"node": 2 * k + core}, device_id_type=MESH)
    pl.semaphore_signal(barrier, inc=1, device_id=sibling, device_id_type=MESH)

    def to_group(phase, g, src, dst):
        return remote(src, dst, send_sem.at[phase, g], recv_sem.at[phase, me], {"meta": g})

    def from_group(phase, g, dst):
        return remote(dst, dst, send_sem.at[phase, g], recv_sem.at[phase, g], {"meta": g})

    def to_chip(phase, k, src, dst):
        return remote(src, dst, send_sem.at[phase, k], recv_sem.at[phase, chip], {"node": 2 * k + core})

    def from_chip(phase, k, dst):
        return remote(dst, dst, send_sem.at[phase, k], recv_sem.at[phase, k], {"node": 2 * k + core})

    def to_sibling(phase, src, dst):
        return remote(src, dst, sib_send.at[phase], sib_recv.at[phase], sibling)

    def to_column(src, dst):
        eye = iota((128, 128), 0) == iota((128, 128), 1)
        for t in range(src.shape[0]):
            row = jnp.broadcast_to(src[t : t + 1, :].astype(F32), (128, 128))
            dst[t * 128 : (t + 1) * 128, :] = jnp.sum(jnp.where(eye, row, 0.0), axis=1, keepdims=True).astype(jnp.int32)

    def part(h):
        return pl.ds(pl.multiple_of(h * HALF, HALF), HALF)

    def out_copy(g, h, m):
        return remote(
            outbox.at[m, g, part(h), :],
            hidden.at[2 * me + m, part(h), :],
            out_sem.at[g, 2 * h + m],
            in_sem.at[me, 2 * h + m],
            {"meta": g},
        )

    def in_copy(g, h, m):
        here = hidden.at[2 * g + m, part(h), :]
        return remote(here, here, out_sem.at[g, 2 * h + m], in_sem.at[g, 2 * h + m], {"meta": g})

    def front(agg, w_proj, w_class, ids):
        loads = []
        step = rows // 4
        for m in range(2):
            for q in range(4):
                at = pl.ds(q * step, step)
                loads.append(pltpu.make_async_copy(agg_hbm.at[m, at, :], agg.at[m, at, :], load_sem.at[4 * m + q]))
        loads.append(pltpu.make_async_copy(w_proj_hbm, w_proj, load_sem.at[8]))
        loads.append(pltpu.make_async_copy(w_class_hbm, w_class, load_sem.at[9]))
        for load in loads:
            load.start()
        to_column(ids_ref, ids)
        for load in loads[:9]:
            load.wait()
        pl.semaphore_wait(barrier, GROUPS - 1 + CHIPS)

        def project_pair(p, h, with_own):
            first = lax.rem(me // 2 + p + 1, 4) * 2 + lax.rem(me + p, 2)
            second = lax.rem(me // 2 + 3 - p, 4) * 2 + lax.rem(me + p + 1, 2)
            if with_own:
                second = me
            spots = [pl.ds(pl.multiple_of(g * PAPERS + h * HALF, HALF), HALF) for g in (first, second)]
            column = jnp.concatenate([ids[spot, :] for spot in spots], axis=0)
            picks = where_one(column == iota((2 * HALF, rows), 1))
            for m in range(2):
                got = dot(picks, agg[m]).astype(BF16)
                row = dot(got, w_proj[m]).astype(BF16)
                for q, g in enumerate((first, second)):
                    gathered[m, spots[q], :] = got[q * HALF : (q + 1) * HALF]
                    mine = row[q * HALF : (q + 1) * HALF]
                    outbox[m, g, part(h), :] = mine
                    if with_own and q == 1:
                        hidden[2 * me + m, part(h), :] = mine
                    else:
                        out_copy(g, h, m).start()

        def project_half(h, carry):
            def one(p, c):
                project_pair(p, h, False)
                return c

            lax.fori_loop(0, 3, one, 0)
            project_pair(3, h, True)
            return carry

        lax.fori_loop(0, 2, project_half, 0)

        to_column(labels_ref, ids)
        labels[...] = ids[pl.ds(pl.multiple_of(me * PAPERS, PAPERS), PAPERS), :]

        swap = where_one(lax.rem(iota((2 * KEY, 2 * KEY), 0) + KEY, 2 * KEY) == iota((2 * KEY, 2 * KEY), 1))
        w_all[:, :width] = w_value[...]
        w_all[:, width : width + 2 * KEY] = w_qk[...]
        w_all[:, width + 2 * KEY :] = dot(w_qk[...], swap).astype(BF16)
        w_back[:width, :] = w_value[...].astype(F32).T.astype(BF16)
        w_back[width:, :] = w_qk[...].astype(F32).T.astype(BF16)
        loads[9].wait()
        for m in range(METAS):
            lanes = slice(m * width, (m + 1) * width)
            w_mix[128 * m : 128 * (m + 1), :] = w_class[:128, lanes]
            last = w_class[128:class_count, lanes].astype(F32)
            zeros = jnp.zeros((CLASS_PAD - class_count, width), F32)
            w_mix[tail_at + TAIL * m : tail_at + TAIL * (m + 1), :] = jnp.concatenate([last, zeros], axis=0).astype(BF16)

    pl.run_scoped(
        front,
        pltpu.VMEM(agg_hbm.shape, BF16),
        pltpu.VMEM(w_proj_hbm.shape, BF16),
        pltpu.VMEM(w_class_hbm.shape, BF16),
        pltpu.VMEM((GROUPS * PAPERS, 1), jnp.int32),
    )
    def class_rows(m):
        main = w_mix[pl.ds(pl.multiple_of(128 * m, 128), 128), :]
        tail = w_mix[pl.ds(pl.multiple_of(tail_at + TAIL * m, TAIL), TAIL), :]
        return jnp.concatenate([main, tail], axis=0)

    def class_rows_wide(m):
        return jnp.concatenate([class_rows(m), jnp.zeros((256 - CLASS_PAD, width), BF16)], axis=0)

    scale = KEY ** (-0.5)
    side = BLOCK * METAS
    same = lax.rem(iota((side, side), 0), BLOCK) == lax.rem(iota((side, side), 1), BLOCK)
    first = iota((side, 2 * KEY), 1) < KEY
    by_key = where_one(iota((side, side), 0) // BLOCK == iota((side, side), 1) // BLOCK)
    by_query = iota((side, side), 0) // BLOCK == lax.rem(iota((side, side), 1), METAS)

    def mail_to(g, h):
        return remote(
            mail.at[g, part(h), :], mail_in.at[me, part(h), :], mail_send.at[g, h], mail_recv.at[me, h], {"meta": g}
        )

    def mail_from(g, h):
        here = mail_in.at[g, part(h), :]
        return remote(here, here, mail_send.at[g, h], mail_recv.at[g, h], {"meta": g})

    def key_rows(g, h):
        return pl.ds(pl.multiple_of(g * PAPERS + h * HALF, HALF), HALF)

    def keys_to(g, h):
        return remote(
            d_vq.at[pl.ds(2 * g, 2), part(h), pl.ds(width, 2 * KEY)],
            d_vk.at[:, key_rows(me, h), pl.ds(width, 2 * KEY)],
            mail_send.at[g, 2 + h],
            mail_recv.at[me, 2 + h],
            {"meta": g},
        )

    def keys_from(g, h):
        here = d_vk.at[:, key_rows(g, h), pl.ds(width, 2 * KEY)]
        return remote(here, here, mail_send.at[g, 2 + h], mail_recv.at[g, 2 + h], {"meta": g})

    def head(values, attention, qk, kq, h, carry):
        for g in groups:
            for m in range(2):
                in_copy(g, h, m).wait_recv()

        @pl.when(h == 1)
        def _():
            for g in groups:
                mail_to(g, 0).start()
            for g in groups:
                keys_to(g, 0).start()

        def mix(t, c):
            metas = pl.ds(4 * t, 4)
            mixed = dot(hidden[metas, part(h), :].reshape(4 * HALF, width), w_all[...]).astype(BF16)
            mixed = mixed.reshape(4, HALF, width + 4 * KEY)
            values[metas, part(h), :] = mixed[:, :, :width]
            qk[metas, part(h), :] = mixed[:, :, width : width + 2 * KEY]
            kq[metas, part(h), :] = mixed[:, :, width + 2 * KEY :]
            return c

        lax.fori_loop(0, METAS // 4, mix, 0, unroll=2)

        def forward(t, c):
            b = h * (HALF // BLOCK) + t
            at = pl.ds(pl.multiple_of(b * BLOCK, BLOCK), BLOCK)
            here = hidden[:, at, :].reshape(side, width)
            v = values[:, at, :].reshape(side, width)
            q = jnp.where(first, qk[:, at, :].reshape(side, 2 * KEY).astype(F32), 0.0).astype(BF16)
            scores = dot_nt(q, kq[:, at, :].reshape(side, 2 * KEY)) * scale
            weights = jnp.where(same, jnp.exp(scores), 0.0)
            att = weights * (1.0 / jnp.sum(weights, axis=1, keepdims=True))
            attention[b] = att
            att = att.astype(BF16)
            out = (dot(att, v) + here.astype(F32)).astype(BF16)
            joined[:, at, :] = out.reshape(METAS, BLOCK, width)
            wide = jnp.where(by_query, dot(att, by_key), 0.0)
            attended[at, :] = jnp.sum(wide.reshape(METAS, BLOCK, side), axis=0).astype(BF16)
            return c

        lax.fori_loop(0, HALF // BLOCK, forward, 0, unroll=UNROLL)

        logits = lax.fori_loop(
            0,
            METAS,
            lambda m, t: t + dot_nt(joined[m, part(h), :], class_rows_wide(m)),
            jnp.zeros((HALF, 256), F32),
            unroll=8,
        )
        class_at = iota((HALF, 256), 1)
        exps = jnp.where(class_at < class_count, jnp.exp(logits), 0.0)
        total = jnp.sum(exps, axis=1, keepdims=True)
        onehot = (labels[part(h), :] == class_at).astype(F32)
        loss_rows = jnp.log(total) - jnp.sum(onehot * logits, axis=1, keepdims=True)
        loss_acc[h] = jnp.zeros((8, 128), F32) + jnp.sum(loss_rows)
        dl = (seed * (exps / total - onehot)).astype(BF16)
        dlogits[part(h), :] = dl

        lane = iota((side, 128), 1)
        for j in range(GROUPS):
            g = lax.rem(me + j, GROUPS)
            choose = where_one(jnp.logical_and(iota((side, 128), 0) == lane + 2 * METAS * g - TAIL, lane >= TAIL) & (lane < TAIL + 2 * METAS))
            second = (dl[:, 128:].astype(F32) + dot(attended[part(h), :], choose)).astype(BF16)
            box = mail_in if j == 0 else mail
            box[g, part(h), :128] = dl[:, :128]
            box[g, part(h), 128:] = second

        @pl.when(h == 1)
        def _():
            for g in groups:
                mail_to(g, 1).start()

        def spread(m, c):
            d_joined[m, part(h), :] = dot(dl[:, :CLASS_PAD], class_rows(m)).astype(BF16)
            return c

        lax.fori_loop(0, METAS, spread, 0, unroll=8)

        def backward(t, c):
            b = h * (HALF // BLOCK) + t
            at = pl.ds(pl.multiple_of(b * BLOCK, BLOCK), BLOCK)
            dj = d_joined[:, at, :].reshape(side, width)
            att = attention[b]
            d_att = dot_nt(dj, values[:, at, :].reshape(side, width))
            mean = jnp.sum(att * d_att, axis=1, keepdims=True)
            d_scores = (att * (d_att - mean) * scale).astype(BF16)
            swapped = kq[:, at, :].reshape(side, 2 * KEY)
            grad = jnp.where(first, dot(d_scores, swapped), dot_tn(d_scores, swapped))
            d_vq[:, at, width:] = grad.astype(BF16).reshape(METAS, BLOCK, 2 * KEY)
            d_val = dot_tn(att.astype(BF16), dj)
            d_vq[:, at, :width] = d_val.astype(BF16).reshape(METAS, BLOCK, width)
            return c

        lax.fori_loop(0, HALF // BLOCK, backward, 0, unroll=UNROLL)

        @pl.when(h == 1)
        def _():
            for g in groups:
                keys_to(g, 1).start()

        for m in range(2):
            d_vk[m, key_rows(me, h), width:] = d_vq[2 * me + m, part(h), width:]
        return carry

    def heads(*held):
        lax.fori_loop(0, 2, functools.partial(head, *held), 0)

    blocks = PAPERS // BLOCK
    pl.run_scoped(
        heads,
        pltpu.VMEM((METAS, PAPERS, width), BF16),
        pltpu.VMEM((blocks, side, side), F32),
        pltpu.VMEM((METAS, PAPERS, 2 * KEY), BF16),
        pltpu.VMEM((METAS, PAPERS, 2 * KEY), BF16),
    )

    def classes(g, carry):
        for m in range(2):
            grad = dot_tn(dlogits[:, :CLASS_PAD], joined[2 * g + m]).astype(BF16)
            for q in range(4):
                lanes = slice(q * 128, (q + 1) * 128)
                for p in range(2):
                    top = p * (CLASS_PAD // 2)
                    cx[p, g, 4 * m + q] = grad[top : top + META_ROWS, lanes]
                    cy[p, 4 * m + q, g] = grad[top + META_ROWS : top + CLASS_PAD // 2, lanes]
        return carry

    lax.fori_loop(0, GROUPS, classes, 0, unroll=4)
    c0 = [to_sibling(0, cx.at[other], cx_in), to_sibling(7, cy.at[other], cy_in)]
    for copy in c0:
        copy.start()

    batch = GROUPS * PAPERS
    part_rows = qv.shape[2]
    for c in range(4):
        cols = slice(c * 128, (c + 1) * 128)
        grad = dot_tn(
            hidden[:, :, cols].reshape(METAS * PAPERS, 128), d_vq[...].reshape(METAS * PAPERS, width + 2 * KEY)
        ).astype(BF16)
        for r in range(128 // part_rows):
            piece = c * (128 // part_rows) + r
            qv[piece // CHIPS, piece % CHIPS] = grad[r * part_rows : (r + 1) * part_rows]
    q0 = to_sibling(1, qv.at[other], qv_in)
    q0.start()

    for copy in c0:
        copy.wait_recv()

    def pair_class(g, carry):
        cx_in[g] = (cx[core, g].astype(F32) + cx_in[g].astype(F32)).astype(BF16)
        cy_in[g] = (cy[core, g].astype(F32) + cy_in[g].astype(F32)).astype(BF16)
        return carry

    lax.fori_loop(0, GROUPS, pair_class, 0, unroll=4)
    for k in chips:
        to_chip(0, k, cy_in.at[k], cy_chip.at[chip]).start()
    for g in groups:
        to_group(1, g, cx_in.at[g], cx_meta.at[me]).start()
    cx_meta[me] = cx_in[me]
    cy_chip[chip] = cy_in[chip]

    q0.wait_recv()

    def pair_qv(k, carry):
        qv_in[k] = (qv[core, k].astype(F32) + qv_in[k].astype(F32)).astype(BF16)
        return carry

    lax.fori_loop(0, CHIPS, pair_qv, 0, unroll=4)
    for k in chips:
        to_chip(2, k, qv_in.at[k], qv_chip.at[chip]).start()
    qv_chip[chip] = qv_in[chip]

    for g in groups:
        for h in range(2):
            mail_from(g, h).wait_recv()
    tail_lane = iota((128, TAIL * METAS), 1)
    tail_row = iota((128, TAIL * METAS), 0)
    repeat = where_one((tail_row < TAIL) & (lax.rem(tail_lane, TAIL) == tail_row))
    widen = [where_one(tail_row == TAIL + METAS * j + tail_lane // TAIL) for j in range(2)]

    def home_values(q, x_even, x_odd):
        def build(j, x):
            for u in range(2):
                s = lax.rem(2 * j + u, GROUPS)
                at = slice(u * PAPERS, (u + 1) * PAPERS)
                main = mail_in[s, :, :128].astype(F32)
                second = mail_in[s, :, 128:]
                second_f = second.astype(F32)
                x[at, tail_at:] = (dot(second, repeat) * dot(second, widen[q])).astype(BF16)
                for i in range(METAS):
                    lane = TAIL + METAS * q + i
                    x[at, 128 * i : 128 * (i + 1)] = (second_f[:, lane : lane + 1] * main).astype(BF16)

        def multiply(j, x):
            at = pl.ds(pl.multiple_of(2 * j * PAPERS, 2 * PAPERS), 2 * PAPERS)
            d_vk[q, at, :width] = dot(x[...], w_mix[...]).astype(BF16)

        build(0, x_even)

        def two(t, carry):
            build(2 * t + 1, x_odd)
            multiply(2 * t, x_even)
            build(2 * t + 2, x_even)
            multiply(2 * t + 1, x_odd)
            return carry

        lax.fori_loop(0, GROUPS // 4, two, 0)

    spread_shape = pltpu.VMEM((2 * PAPERS, METAS * CLASS_PAD), BF16)

    d_hidden = d_joined

    def home_hidden(m):
        def some(r, carry):
            at = pl.ds(pl.multiple_of(r * 2 * PAPERS, 2 * PAPERS), 2 * PAPERS)
            letters = mail_in[pl.ds(2 * r, 2)].reshape(2 * PAPERS, 256)[:, :CLASS_PAD]
            grad = dot(letters, class_rows(2 * me + m)) + dot(d_vk[m, at, :], w_back[...])
            d_hidden[pl.ds(GROUPS * m + 2 * r, 2)] = grad.astype(BF16).reshape(2, PAPERS, width)
            return carry

        lax.fori_loop(0, GROUPS // 2, some, 0, unroll=4)

    part_feat = gp.shape[3]

    def project(m, p):
        back = d_hidden[GROUPS * m : GROUPS * (m + 1)].reshape(batch, width)
        cols = pl.ds(pl.multiple_of(p * CHIPS * part_feat, 128), CHIPS * part_feat)
        grad = dot_tn(gathered[m, :, cols], back).astype(BF16)
        for k in range(CHIPS):
            gp[m, p, k] = grad[k * part_feat : (k + 1) * part_feat]

    def pair_proj(m):
        def one(k, carry):
            gp_in[m, k] = (gp[m, core, k].astype(F32) + gp_in[m, k].astype(F32)).astype(BF16)
            return carry

        lax.fori_loop(0, CHIPS, one, 0, unroll=4)
        for k in chips:
            to_chip(9 + m, k, gp_in.at[m, k], gp_chip.at[m, chip]).start()
        gp_chip[m, chip] = gp_in[m, chip]

    def across(m, k):
        here = gp_all.at[m, core, k]
        return remote(here, here, send_sem.at[13 + m, k], recv_sem.at[13 + m, k], sibling)

    def across_in(m, k):
        here = gp_all.at[m, other, k]
        return remote(here, here, send_sem.at[13 + m, k], recv_sem.at[13 + m, k], sibling)

    def chip_proj(m):
        for k in chips:
            from_chip(9 + m, k, gp_chip.at[m, k]).wait_recv()
        gp_all[m, core, chip] = jnp.sum(gp_chip[m].astype(F32), axis=0).astype(BF16)
        for k in chips:
            to_chip(11 + m, k, gp_all.at[m, core, chip], gp_all.at[m, core, chip]).start()
        across(m, chip).start()

    def pass_on(m):
        for k in chips:
            from_chip(11 + m, k, gp_all.at[m, core, k]).wait_recv()
            across(m, k).start()

    g0 = [to_sibling(2 + 4 * m, gp.at[m, other], gp_in.at[m]) for m in range(2)]

    def first_sum(m):
        project(m, other)
        g0[m].start()
        project(m, core)
        g0[m].wait_recv()
        pair_proj(m)

    pl.run_scoped(functools.partial(home_values, 0), spread_shape, spread_shape)
    for g in groups:
        for h in range(2):
            keys_from(g, h).wait_recv()
    home_hidden(0)
    first_sum(0)
    pl.run_scoped(functools.partial(home_values, 1), spread_shape, spread_shape)

    for k in chips:
        from_chip(0, k, cy_chip.at[k]).wait_recv()

    def chip_sum(g, carry):
        cy_sum[g] = jnp.sum(cy_chip[:, g].astype(F32), axis=0).astype(BF16)
        return carry

    lax.fori_loop(0, GROUPS, chip_sum, 0, unroll=4)
    for g in groups:
        to_group(15, g, cy_sum.at[g], cy_meta.at[me]).start()
    cy_meta[me] = cy_sum[me]

    for k in chips:
        from_chip(2, k, qv_chip.at[k]).wait_recv()
    qv_meta[me] = jnp.sum(qv_chip[...].astype(F32), axis=0).astype(BF16)
    loss_meta[me] = loss_acc[0] + loss_acc[1]
    for g in groups:
        to_group(4, g, qv_meta.at[me], qv_meta.at[me]).start()
        to_group(5, g, loss_meta.at[me], loss_meta.at[me]).start()

    home_hidden(1)
    chip_proj(0)
    first_sum(1)

    for g in groups:
        from_group(1, g, cx_meta.at[g]).wait_recv()

    def meta_sum(k, carry):
        cx_sum[k] = jnp.sum(cx_meta[:, k].astype(F32), axis=0).astype(BF16)
        return carry

    lax.fori_loop(0, CHIPS, meta_sum, 0, unroll=4)
    for k in chips:
        to_chip(3, k, cx_sum.at[k], cx_chip.at[chip]).start()
    cx_chip[chip] = cx_sum[chip]

    for g in groups:
        from_group(4, g, qv_meta.at[g]).wait_recv()
        from_group(5, g, loss_meta.at[g]).wait_recv()
        from_group(15, g, cy_meta.at[g]).wait_recv()
    qv_all[core, chip] = jnp.sum(qv_meta[...].astype(F32), axis=0).astype(BF16)
    loss_node[core, chip] = jnp.sum(loss_meta[...], axis=0)
    cls_all[core, chip, META_ROWS:, :] = jnp.sum(cy_meta[...].astype(F32), axis=0).astype(BF16)
    for k in chips:
        to_chip(7, k, qv_all.at[core, chip], qv_all.at[core, chip]).start()
        to_chip(8, k, loss_node.at[core, chip], loss_node.at[core, chip]).start()

    pass_on(0)

    for k in chips:
        from_chip(3, k, cx_chip.at[k]).wait_recv()
    cls_all[core, chip, :META_ROWS, :] = jnp.sum(cx_chip[...].astype(F32), axis=0).astype(BF16)
    for k in chips:
        to_chip(6, k, cls_all.at[core, chip], cls_all.at[core, chip]).start()

    chip_proj(1)

    for k in chips:
        from_chip(6, k, cls_all.at[core, k]).wait_recv()
        from_chip(7, k, qv_all.at[core, k]).wait_recv()
        from_chip(8, k, loss_node.at[core, k]).wait_recv()
    finals = [
        to_sibling(3, cls_all.at[core], cls_all.at[core]),
        to_sibling(4, qv_all.at[core], qv_all.at[core]),
        to_sibling(5, loss_node.at[core], loss_node.at[core]),
    ]
    for copy in finals:
        copy.start()

    pass_on(1)

    for m in range(2):
        for k in [chip] + chips:
            across_in(m, k).wait_recv()
    remote(cls_all.at[other], cls_all.at[other], sib_send.at[3], sib_recv.at[3], sibling).wait_recv()
    remote(qv_all.at[other], qv_all.at[other], sib_send.at[4], sib_recv.at[4], sibling).wait_recv()
    remote(loss_node.at[other], loss_node.at[other], sib_send.at[5], sib_recv.at[5], sibling).wait_recv()

    q0.wait_send()
    for copy in c0 + g0 + finals:
        copy.wait_send()
    for g in groups:
        for h in range(2):
            for m in range(2):
                out_copy(g, h, m).wait_send()
            mail_to(g, h).wait_send()
            keys_to(g, h).wait_send()
        to_group(1, g, cx_in.at[g], cx_meta.at[me]).wait_send()
        to_group(15, g, cy_sum.at[g], cy_meta.at[me]).wait_send()
        to_group(4, g, qv_meta.at[me], qv_meta.at[me]).wait_send()
        to_group(5, g, loss_meta.at[me], loss_meta.at[me]).wait_send()
    for k in chips:
        to_chip(2, k, qv_in.at[k], qv_chip.at[chip]).wait_send()
        to_chip(0, k, cy_in.at[k], cy_chip.at[chip]).wait_send()
        to_chip(3, k, cx_sum.at[k], cx_chip.at[chip]).wait_send()
        to_chip(6, k, cls_all.at[core, chip], cls_all.at[core, chip]).wait_send()
        to_chip(7, k, qv_all.at[core, chip], qv_all.at[core, chip]).wait_send()
        to_chip(8, k, loss_node.at[core, chip], loss_node.at[core, chip]).wait_send()
    for m in range(2):
        for k in chips:
            to_chip(9 + m, k, gp_in.at[m, k], gp_chip.at[m, chip]).wait_send()
            to_chip(11 + m, k, gp_all.at[m, core, chip], gp_all.at[m, core, chip]).wait_send()
        for k in [chip] + chips:
            across(m, k).wait_send()


def finish_kernel(
    batch_total, class_count,
    gp_hbm, cls_hbm, qv_hbm, loss_hbm, proj_hbm, qk_out, value_out, class_out, loss_out,
    gp, cls, qv, loss, proj, in_sem, out_sem,
):
    part_feat, width = gp.shape[3:]
    part_rows = qv.shape[2]
    half_rows = cls.shape[2]
    loads = [pltpu.make_async_copy(gp_hbm.at[m], gp.at[m], in_sem.at[m]) for m in range(2)]
    for q, (src, dst) in enumerate(((cls_hbm, cls), (qv_hbm, qv), (loss_hbm, loss))):
        loads.append(pltpu.make_async_copy(src, dst, in_sem.at[2 + q]))
    for load in loads:
        load.start()
    stores = []
    for m in range(2):
        loads[m].wait()
        for p in range(2):
            for k in range(CHIPS):
                start = (p * CHIPS + k) * part_feat
                proj[m, start : start + part_feat, :] = gp[m, p, k].astype(F32)
        stores.append(pltpu.make_async_copy(proj.at[m], proj_hbm.at[m], out_sem.at[m]))
        stores[m].start()
    for load in loads[2:]:
        load.wait()
    for p in range(2):
        for k in range(CHIPS):
            start = (p * CHIPS + k) * part_rows
            block = qv[p, k].astype(F32)
            value_out[start : start + part_rows, :] = block[:, :width]
            qk_out[start : start + part_rows, :] = block[:, width:]
            lanes = slice(k * 128, (k + 1) * 128)
            if p == 0:
                class_out[:half_rows, lanes] = cls[0, k].astype(F32)
            else:
                class_out[half_rows:, lanes] = cls[1, k].astype(F32)[: class_count - half_rows]
    loss_out[0, 0] = jnp.sum(loss[...].reshape(2 * CHIPS, 8, 128), axis=0)[0, 0] / batch_total
    for store in stores:
        store.wait()


def local(aggregates, batch_ids, labels, w_proj, w_qk, w_value, w_class):
    batch_total = labels.shape[0] * lax.axis_size("node")
    class_count = w_class.shape[0]
    count, rows, feat = aggregates.shape
    batch = batch_ids.shape[0]
    width = w_value.shape[0]
    side = BLOCK * METAS
    mixed = width + 2 * KEY
    half = CLASS_PAD // 2
    part = feat // (2 * CHIPS)
    part_rows = width // (2 * CHIPS)
    vmem = pl.BlockSpec(memory_space=pltpu.VMEM)
    anywhere = pl.BlockSpec(memory_space=pl.ANY)
    sums = pl.pallas_call(
        functools.partial(step_kernel, 1.0 / batch_total**0.5, class_count),
        out_shape=(
            jax.ShapeDtypeStruct((count, 2, CHIPS, part, width), BF16),
            jax.ShapeDtypeStruct((2, CHIPS, half, 128), BF16),
            jax.ShapeDtypeStruct((2, CHIPS, part_rows, mixed), BF16),
            jax.ShapeDtypeStruct((2, CHIPS, 8, 128), F32),
        ),
        in_specs=[vmem, vmem, anywhere, anywhere, vmem, vmem, anywhere],
        out_specs=(vmem,) * 4,
        scratch_shapes=[
            pltpu.SemaphoreType.DMA((10,)),
            pltpu.VMEM((PAPERS, 1), jnp.int32),
            pltpu.VMEM((count, batch, feat), BF16),
            pltpu.VMEM((count, GROUPS, PAPERS, width), BF16),
            pltpu.VMEM((METAS, PAPERS, width), BF16),
            pltpu.VMEM((width, width + 4 * KEY), BF16),
            pltpu.VMEM((mixed, width), BF16),
            pltpu.VMEM((METAS * CLASS_PAD, width), BF16),
            pltpu.VMEM((METAS, PAPERS, width), BF16),
            pltpu.VMEM((METAS, PAPERS, width), BF16),
            pltpu.VMEM((PAPERS, 256), BF16),
            pltpu.VMEM((PAPERS, side), BF16),
            pltpu.VMEM((GROUPS, PAPERS, 256), BF16),
            pltpu.VMEM((GROUPS, PAPERS, 256), BF16),
            pltpu.VMEM((METAS, PAPERS, mixed), BF16),
            pltpu.VMEM((count, batch, mixed), BF16),
            pltpu.VMEM((2, GROUPS, CHIPS, META_ROWS, 128), BF16),
            pltpu.VMEM((GROUPS, CHIPS, META_ROWS, 128), BF16),
            pltpu.VMEM((GROUPS, CHIPS, META_ROWS, 128), BF16),
            pltpu.VMEM((CHIPS, META_ROWS, 128), BF16),
            pltpu.VMEM((CHIPS, META_ROWS, 128), BF16),
            pltpu.VMEM((2, CHIPS, GROUPS, half - META_ROWS, 128), BF16),
            pltpu.VMEM((CHIPS, GROUPS, half - META_ROWS, 128), BF16),
            pltpu.VMEM((CHIPS, GROUPS, half - META_ROWS, 128), BF16),
            pltpu.VMEM((GROUPS, half - META_ROWS, 128), BF16),
            pltpu.VMEM((GROUPS, half - META_ROWS, 128), BF16),
            pltpu.VMEM((2, CHIPS, part_rows, mixed), BF16),
            pltpu.VMEM((CHIPS, part_rows, mixed), BF16),
            pltpu.VMEM((CHIPS, part_rows, mixed), BF16),
            pltpu.VMEM((GROUPS, part_rows, mixed), BF16),
            pltpu.VMEM((count, 2, CHIPS, part, width), BF16),
            pltpu.VMEM((count, CHIPS, part, width), BF16),
            pltpu.VMEM((count, CHIPS, part, width), BF16),
            pltpu.VMEM((2, 8, 128), F32),
            pltpu.VMEM((GROUPS, 8, 128), F32),
            pltpu.SemaphoreType.DMA((GROUPS, 4)),
            pltpu.SemaphoreType.DMA((GROUPS, 4)),
            pltpu.SemaphoreType.DMA((GROUPS, 4)),
            pltpu.SemaphoreType.DMA((GROUPS, 4)),
            pltpu.SemaphoreType.DMA((16, 8)),
            pltpu.SemaphoreType.DMA((16, 8)),
            pltpu.SemaphoreType.DMA((8,)),
            pltpu.SemaphoreType.DMA((8,)),
        ],
        compiler_params=pltpu.CompilerParams(
            collective_id=1, has_side_effects=True, vmem_limit_bytes=62 * 1024 * 1024
        ),
    )(
        batch_ids.reshape(batch // 128, 128), labels.reshape(batch // 128, 128), aggregates, w_proj, w_qk, w_value, w_class
    )
    grad_proj, grad_qk, grad_value, grad_class, loss = pl.pallas_call(
        functools.partial(finish_kernel, batch_total, class_count),
        out_shape=(
            jax.ShapeDtypeStruct((count, feat, width), F32),
            jax.ShapeDtypeStruct((width, 2 * KEY), F32),
            jax.ShapeDtypeStruct((width, width), F32),
            jax.ShapeDtypeStruct((class_count, count * width), F32),
            jax.ShapeDtypeStruct((1, 1), F32),
        ),
        in_specs=[anywhere] * 4,
        out_specs=(anywhere,) + (vmem,) * 3 + (pl.BlockSpec(memory_space=pltpu.SMEM),),
        scratch_shapes=[
            pltpu.VMEM((count, 2, CHIPS, part, width), BF16),
            pltpu.VMEM((2, CHIPS, half, 128), BF16),
            pltpu.VMEM((2, CHIPS, part_rows, mixed), BF16),
            pltpu.VMEM((2, CHIPS, 8, 128), F32),
            pltpu.VMEM((count, feat, width), F32),
            pltpu.SemaphoreType.DMA((5,)),
            pltpu.SemaphoreType.DMA((2,)),
        ],
        compiler_params=pltpu.CompilerParams(vmem_limit_bytes=62 * 1024 * 1024),
    )(*sums)
    return (grad_proj, grad_qk, grad_value, grad_class, loss.reshape(()))


def solution(mesh):
    in_specs = (P("meta", "node", None), P("node"), P("node"), P("meta", None, None), P(), P(), P())
    out_specs = (P("meta", None, None), P(), P(), P(None, "meta"), P())
    return jax.shard_map(local, mesh=mesh, in_specs=in_specs, out_specs=out_specs, check_vma=False)
```

```python
import functools

import jax
import jax.numpy as jnp
from jax import lax
from jax.experimental import pallas as pl
from jax.experimental.pallas import tpu as pltpu
from jax.sharding import PartitionSpec as P

MESH = pl.DeviceIdType.MESH
F32 = jnp.float32
BF16 = jnp.bfloat16
GROUPS = 8
CHIPS = 8
PAPERS = 192
HALF = 96
BLOCK = 16
METAS = 16
KEY = 64
CLASS_PAD = 160
TAIL = CLASS_PAD - 128
META_ROWS = 64
UNROLL = 6


def dot(a, b):
    return jnp.dot(a, b, preferred_element_type=F32)


def dot_nt(a, b):
    return lax.dot_general(a, b, (((1,), (1,)), ((), ())), preferred_element_type=F32)


def dot_tn(a, b):
    return lax.dot_general(a, b, (((0,), (0,)), ((), ())), preferred_element_type=F32)


def iota(shape, axis):
    return lax.broadcasted_iota(jnp.int32, shape, axis)


def where_one(mask):
    return mask.astype(F32).astype(BF16)


def remote(src, dst, send_sem, recv_sem, where):
    return pltpu.make_async_remote_copy(
        src_ref=src, dst_ref=dst, send_sem=send_sem, recv_sem=recv_sem, device_id=where, device_id_type=MESH
    )


def step_kernel(
    seed, class_count,
    ids_ref, labels_ref, agg_hbm, w_proj_hbm, w_qk, w_value, w_class_hbm,
    gp_all, cls_all, qv_all, loss_node,
    load_sem, labels, gathered, outbox, hidden, w_all, w_back, w_mix,
    joined, d_joined, dlogits, attended, mail, mail_in, d_vq, d_vk,
    cx, cx_in, cx_meta, cx_sum, cx_chip, cy, cy_in, cy_chip, cy_sum, cy_meta,
    qv, qv_in, qv_chip, qv_meta,
    gp, gp_in, gp_chip, loss_acc, loss_meta,
    out_sem, in_sem, mail_send, mail_recv, send_sem, recv_sem, sib_send, sib_recv,
):
    me = lax.axis_index("meta")
    node = lax.axis_index("node")
    chip, core = node // 2, lax.rem(node, 2)
    other = 1 - core
    sibling = {"node": 2 * chip + other}
    groups = [lax.rem(me + j, GROUPS) for j in range(1, GROUPS)]
    chips = [lax.rem(chip + j, CHIPS) for j in range(1, CHIPS)]
    width = w_value.shape[0]
    rows, feat = agg_hbm.shape[1:]
    tail_at = 128 * METAS

    barrier = pltpu.get_barrier_semaphore()
    for g in groups:
        pl.semaphore_signal(barrier, inc=1, device_id={"meta": g}, device_id_type=MESH)
    for k in chips:
        pl.semaphore_signal(barrier, inc=1, device_id={"node": 2 * k + core}, device_id_type=MESH)
    pl.semaphore_signal(barrier, inc=1, device_id=sibling, device_id_type=MESH)

    def to_group(phase, g, src, dst):
        return remote(src, dst, send_sem.at[phase, g], recv_sem.at[phase, me], {"meta": g})

    def from_group(phase, g, dst):
        return remote(dst, dst, send_sem.at[phase, g], recv_sem.at[phase, g], {"meta": g})

    def to_chip(phase, k, src, dst):
        return remote(src, dst, send_sem.at[phase, k], recv_sem.at[phase, chip], {"node": 2 * k + core})

    def from_chip(phase, k, dst):
        return remote(dst, dst, send_sem.at[phase, k], recv_sem.at[phase, k], {"node": 2 * k + core})

    def to_sibling(phase, src, dst):
        return remote(src, dst, sib_send.at[phase], sib_recv.at[phase], sibling)

    def to_column(src, dst):
        eye = iota((128, 128), 0) == iota((128, 128), 1)
        for t in range(src.shape[0]):
            row = jnp.broadcast_to(src[t : t + 1, :].astype(F32), (128, 128))
            dst[t * 128 : (t + 1) * 128, :] = jnp.sum(jnp.where(eye, row, 0.0), axis=1, keepdims=True).astype(jnp.int32)

    def part(h):
        return pl.ds(pl.multiple_of(h * HALF, HALF), HALF)

    def out_copy(g, h, m):
        return remote(
            outbox.at[m, g, part(h), :],
            hidden.at[2 * me + m, part(h), :],
            out_sem.at[g, 2 * h + m],
            in_sem.at[me, 2 * h + m],
            {"meta": g},
        )

    def in_copy(g, h, m):
        here = hidden.at[2 * g + m, part(h), :]
        return remote(here, here, out_sem.at[g, 2 * h + m], in_sem.at[g, 2 * h + m], {"meta": g})

    def front(agg, w_proj, w_class, ids):
        loads = []
        step = rows // 4
        for m in range(2):
            for q in range(4):
                at = pl.ds(q * step, step)
                loads.append(pltpu.make_async_copy(agg_hbm.at[m, at, :], agg.at[m, at, :], load_sem.at[4 * m + q]))
        loads.append(pltpu.make_async_copy(w_proj_hbm, w_proj, load_sem.at[8]))
        loads.append(pltpu.make_async_copy(w_class_hbm, w_class, load_sem.at[9]))
        for load in loads:
            load.start()
        to_column(ids_ref, ids)
        for load in loads[:9]:
            load.wait()
        pl.semaphore_wait(barrier, GROUPS - 1 + CHIPS)

        def project_pair(p, h, with_own):
            first = lax.rem(me // 2 + p + 1, 4) * 2 + lax.rem(me + p, 2)
            second = lax.rem(me // 2 + 3 - p, 4) * 2 + lax.rem(me + p + 1, 2)
            if with_own:
                second = me
            spots = [pl.ds(pl.multiple_of(g * PAPERS + h * HALF, HALF), HALF) for g in (first, second)]
            column = jnp.concatenate([ids[spot, :] for spot in spots], axis=0)
            picks = where_one(column == iota((2 * HALF, rows), 1))
            for m in range(2):
                got = dot(picks, agg[m]).astype(BF16)
                row = dot(got, w_proj[m]).astype(BF16)
                for q, g in enumerate((first, second)):
                    gathered[m, spots[q], :] = got[q * HALF : (q + 1) * HALF]
                    mine = row[q * HALF : (q + 1) * HALF]
                    outbox[m, g, part(h), :] = mine
                    if with_own and q == 1:
                        hidden[2 * me + m, part(h), :] = mine
                    else:
                        out_copy(g, h, m).start()

        def project_half(h, carry):
            def one(p, c):
                project_pair(p, h, False)
                return c

            lax.fori_loop(0, 3, one, 0)
            project_pair(3, h, True)
            return carry

        lax.fori_loop(0, 2, project_half, 0)

        to_column(labels_ref, ids)
        labels[...] = ids[pl.ds(pl.multiple_of(me * PAPERS, PAPERS), PAPERS), :]

        swap = where_one(lax.rem(iota((2 * KEY, 2 * KEY), 0) + KEY, 2 * KEY) == iota((2 * KEY, 2 * KEY), 1))
        w_all[:, :width] = w_value[...]
        w_all[:, width : width + 2 * KEY] = w_qk[...]
        w_all[:, width + 2 * KEY :] = dot(w_qk[...], swap).astype(BF16)
        w_back[:width, :] = w_value[...].astype(F32).T.astype(BF16)
        w_back[width:, :] = w_qk[...].astype(F32).T.astype(BF16)
        loads[9].wait()
        for m in range(METAS):
            lanes = slice(m * width, (m + 1) * width)
            w_mix[128 * m : 128 * (m + 1), :] = w_class[:128, lanes]
            last = w_class[128:class_count, lanes].astype(F32)
            zeros = jnp.zeros((CLASS_PAD - class_count, width), F32)
            w_mix[tail_at + TAIL * m : tail_at + TAIL * (m + 1), :] = jnp.concatenate([last, zeros], axis=0).astype(BF16)

    pl.run_scoped(
        front,
        pltpu.VMEM(agg_hbm.shape, BF16),
        pltpu.VMEM(w_proj_hbm.shape, BF16),
        pltpu.VMEM(w_class_hbm.shape, BF16),
        pltpu.VMEM((GROUPS * PAPERS, 1), jnp.int32),
    )
    def class_rows(m):
        main = w_mix[pl.ds(pl.multiple_of(128 * m, 128), 128), :]
        tail = w_mix[pl.ds(pl.multiple_of(tail_at + TAIL * m, TAIL), TAIL), :]
        return jnp.concatenate([main, tail], axis=0)

    def class_rows_wide(m):
        return jnp.concatenate([class_rows(m), jnp.zeros((256 - CLASS_PAD, width), BF16)], axis=0)

    scale = KEY ** (-0.5)
    side = BLOCK * METAS
    same = lax.rem(iota((side, side), 0), BLOCK) == lax.rem(iota((side, side), 1), BLOCK)
    first = iota((side, 2 * KEY), 1) < KEY
    by_key = where_one(iota((side, side), 0) // BLOCK == iota((side, side), 1) // BLOCK)
    by_query = iota((side, side), 0) // BLOCK == lax.rem(iota((side, side), 1), METAS)

    def mail_to(g, h):
        return remote(
            mail.at[g, part(h), :], mail_in.at[me, part(h), :], mail_send.at[g, h], mail_recv.at[me, h], {"meta": g}
        )

    def mail_from(g, h):
        here = mail_in.at[g, part(h), :]
        return remote(here, here, mail_send.at[g, h], mail_recv.at[g, h], {"meta": g})

    def key_rows(g, h):
        return pl.ds(pl.multiple_of(g * PAPERS + h * HALF, HALF), HALF)

    def keys_to(g, h):
        return remote(
            d_vq.at[pl.ds(2 * g, 2), part(h), pl.ds(width, 2 * KEY)],
            d_vk.at[:, key_rows(me, h), pl.ds(width, 2 * KEY)],
            mail_send.at[g, 2 + h],
            mail_recv.at[me, 2 + h],
            {"meta": g},
        )

    def keys_from(g, h):
        here = d_vk.at[:, key_rows(g, h), pl.ds(width, 2 * KEY)]
        return remote(here, here, mail_send.at[g, 2 + h], mail_recv.at[g, 2 + h], {"meta": g})

    def head(values, attention, kq, h, carry):
        for g in groups:
            for m in range(2):
                in_copy(g, h, m).wait_recv()

        @pl.when(h == 1)
        def _():
            for g in groups:
                mail_to(g, 0).start()
            for g in groups:
                keys_to(g, 0).start()

        def forward(t, c):
            b = h * (HALF // BLOCK) + t
            at = pl.ds(pl.multiple_of(b * BLOCK, BLOCK), BLOCK)
            here = hidden[:, at, :].reshape(side, width)
            mixed = dot(here, w_all[...]).astype(BF16)
            v = mixed[:, :width]
            swapped = mixed[:, width + 2 * KEY :]
            values[b] = v
            kq[b] = swapped
            q = jnp.where(first, mixed[:, width : width + 2 * KEY].astype(F32), 0.0).astype(BF16)
            scores = dot_nt(q, swapped) * scale
            weights = jnp.where(same, jnp.exp(scores), 0.0)
            att = weights * (1.0 / jnp.sum(weights, axis=1, keepdims=True))
            attention[b] = att
            att = att.astype(BF16)
            out = (dot(att, v) + here.astype(F32)).astype(BF16)
            joined[:, at, :] = out.reshape(METAS, BLOCK, width)
            wide = jnp.where(by_query, dot(att, by_key), 0.0)
            attended[at, :] = jnp.sum(wide.reshape(METAS, BLOCK, side), axis=0).astype(BF16)
            return c

        lax.fori_loop(0, HALF // BLOCK, forward, 0, unroll=UNROLL)

        logits = lax.fori_loop(
            0,
            METAS,
            lambda m, t: t + dot_nt(joined[m, part(h), :], class_rows_wide(m)),
            jnp.zeros((HALF, 256), F32),
        )
        class_at = iota((HALF, 256), 1)
        exps = jnp.where(class_at < class_count, jnp.exp(logits), 0.0)
        total = jnp.sum(exps, axis=1, keepdims=True)
        onehot = (labels[part(h), :] == class_at).astype(F32)
        loss_rows = jnp.log(total) - jnp.sum(onehot * logits, axis=1, keepdims=True)
        loss_acc[h] = jnp.zeros((8, 128), F32) + jnp.sum(loss_rows)
        dl = (seed * (exps / total - onehot)).astype(BF16)
        dlogits[part(h), :] = dl

        lane = iota((side, 128), 1)
        for j in range(GROUPS):
            g = lax.rem(me + j, GROUPS)
            choose = where_one(jnp.logical_and(iota((side, 128), 0) == lane + 2 * METAS * g - TAIL, lane >= TAIL) & (lane < TAIL + 2 * METAS))
            second = (dl[:, 128:].astype(F32) + dot(attended[part(h), :], choose)).astype(BF16)
            box = mail_in if j == 0 else mail
            box[g, part(h), :128] = dl[:, :128]
            box[g, part(h), 128:] = second

        @pl.when(h == 1)
        def _():
            for g in groups:
                mail_to(g, 1).start()

        def spread(m, c):
            d_joined[m, part(h), :] = dot(dl[:, :CLASS_PAD], class_rows(m)).astype(BF16)
            return c

        lax.fori_loop(0, METAS, spread, 0)

        def backward(t, c):
            b = h * (HALF // BLOCK) + t
            at = pl.ds(pl.multiple_of(b * BLOCK, BLOCK), BLOCK)
            dj = d_joined[:, at, :].reshape(side, width)
            att = attention[b]
            d_att = dot_nt(dj, values[b])
            mean = jnp.sum(att * d_att, axis=1, keepdims=True)
            d_scores = (att * (d_att - mean) * scale).astype(BF16)
            swapped = kq[b]
            grad = jnp.where(first, dot(d_scores, swapped), dot_tn(d_scores, swapped))
            d_vq[:, at, width:] = grad.astype(BF16).reshape(METAS, BLOCK, 2 * KEY)
            d_val = dot_tn(att.astype(BF16), dj)
            d_vq[:, at, :width] = d_val.astype(BF16).reshape(METAS, BLOCK, width)
            return c

        lax.fori_loop(0, HALF // BLOCK, backward, 0, unroll=UNROLL)

        @pl.when(h == 1)
        def _():
            for g in groups:
                keys_to(g, 1).start()

        for m in range(2):
            d_vk[m, key_rows(me, h), width:] = d_vq[2 * me + m, part(h), width:]
        return carry

    def heads(*held):
        lax.fori_loop(0, 2, functools.partial(head, *held), 0)

    blocks = PAPERS // BLOCK
    pl.run_scoped(
        heads,
        pltpu.VMEM((blocks, side, width), BF16),
        pltpu.VMEM((blocks, side, side), F32),
        pltpu.VMEM((blocks, side, 2 * KEY), BF16),
    )

    def classes(g, carry):
        for m in range(2):
            grad = dot_tn(dlogits[:, :CLASS_PAD], joined[2 * g + m]).astype(BF16)
            for q in range(4):
                lanes = slice(q * 128, (q + 1) * 128)
                for p in range(2):
                    top = p * (CLASS_PAD // 2)
                    cx[p, g, 4 * m + q] = grad[top : top + META_ROWS, lanes]
                    cy[p, 4 * m + q, g] = grad[top + META_ROWS : top + CLASS_PAD // 2, lanes]
        return carry

    lax.fori_loop(0, GROUPS, classes, 0)
    c0 = [to_sibling(0, cx.at[other], cx_in), to_sibling(7, cy.at[other], cy_in)]
    for copy in c0:
        copy.start()

    batch = GROUPS * PAPERS
    part_rows = qv.shape[2]
    for c in range(4):
        cols = slice(c * 128, (c + 1) * 128)
        grad = dot_tn(
            hidden[:, :, cols].reshape(METAS * PAPERS, 128), d_vq[...].reshape(METAS * PAPERS, width + 2 * KEY)
        ).astype(BF16)
        for r in range(128 // part_rows):
            piece = c * (128 // part_rows) + r
            qv[piece // CHIPS, piece % CHIPS] = grad[r * part_rows : (r + 1) * part_rows]
    q0 = to_sibling(1, qv.at[other], qv_in)
    q0.start()

    for copy in c0:
        copy.wait_recv()

    def pair_class(g, carry):
        cx_in[g] = (cx[core, g].astype(F32) + cx_in[g].astype(F32)).astype(BF16)
        cy_in[g] = (cy[core, g].astype(F32) + cy_in[g].astype(F32)).astype(BF16)
        return carry

    lax.fori_loop(0, GROUPS, pair_class, 0, unroll=4)
    for k in chips:
        to_chip(0, k, cy_in.at[k], cy_chip.at[chip]).start()
    for g in groups:
        to_group(1, g, cx_in.at[g], cx_meta.at[me]).start()
    cx_meta[me] = cx_in[me]
    cy_chip[chip] = cy_in[chip]

    q0.wait_recv()

    def pair_qv(k, carry):
        qv_in[k] = (qv[core, k].astype(F32) + qv_in[k].astype(F32)).astype(BF16)
        return carry

    lax.fori_loop(0, CHIPS, pair_qv, 0, unroll=4)
    for k in chips:
        to_chip(2, k, qv_in.at[k], qv_chip.at[chip]).start()
    qv_chip[chip] = qv_in[chip]

    for g in groups:
        for h in range(2):
            mail_from(g, h).wait_recv()
    tail_lane = iota((128, TAIL * METAS), 1)
    tail_row = iota((128, TAIL * METAS), 0)
    repeat = where_one((tail_row < TAIL) & (lax.rem(tail_lane, TAIL) == tail_row))
    widen = [where_one(tail_row == TAIL + METAS * j + tail_lane // TAIL) for j in range(2)]

    def home_values(q, x_even, x_odd):
        def build(j, x):
            for u in range(2):
                s = lax.rem(2 * j + u, GROUPS)
                at = slice(u * PAPERS, (u + 1) * PAPERS)
                main = mail_in[s, :, :128].astype(F32)
                second = mail_in[s, :, 128:]
                second_f = second.astype(F32)
                x[at, tail_at:] = (dot(second, repeat) * dot(second, widen[q])).astype(BF16)
                for i in range(METAS):
                    lane = TAIL + METAS * q + i
                    x[at, 128 * i : 128 * (i + 1)] = (second_f[:, lane : lane + 1] * main).astype(BF16)

        def multiply(j, x):
            at = pl.ds(pl.multiple_of(2 * j * PAPERS, 2 * PAPERS), 2 * PAPERS)
            d_vk[q, at, :width] = dot(x[...], w_mix[...]).astype(BF16)

        build(0, x_even)

        def two(t, carry):
            build(2 * t + 1, x_odd)
            multiply(2 * t, x_even)
            build(2 * t + 2, x_even)
            multiply(2 * t + 1, x_odd)
            return carry

        lax.fori_loop(0, GROUPS // 4, two, 0)

    spread_shape = pltpu.VMEM((2 * PAPERS, METAS * CLASS_PAD), BF16)

    d_hidden = d_joined

    def home_hidden(m):
        def some(r, carry):
            at = pl.ds(pl.multiple_of(r * 2 * PAPERS, 2 * PAPERS), 2 * PAPERS)
            letters = mail_in[pl.ds(2 * r, 2)].reshape(2 * PAPERS, 256)[:, :CLASS_PAD]
            grad = dot(letters, class_rows(2 * me + m)) + dot(d_vk[m, at, :], w_back[...])
            d_hidden[pl.ds(GROUPS * m + 2 * r, 2)] = grad.astype(BF16).reshape(2, PAPERS, width)
            return carry

        lax.fori_loop(0, GROUPS // 2, some, 0, unroll=4)

    part_feat = gp.shape[3]

    def project(m, p):
        back = d_hidden[GROUPS * m : GROUPS * (m + 1)].reshape(batch, width)
        cols = pl.ds(pl.multiple_of(p * CHIPS * part_feat, 128), CHIPS * part_feat)
        grad = dot_tn(gathered[m, :, cols], back).astype(BF16)
        for k in range(CHIPS):
            gp[m, p, k] = grad[k * part_feat : (k + 1) * part_feat]

    def pair_proj(m):
        def one(k, carry):
            gp_in[m, k] = (gp[m, core, k].astype(F32) + gp_in[m, k].astype(F32)).astype(BF16)
            return carry

        lax.fori_loop(0, CHIPS, one, 0, unroll=4)
        for k in chips:
            to_chip(9 + m, k, gp_in.at[m, k], gp_chip.at[m, chip]).start()
        gp_chip[m, chip] = gp_in[m, chip]

    def across(m, k):
        here = gp_all.at[m, core, k]
        return remote(here, here, send_sem.at[13 + m, k], recv_sem.at[13 + m, k], sibling)

    def across_in(m, k):
        here = gp_all.at[m, other, k]
        return remote(here, here, send_sem.at[13 + m, k], recv_sem.at[13 + m, k], sibling)

    def chip_proj(m):
        for k in chips:
            from_chip(9 + m, k, gp_chip.at[m, k]).wait_recv()
        gp_all[m, core, chip] = jnp.sum(gp_chip[m].astype(F32), axis=0).astype(BF16)
        for k in chips:
            to_chip(11 + m, k, gp_all.at[m, core, chip], gp_all.at[m, core, chip]).start()
        across(m, chip).start()

    def pass_on(m):
        for k in chips:
            from_chip(11 + m, k, gp_all.at[m, core, k]).wait_recv()
            across(m, k).start()

    g0 = [to_sibling(2 + 4 * m, gp.at[m, other], gp_in.at[m]) for m in range(2)]

    def first_sum(m):
        project(m, other)
        g0[m].start()
        project(m, core)
        g0[m].wait_recv()
        pair_proj(m)

    pl.run_scoped(functools.partial(home_values, 0), spread_shape, spread_shape)
    for g in groups:
        for h in range(2):
            keys_from(g, h).wait_recv()
    home_hidden(0)
    first_sum(0)
    pl.run_scoped(functools.partial(home_values, 1), spread_shape, spread_shape)

    for k in chips:
        from_chip(0, k, cy_chip.at[k]).wait_recv()

    def chip_sum(g, carry):
        cy_sum[g] = jnp.sum(cy_chip[:, g].astype(F32), axis=0).astype(BF16)
        return carry

    lax.fori_loop(0, GROUPS, chip_sum, 0, unroll=4)
    for g in groups:
        to_group(15, g, cy_sum.at[g], cy_meta.at[me]).start()
    cy_meta[me] = cy_sum[me]

    for k in chips:
        from_chip(2, k, qv_chip.at[k]).wait_recv()
    qv_meta[me] = jnp.sum(qv_chip[...].astype(F32), axis=0).astype(BF16)
    loss_meta[me] = loss_acc[0] + loss_acc[1]
    for g in groups:
        to_group(4, g, qv_meta.at[me], qv_meta.at[me]).start()
        to_group(5, g, loss_meta.at[me], loss_meta.at[me]).start()

    home_hidden(1)
    chip_proj(0)
    first_sum(1)

    for g in groups:
        from_group(1, g, cx_meta.at[g]).wait_recv()

    def meta_sum(k, carry):
        cx_sum[k] = jnp.sum(cx_meta[:, k].astype(F32), axis=0).astype(BF16)
        return carry

    lax.fori_loop(0, CHIPS, meta_sum, 0, unroll=4)
    for k in chips:
        to_chip(3, k, cx_sum.at[k], cx_chip.at[chip]).start()
    cx_chip[chip] = cx_sum[chip]

    for g in groups:
        from_group(4, g, qv_meta.at[g]).wait_recv()
        from_group(5, g, loss_meta.at[g]).wait_recv()
        from_group(15, g, cy_meta.at[g]).wait_recv()
    qv_all[core, chip] = jnp.sum(qv_meta[...].astype(F32), axis=0).astype(BF16)
    loss_node[core, chip] = jnp.sum(loss_meta[...], axis=0)
    cls_all[core, chip, META_ROWS:, :] = jnp.sum(cy_meta[...].astype(F32), axis=0).astype(BF16)
    for k in chips:
        to_chip(7, k, qv_all.at[core, chip], qv_all.at[core, chip]).start()
        to_chip(8, k, loss_node.at[core, chip], loss_node.at[core, chip]).start()

    pass_on(0)

    for k in chips:
        from_chip(3, k, cx_chip.at[k]).wait_recv()
    cls_all[core, chip, :META_ROWS, :] = jnp.sum(cx_chip[...].astype(F32), axis=0).astype(BF16)
    for k in chips:
        to_chip(6, k, cls_all.at[core, chip], cls_all.at[core, chip]).start()

    chip_proj(1)

    for k in chips:
        from_chip(6, k, cls_all.at[core, k]).wait_recv()
        from_chip(7, k, qv_all.at[core, k]).wait_recv()
        from_chip(8, k, loss_node.at[core, k]).wait_recv()
    finals = [
        to_sibling(3, cls_all.at[core], cls_all.at[core]),
        to_sibling(4, qv_all.at[core], qv_all.at[core]),
        to_sibling(5, loss_node.at[core], loss_node.at[core]),
    ]
    for copy in finals:
        copy.start()

    pass_on(1)

    for m in range(2):
        for k in [chip] + chips:
            across_in(m, k).wait_recv()
    remote(cls_all.at[other], cls_all.at[other], sib_send.at[3], sib_recv.at[3], sibling).wait_recv()
    remote(qv_all.at[other], qv_all.at[other], sib_send.at[4], sib_recv.at[4], sibling).wait_recv()
    remote(loss_node.at[other], loss_node.at[other], sib_send.at[5], sib_recv.at[5], sibling).wait_recv()

    q0.wait_send()
    for copy in c0 + g0 + finals:
        copy.wait_send()
    for g in groups:
        for h in range(2):
            for m in range(2):
                out_copy(g, h, m).wait_send()
            mail_to(g, h).wait_send()
            keys_to(g, h).wait_send()
        to_group(1, g, cx_in.at[g], cx_meta.at[me]).wait_send()
        to_group(15, g, cy_sum.at[g], cy_meta.at[me]).wait_send()
        to_group(4, g, qv_meta.at[me], qv_meta.at[me]).wait_send()
        to_group(5, g, loss_meta.at[me], loss_meta.at[me]).wait_send()
    for k in chips:
        to_chip(2, k, qv_in.at[k], qv_chip.at[chip]).wait_send()
        to_chip(0, k, cy_in.at[k], cy_chip.at[chip]).wait_send()
        to_chip(3, k, cx_sum.at[k], cx_chip.at[chip]).wait_send()
        to_chip(6, k, cls_all.at[core, chip], cls_all.at[core, chip]).wait_send()
        to_chip(7, k, qv_all.at[core, chip], qv_all.at[core, chip]).wait_send()
        to_chip(8, k, loss_node.at[core, chip], loss_node.at[core, chip]).wait_send()
    for m in range(2):
        for k in chips:
            to_chip(9 + m, k, gp_in.at[m, k], gp_chip.at[m, chip]).wait_send()
            to_chip(11 + m, k, gp_all.at[m, core, chip], gp_all.at[m, core, chip]).wait_send()
        for k in [chip] + chips:
            across(m, k).wait_send()


def finish_kernel(
    batch_total, class_count,
    gp_hbm, cls_hbm, qv_hbm, loss_hbm, proj_hbm, qk_out, value_out, class_out, loss_out,
    gp, cls, qv, loss, proj, in_sem, out_sem,
):
    part_feat, width = gp.shape[3:]
    part_rows = qv.shape[2]
    half_rows = cls.shape[2]
    loads = [pltpu.make_async_copy(gp_hbm.at[m], gp.at[m], in_sem.at[m]) for m in range(2)]
    for q, (src, dst) in enumerate(((cls_hbm, cls), (qv_hbm, qv), (loss_hbm, loss))):
        loads.append(pltpu.make_async_copy(src, dst, in_sem.at[2 + q]))
    for load in loads:
        load.start()
    stores = []
    for m in range(2):
        loads[m].wait()
        for p in range(2):
            for k in range(CHIPS):
                start = (p * CHIPS + k) * part_feat
                proj[m, start : start + part_feat, :] = gp[m, p, k].astype(F32)
        stores.append(pltpu.make_async_copy(proj.at[m], proj_hbm.at[m], out_sem.at[m]))
        stores[m].start()
    for load in loads[2:]:
        load.wait()
    for p in range(2):
        for k in range(CHIPS):
            start = (p * CHIPS + k) * part_rows
            block = qv[p, k].astype(F32)
            value_out[start : start + part_rows, :] = block[:, :width]
            qk_out[start : start + part_rows, :] = block[:, width:]
            lanes = slice(k * 128, (k + 1) * 128)
            if p == 0:
                class_out[:half_rows, lanes] = cls[0, k].astype(F32)
            else:
                class_out[half_rows:, lanes] = cls[1, k].astype(F32)[: class_count - half_rows]
    loss_out[0, 0] = jnp.sum(loss[...].reshape(2 * CHIPS, 8, 128), axis=0)[0, 0] / batch_total
    for store in stores:
        store.wait()


def local(aggregates, batch_ids, labels, w_proj, w_qk, w_value, w_class):
    batch_total = labels.shape[0] * lax.axis_size("node")
    class_count = w_class.shape[0]
    count, rows, feat = aggregates.shape
    batch = batch_ids.shape[0]
    width = w_value.shape[0]
    side = BLOCK * METAS
    mixed = width + 2 * KEY
    half = CLASS_PAD // 2
    part = feat // (2 * CHIPS)
    part_rows = width // (2 * CHIPS)
    vmem = pl.BlockSpec(memory_space=pltpu.VMEM)
    anywhere = pl.BlockSpec(memory_space=pl.ANY)
    sums = pl.pallas_call(
        functools.partial(step_kernel, 1.0 / batch_total**0.5, class_count),
        out_shape=(
            jax.ShapeDtypeStruct((count, 2, CHIPS, part, width), BF16),
            jax.ShapeDtypeStruct((2, CHIPS, half, 128), BF16),
            jax.ShapeDtypeStruct((2, CHIPS, part_rows, mixed), BF16),
            jax.ShapeDtypeStruct((2, CHIPS, 8, 128), F32),
        ),
        in_specs=[vmem, vmem, anywhere, anywhere, vmem, vmem, anywhere],
        out_specs=(vmem,) * 4,
        scratch_shapes=[
            pltpu.SemaphoreType.DMA((10,)),
            pltpu.VMEM((PAPERS, 1), jnp.int32),
            pltpu.VMEM((count, batch, feat), BF16),
            pltpu.VMEM((count, GROUPS, PAPERS, width), BF16),
            pltpu.VMEM((METAS, PAPERS, width), BF16),
            pltpu.VMEM((width, width + 4 * KEY), BF16),
            pltpu.VMEM((mixed, width), BF16),
            pltpu.VMEM((METAS * CLASS_PAD, width), BF16),
            pltpu.VMEM((METAS, PAPERS, width), BF16),
            pltpu.VMEM((METAS, PAPERS, width), BF16),
            pltpu.VMEM((PAPERS, 256), BF16),
            pltpu.VMEM((PAPERS, side), BF16),
            pltpu.VMEM((GROUPS, PAPERS, 256), BF16),
            pltpu.VMEM((GROUPS, PAPERS, 256), BF16),
            pltpu.VMEM((METAS, PAPERS, mixed), BF16),
            pltpu.VMEM((count, batch, mixed), BF16),
            pltpu.VMEM((2, GROUPS, CHIPS, META_ROWS, 128), BF16),
            pltpu.VMEM((GROUPS, CHIPS, META_ROWS, 128), BF16),
            pltpu.VMEM((GROUPS, CHIPS, META_ROWS, 128), BF16),
            pltpu.VMEM((CHIPS, META_ROWS, 128), BF16),
            pltpu.VMEM((CHIPS, META_ROWS, 128), BF16),
            pltpu.VMEM((2, CHIPS, GROUPS, half - META_ROWS, 128), BF16),
            pltpu.VMEM((CHIPS, GROUPS, half - META_ROWS, 128), BF16),
            pltpu.VMEM((CHIPS, GROUPS, half - META_ROWS, 128), BF16),
            pltpu.VMEM((GROUPS, half - META_ROWS, 128), BF16),
            pltpu.VMEM((GROUPS, half - META_ROWS, 128), BF16),
            pltpu.VMEM((2, CHIPS, part_rows, mixed), BF16),
            pltpu.VMEM((CHIPS, part_rows, mixed), BF16),
            pltpu.VMEM((CHIPS, part_rows, mixed), BF16),
            pltpu.VMEM((GROUPS, part_rows, mixed), BF16),
            pltpu.VMEM((count, 2, CHIPS, part, width), BF16),
            pltpu.VMEM((count, CHIPS, part, width), BF16),
            pltpu.VMEM((count, CHIPS, part, width), BF16),
            pltpu.VMEM((2, 8, 128), F32),
            pltpu.VMEM((GROUPS, 8, 128), F32),
            pltpu.SemaphoreType.DMA((GROUPS, 4)),
            pltpu.SemaphoreType.DMA((GROUPS, 4)),
            pltpu.SemaphoreType.DMA((GROUPS, 4)),
            pltpu.SemaphoreType.DMA((GROUPS, 4)),
            pltpu.SemaphoreType.DMA((16, 8)),
            pltpu.SemaphoreType.DMA((16, 8)),
            pltpu.SemaphoreType.DMA((8,)),
            pltpu.SemaphoreType.DMA((8,)),
        ],
        compiler_params=pltpu.CompilerParams(
            collective_id=1, has_side_effects=True, vmem_limit_bytes=62 * 1024 * 1024
        ),
    )(
        batch_ids.reshape(batch // 128, 128), labels.reshape(batch // 128, 128), aggregates, w_proj, w_qk, w_value, w_class
    )
    grad_proj, grad_qk, grad_value, grad_class, loss = pl.pallas_call(
        functools.partial(finish_kernel, batch_total, class_count),
        out_shape=(
            jax.ShapeDtypeStruct((count, feat, width), F32),
            jax.ShapeDtypeStruct((width, 2 * KEY), F32),
            jax.ShapeDtypeStruct((width, width), F32),
            jax.ShapeDtypeStruct((class_count, count * width), F32),
            jax.ShapeDtypeStruct((1, 1), F32),
        ),
        in_specs=[anywhere] * 4,
        out_specs=(anywhere,) + (vmem,) * 3 + (pl.BlockSpec(memory_space=pltpu.SMEM),),
        scratch_shapes=[
            pltpu.VMEM((count, 2, CHIPS, part, width), BF16),
            pltpu.VMEM((2, CHIPS, half, 128), BF16),
            pltpu.VMEM((2, CHIPS, part_rows, mixed), BF16),
            pltpu.VMEM((2, CHIPS, 8, 128), F32),
            pltpu.VMEM((count, feat, width), F32),
            pltpu.SemaphoreType.DMA((5,)),
            pltpu.SemaphoreType.DMA((2,)),
        ],
        compiler_params=pltpu.CompilerParams(vmem_limit_bytes=62 * 1024 * 1024),
    )(*sums)
    return (grad_proj, grad_qk, grad_value, grad_class, loss.reshape(()))


def solution(mesh):
    in_specs = (P("meta", "node", None), P("node"), P("node"), P("meta", None, None), P(), P(), P())
    out_specs = (P("meta", None, None), P(), P(), P(None, "meta"), P())
    return jax.shard_map(local, mesh=mesh, in_specs=in_specs, out_specs=out_specs, check_vma=False)
```
